32 devices in a mesh: section: 4 (over y, x), nodes: 8 (over z, core).
Axes of the slice: x: 2, y: 2, z: 4, core: 2. Of those that a mesh axis runs over, the one named last changes fastest.
Arguments:
- features: float32 [4, 2048, 256], P(None, 'nodes'), may hold values from -18 to 18
- cotangent: float32 [4, 2048, 256], P(None, 'nodes'), may hold values from -6 to 6
- train_mask: int32 [4, 2048], P(None, 'nodes'), may hold values 0 or 1
- degree: int32 [4, 2048], P(None, 'nodes'), may hold values from 2 to 8, as said below
- neighbours: int32 [4, 2048, 8], P(None, 'nodes'), may hold values from 0 to 287, as said below
- send_rows: int32 [4, 256], P(None, 'nodes'), may hold values from 0 to 255, as said below
- w_left: float32 [2, 256, 256], replicated, may hold values from -0.375 to 0.375
- w_right: float32 [2, 256, 256], replicated, may hold values from -0.375 to 0.375
- w_res: float32 [2, 256, 256], replicated, may hold values from -0.1875 to 0.1875
- attn_vec: float32 [2, 256], replicated, may hold values from -1.5 to 1.5
- bn_gain: float32 [2, 256], replicated, may hold values from 0.5 to 1.5
- bn_shift: float32 [2, 256], replicated, may hold values from -2 to 2
Outputs:
- outputs: float32 [4, 2048, 256], P('section', 'nodes')
- input_grad: float32 [4, 2048, 256], P('section', 'nodes')
- grad_left: float32 [2, 256, 256], replicated
- grad_right: float32 [2, 256, 256], replicated
- grad_res: float32 [2, 256, 256], replicated
- grad_vec: float32 [2, 256], replicated
- grad_gain: float32 [2, 256], replicated
- grad_shift: float32 [2, 256], replicated
The draws below stay inside these ranges and needn't reach their ends.
Inputs may be any that keep to these rules, and one draw needn't show every extreme that they name: `degree`: each node has between 2 and 8 live slots; on every partition some node uses all 8. `neighbours`: an entry below 256 is a row of the same partition in that micro-batch, and slot 0 is the node itself; an entry 256 + q * 4 + s is the s-th row that partition q sends to this partition in that micro-batch. `send_rows`: partition q's entries p * 4 to p * 4 + 3 name the local rows that q sends to partition p in that micro-batch.
All inputs are finite; a program needn't handle non-finite values. No bound on the sum of `train_mask` on one device may be relied on, other than what follows from the above.
Results may differ from the reference program's by a relative error of at most 0.0003.
Values sent between devices are 32-bit elements; how exact they have to be, the bound alone decides.
A program may use at most 128 MiB of HBM per device.

```python
import math
import jax
import jax.numpy as jnp
from jax import lax

D = 256
HEADS = 4
LAYERS = 2
MB = 4
NODE_MB = 256
SLOTS = 8
SEND = 4
HALO = 32
NODES = 2048
N_NODES = 8


def draw_features(key, part):
    key = jax.random.fold_in(key, 11)
    position = jnp.arange(NODES, dtype=jnp.float32) / NODES
    scale = (1.0 + 2.0 * position)[None, :, None]
    return jnp.clip(jax.random.normal(key, (MB, NODES, D), jnp.float32) * scale, -18.0, 18.0)


def draw_degree(key, part):
    key = jax.random.fold_in(key, 12)
    ceiling = jax.random.randint(key, (MB, N_NODES, 1), 4, SLOTS + 1)
    dropped = jax.random.randint(jax.random.fold_in(key, 1), (MB, N_NODES, NODE_MB), 0, 4)
    counts_drawn = jnp.maximum(ceiling - dropped, 2)
    position = jnp.arange(NODE_MB)[None, None, :]
    counts_drawn = jnp.where(position == 0, SLOTS, jnp.where(position == 1, 2, counts_drawn))
    return counts_drawn.reshape(MB, NODES).astype(jnp.int32)


def draw_neighbours(key, part):
    key = jax.random.fold_in(key, 13)
    picks = jax.random.randint(key, (MB, N_NODES, NODE_MB, SLOTS), 0, NODE_MB + HALO)
    itself = jnp.arange(NODE_MB)[None, None, :, None]
    slot_number = jnp.arange(SLOTS)[None, None, None, :]
    picks = jnp.where(slot_number == 0, itself, jnp.where(slot_number == 1, NODE_MB + itself % HALO, picks))
    return picks.reshape(MB, NODES, SLOTS).astype(jnp.int32)


def draw_send_rows(key, part):
    key = jax.random.fold_in(key, 14)
    picks = jax.random.randint(key, (MB, N_NODES * HALO), 0, NODE_MB)
    position = jnp.arange(N_NODES * HALO)[None, :]
    picks = jnp.where(position == 0, NODE_MB - 1, jnp.where(position == 1, 0, picks))
    return picks.astype(jnp.int32)


def with_ends(values, rng, smallest, high):
    longest = values.shape.index(max(values.shape))
    spots = []
    for shift in (0, 1):
        where = [jax.random.randint(jax.random.fold_in(rng, axis), (), 0, length) for axis, length in enumerate(values.shape)]
        where[longest] = (where[longest] + shift) % values.shape[longest]
        spots.append(tuple(where))
    return values.at[spots[0]].set(smallest).at[spots[1]].set(high)


def block_levels(stream_key, dims, cuts, least, top_value):
    def one(dim, blocks):
        steps = jax.random.uniform(jax.random.fold_in(jax.random.fold_in(stream_key, 6), dim), (blocks,), jnp.float32, least / len(cuts), top_value / len(cuts))
        return jnp.repeat(jnp.exp(steps), dims[dim] // blocks).reshape((-1,) + (1,) * (len(dims) - dim - 1))

    level = one(*cuts[0])
    for cut in cuts[1:]:
        level = level * one(*cut)
    return level


def noise(own_key, dims, width, most, cuts=(), held_as=jnp.bfloat16):
    drawn = width * jax.random.normal(own_key, dims, jnp.float32)
    if cuts:
        drawn = drawn * block_levels(own_key, dims, cuts, -0.22, 0.18)
    return jnp.clip(drawn, -most, most).astype(held_as)


def setup_inputs(seed: int = 0) -> dict:
    keys = jax.random.split(jax.random.key(seed), 13)
    return {
        "features": draw_features(jax.random.fold_in(keys[12], 71), 0),
        "cotangent": noise(keys[1], (MB, NODES, D), 1.0, 6.0, ((1, 8),), jnp.float32),
        "train_mask": with_ends((jax.random.randint(keys[2], (MB, NODES), 0, 4) < 3).astype(jnp.int32), jax.random.fold_in(keys[2], 1), 0, 1),
        "degree": draw_degree(jax.random.fold_in(keys[12], 71), 0),
        "neighbours": draw_neighbours(jax.random.fold_in(keys[12], 71), 0),
        "send_rows": draw_send_rows(jax.random.fold_in(keys[12], 71), 0),
        "w_left": noise(keys[6], (LAYERS, D, D), D ** -0.5, 0.375, (), jnp.float32),
        "w_right": noise(keys[7], (LAYERS, D, D), D ** -0.5, 0.375, (), jnp.float32),
        "w_res": noise(keys[8], (LAYERS, D, D), (4 * D) ** -0.5, 0.1875, (), jnp.float32),
        "attn_vec": noise(keys[9], (LAYERS, D), 0.25, 1.5, (), jnp.float32),
        "bn_gain": jnp.clip(1.0 + 0.1 * jax.random.normal(keys[10], (LAYERS, D), jnp.float32), 0.5, 1.5),
        "bn_shift": noise(keys[11], (LAYERS, D), 0.5, 2.0, (), jnp.float32),
    }


@jax.custom_vjp
def low(v):
    return lax.optimization_barrier(v.astype(jnp.bfloat16)).astype(jnp.float32)

@jax.custom_vjp
def low_back(v):
    return v

def low_keep(v):
    return (low(v), None)

def low_pass(kept, grad):
    return (grad,)

def back_keep(v):
    return (v, None)

def back_low(kept, grad):
    return (low(grad),)
low.defvjp(low_keep, low_pass)
low_back.defvjp(back_keep, back_low)
MASKED_SCORE = -1e+30
VARIANCE_EPS = 1e-05
PRECISE = lax.Precision.HIGHEST

def matmul(lhs_rows, rhs_rows):
    return jnp.dot(lhs_rows, rhs_rows, precision=PRECISE, preferred_element_type=jnp.float32)

def attend(row_table, right_rows, slot_index, slot_live, vector):
    node_count, feat_width = right_rows.shape
    slot_count = slot_index.shape[1]
    head_width = feat_width // HEADS
    picked = jnp.take(row_table, slot_index, axis=0)
    activated = jax.nn.silu(picked + right_rows[:, None, :])
    scores = lax.optimization_barrier(jnp.sum((activated * vector).reshape(node_count, slot_count, HEADS, head_width), axis=3))
    scores = jnp.where(slot_live[:, :, None], scores, MASKED_SCORE)
    highest = lax.optimization_barrier(jnp.max(scores, axis=1, keepdims=True))
    weights = jnp.exp(scores - highest)
    weights = weights / lax.optimization_barrier(jnp.sum(weights, axis=1, keepdims=True))
    values = picked.reshape(node_count, slot_count, HEADS, head_width)
    joined = jnp.einsum('nkh,nkhc->nhc', weights, values, precision=PRECISE)
    return joined.reshape(node_count, feat_width)

def block_attend(row_table, vector, pieces):
    return attend(row_table, pieces[0], pieces[1], pieces[2], vector)

def attend_blocks(row_table, right_rows, slot_index, slot_live, vector):
    node_count = right_rows.shape[0]
    block_rows = math.gcd(node_count, 4096)
    blocks = node_count // block_rows
    checked = jax.checkpoint(block_attend)
    result = lax.map(lambda pieces: checked(row_table, vector, pieces), (right_rows.reshape(blocks, block_rows, -1), slot_index.reshape(blocks, block_rows, -1), slot_live.reshape(blocks, block_rows, -1)))
    return result.reshape(node_count, -1)

def global_index(local_slots, send_list):
    owner = (jnp.arange(NODES, dtype=jnp.int32) // NODE_MB)[:, None]
    offset = local_slots - NODE_MB
    sender = jnp.clip(offset // SEND, 0, N_NODES - 1)
    within = offset % SEND
    picked = jnp.clip(sender * HALO + owner * SEND + within, 0, N_NODES * HALO - 1)
    remote = sender * NODE_MB + jnp.take(send_list, picked)
    return jnp.where(local_slots < NODE_MB, owner * NODE_MB + local_slots, remote).astype(jnp.int32)

def forward(features, w_left, w_right, w_res, attn_vec, bn_gain, bn_shift, slot_global, slot_live):
    results = []
    for batch_index in range(MB):
        hidden = features[batch_index]
        for layer_index in range(LAYERS):
            left_rows = matmul(hidden, w_left[layer_index])
            right_rows = matmul(hidden, w_right[layer_index])
            joined = attend_blocks(left_rows, right_rows, slot_global[batch_index], slot_live[batch_index], attn_vec[layer_index])
            mixed_rows = joined + matmul(hidden, w_res[layer_index])
            mean_row = lax.optimization_barrier(jnp.mean(mixed_rows, axis=0))
            inverse = lax.rsqrt(lax.optimization_barrier(jnp.mean(mixed_rows * mixed_rows, axis=0)) - mean_row * mean_row + VARIANCE_EPS)
            hidden = jax.nn.elu(bn_gain[layer_index] * ((mixed_rows - mean_row) * inverse) + bn_shift[layer_index])
        results.append(hidden)
    return jnp.stack(results)

def reference(features, cotangent, train_mask, degree, neighbours, send_rows, w_left, w_right, w_res, attn_vec, bn_gain, bn_shift):
    slot_global = jnp.stack([global_index(neighbours[batch_index], send_rows[batch_index]) for batch_index in range(MB)])
    slot_live = jnp.arange(SLOTS, dtype=jnp.int32)[None, None, :] < degree[:, :, None]

    def run(feats, left_w, right_w, skip_w, vector, gains, shifts):
        return forward(feats, left_w, right_w, skip_w, vector, gains, shifts, slot_global, slot_live)
    outputs, pull_back = jax.vjp(run, features, w_left, w_right, w_res, attn_vec, bn_gain, bn_shift)
    masked_rows = cotangent * train_mask.astype(cotangent.dtype)[:, :, None]
    grads = pull_back(masked_rows)
    return (outputs, grads[0], grads[1], grads[2], grads[3], grads[4], grads[5], grads[6])
```

```python
import functools
import types

import jax
import jax.numpy as jnp
from jax import lax
from jax.experimental import pallas as pl
from jax.experimental.pallas import tpu as pltpu
from jax.sharding import PartitionSpec as P

HEADS = 4
MASKED_SCORE = -1e30
VARIANCE_EPS = 1e-05
F32 = jnp.float32
BF16 = jnp.bfloat16
MESH = pl.DeviceIdType.MESH
LANES = 128
TILE = 8
CHUNK = 16

FEATURES, MIXED, SUMS, BACK_SUMS, BACK_ROWS, INPUT_ROWS, SMALL = range(7)
EXCHANGES = 7
CORE, SECTION, OUTER, OUTER_BACK, SECTION_BACK, CORE_BACK = range(6)
STAGES = 6


def halves(values):
    high = values.astype(BF16)
    return high, (values - high.astype(F32)).astype(BF16)


def mm(lhs, rhs):
    return jnp.dot(lhs, rhs, preferred_element_type=F32)


def mm_nt(lhs, rhs):
    return lax.dot_general(lhs, rhs, (((1,), (1,)), ((), ())), preferred_element_type=F32)


def mm3(lhs, rhs, product=mm):
    return product(lhs[0], rhs[0]) + product(lhs[1], rhs[0]) + product(lhs[0], rhs[1])


def iota(shape, dim):
    return lax.broadcasted_iota(jnp.int32, shape, dim)


def as_ones(condition):
    return jnp.where(condition, 1.0, 0.0).astype(BF16)


def sizes_of(sections, partitions, rows, width, slots, listed):
    z = types.SimpleNamespace()
    z.sections, z.partitions, z.outer = sections, partitions, partitions // 2
    z.rows, z.width, z.slots, z.listed = rows, width, slots, listed
    z.send = listed // partitions
    z.halo = partitions * TILE
    z.halo_pad = -(-z.halo // LANES) * LANES
    z.table = rows + z.halo_pad
    z.picked = rows + z.halo
    z.share = rows // sections
    z.piece = max(TILE, z.share // z.outer)
    z.owners = z.share // z.piece
    return z


def scratch_of(z):
    R, D, K, T = z.rows, z.width, z.slots, z.table
    S, O = z.sections, z.outer
    half = D // 2
    vmem = {
        "features_in": ((R, D), F32),
        "cotangent_in": ((R, D), F32),
        "mask_in": (None, jnp.int32),
        "degree_in": (None, jnp.int32),
        "slots_in": ((K, R), jnp.int32),
        "listed_in": (None, jnp.int32),
        "weights_in": ((3, 2, D, D), F32),
        "vector_in": ((2, D), F32),
        "gain_in": ((2, D), F32),
        "shift_in": ((2, D), F32),
        "weights_hi": ((2, 3, D, D), BF16),
        "weights_lo": ((2, 3, D, D), BF16),
        "prep": ((LANES, R), F32),
        "prep_t": ((R, LANES), F32),
        "listed_row": ((TILE, max(LANES, z.listed)), F32),
        "pick": ((K - 1, R, T), BF16),
        "pick_t": ((z.picked, (K - 1) * R), BF16),
        "list": ((z.halo, R), BF16),
        "list_t": ((R, z.halo_pad), BF16),
        "ones": ((2 * D, D), BF16),
        "h": ((T, D), F32),
        "h_hi": ((T, D), BF16),
        "h_lo": ((T, D), BF16),
        "ht_hi": ((2, D, T), BF16),
        "ht_lo": ((2, D, T), BF16),
        "table_hi": ((T, D), BF16),
        "table_lo": ((T, D), BF16),
        "taken": ((2, K, R, D), F32),
        "sig": ((2, K, R, D), F32),
        "alpha": ((2, K, R, D), F32),
        "joined": ((2, R, D), F32),
        "right": ((2, R, D), F32),
        "skip": ((R, D), F32),
        "mixed": ((R, D), F32),
        "normed": ((2, R, D), F32),
        "slope": ((2, R, D), F32),
        "halo_normed": ((z.halo, D), F32),
        "halo_slope": ((z.halo, D), F32),
        "pair": ((K, R, 2 * D), BF16),
        "score": ((K, R, D), F32),
        "dpre": ((R, D), F32),
        "dmixed": ((R, D), F32),
        "dm_hi": ((R, D), BF16),
        "dm_lo": ((R, D), BF16),
        "dr_hi": ((R, D), BF16),
        "dr_lo": ((R, D), BF16),
        "dl_hi": ((T, D), BF16),
        "dl_lo": ((T, D), BF16),
        "dleft_self": ((R, D), F32),
        "dleft_hi": (((K - 1) * R, D), BF16),
        "dleft_lo": (((K - 1) * R, D), BF16),
        "dh": ((R, D), F32),
        "outgoing": ((EXCHANGES, z.halo, D), F32),
        "incoming": ((EXCHANGES, z.halo, D), F32),
        "small": ((TILE, D), F32),
        "small_in": ((S, TILE, D), F32),
        "vector_out": ((2, D), F32),
        "gain_out": ((2, D), F32),
        "shift_out": ((2, D), F32),
        "out_rows": ((R, D), F32),
        "grad_rows": ((R, D), F32),
        "sums": ((2, 3, 2, R, half), F32),
        "from_core": ((2, 3, R, half), F32),
        "from_section": ((2, S - 1, 3, z.share, half), F32),
        "from_outer": ((2, O, 3, z.piece, half), F32),
        "whole": ((2, 3, R, half), F32),
    }
    return vmem


SEMAPHORES = {
    "load": (12,),
    "give": (EXCHANGES,),
    "take": (EXCHANGES,),
    "give_small": (1,),
    "take_small": (1,),
    "give_stage": (2, 3, STAGES),
    "take_stage": (2, 3, STAGES),
    "give_back": (2, 3),
    "take_back": (2, 3),
    "store": (16,),
}


def kernel(z, names, *refs):
    features, cotangent, train_mask, degree, neighbours, send_rows = refs[:6]
    w_left, w_right, w_res, attn_vec, bn_gain, bn_shift = refs[6:12]
    out, grad_in, g_left, g_right, g_res, g_vec, g_gain, g_shift = refs[12:20]
    v = types.SimpleNamespace(**dict(zip(names, refs[20:])))
    grads_out = (g_left, g_right, g_res)
    R, D, K, T = z.rows, z.width, z.slots, z.table
    S, N, O = z.sections, z.partitions, z.outer
    half = D // 2
    total_rows = R * N
    sec = lax.axis_index("section")
    me = lax.axis_index("nodes")
    core = lax.rem(me, 2)
    outer = lax.div(me, 2)
    mate = me + 1 - 2 * core

    barrier = pltpu.get_barrier_semaphore()

    def greet(step, carry):
        pl.semaphore_signal(
            barrier, inc=1, device_id={"nodes": lax.rem(me + step, N)}, device_id_type=MESH
        )
        return carry

    lax.fori_loop(1, N, greet, 0)
    for step in range(1, S):
        pl.semaphore_signal(
            barrier, inc=1, device_id={"section": lax.rem(sec + step, S)}, device_id_type=MESH
        )

    loads = []
    for source, target in (
        (features.at[sec], v.features_in),
        (send_rows, v.listed_in),
        (w_left, v.weights_in.at[0]),
        (w_right, v.weights_in.at[1]),
        (w_res, v.weights_in.at[2]),
        (neighbours.at[sec], v.slots_in),
        (degree, v.degree_in),
        (train_mask, v.mask_in),
        (attn_vec, v.vector_in),
        (bn_gain, v.gain_in),
        (bn_shift, v.shift_in),
        (cotangent.at[sec], v.cotangent_in),
    ):
        copy = pltpu.make_async_copy(source, target, v.load.at[len(loads)])
        copy.start()
        loads.append(copy)

    def rows_loop(body, start):
        return lax.fori_loop(0, R // CHUNK, body, start)

    def chunk(i):
        return pl.ds(pl.multiple_of(i * CHUNK, CHUNK), CHUNK)

    def fold(values):
        return jnp.sum(values.reshape(values.shape[0] // TILE, TILE, values.shape[1]), axis=0)

    def add_rows(values):
        return jnp.sum(values, axis=0, keepdims=True)

    def start_exchange(which, one_tile=False):
        def send(step, carry):
            other = lax.rem(me + step, N)
            place = 0 if one_tile else pl.multiple_of(other * TILE, TILE)
            pltpu.make_async_remote_copy(
                src_ref=v.outgoing.at[which, pl.ds(place, TILE)],
                dst_ref=v.incoming.at[which, pl.ds(pl.multiple_of(me * TILE, TILE), TILE)],
                send_sem=v.give.at[which],
                recv_sem=v.take.at[which],
                device_id={"nodes": other},
                device_id_type=MESH,
            ).start()
            return carry

        lax.fori_loop(1, N, send, 0)
        own = pl.ds(pl.multiple_of(me * TILE, TILE), TILE)
        mine = pl.ds(0, TILE) if one_tile else own
        v.incoming[which, own, :] = v.outgoing[which, mine, :]

    def wait_bytes(ref, semaphore):
        pltpu.make_async_copy(ref, ref, semaphore).wait()

    def end_exchange(which):
        wait_bytes(v.incoming.at[which, pl.ds(0, (N - 1) * TILE)], v.take.at[which])

    def row_in_tile(rows):
        return lax.rem(iota((rows, D), 0), TILE)

    def with_sums(values, first, second):
        row = row_in_tile(values.shape[0])
        return values + jnp.where(row == z.send, first, 0.0) + jnp.where(row == z.send + 1, second, 0.0)

    def arrived_sums(which):
        tile = jnp.sum(v.incoming[which].reshape(N, TILE, D), axis=0)
        return tile[z.send : z.send + 1, :], tile[z.send + 1 : z.send + 2, :]

    def arrived_rows(which):
        values = v.incoming[which]
        return jnp.where(row_in_tile(z.halo) < z.send, values, 0.0)

    def give_rows_back(which):
        high, low = halves(arrived_rows(which))
        listed = v.list_t[:, : z.halo]
        return mm(listed, high) + mm(listed, low)

    def stage_copy(layer, first, stage, source, target, device):
        copy = pltpu.make_async_remote_copy(
            src_ref=source,
            dst_ref=target,
            send_sem=v.give_stage.at[layer, first, stage],
            recv_sem=v.take_stage.at[layer, first, stage],
            device_id=device,
            device_id_type=MESH,
        )
        copy.start()

    sends_to_end = []

    def stage_sent(layer, first, stage, ref):
        sends_to_end.append((ref, v.give_stage.at[layer, first, stage]))

    section_rows = pl.ds(pl.multiple_of(sec * z.share, TILE), z.share)

    def piece_rows(which):
        return pl.ds(pl.multiple_of(sec * z.share + which * z.piece, TILE), z.piece)

    def outer_device(which):
        return {"nodes": which * 2 + core}

    def start_stage(stage, layer, first, count):
        mats = pl.ds(first, count)
        if stage == CORE:
            stage_copy(
                layer,
                first,
                stage,
                v.sums.at[layer, mats, 1 - core],
                v.from_core.at[layer, mats],
                {"nodes": mate},
            )
            stage_sent(layer, first, stage, v.from_core.at[layer, mats])
        elif stage == SECTION:
            for step in range(1, S):
                other = lax.rem(sec + step, S)
                rows = pl.ds(pl.multiple_of(other * z.share, TILE), z.share)
                stage_copy(
                    layer,
                    first,
                    stage,
                    v.sums.at[layer, mats, core, rows],
                    v.from_section.at[layer, step - 1, mats],
                    {"section": other},
                )
            stage_sent(layer, first, stage, v.from_section.at[layer, :, mats])
        elif stage == OUTER:
            if z.owners == O:
                for step in range(1, O):
                    other = lax.rem(outer + step, O)
                    stage_copy(
                        layer,
                        first,
                        stage,
                        v.sums.at[layer, mats, core, piece_rows(other)],
                        v.from_outer.at[layer, step, mats],
                        outer_device(other),
                    )
                stage_sent(layer, first, stage, v.from_outer.at[layer, pl.ds(1, O - 1), mats])
            else:
                for other in range(z.owners):

                    @pl.when(outer != other)
                    def _():
                        stage_copy(
                            layer,
                            first,
                            stage,
                            v.sums.at[layer, mats, core, piece_rows(other)],
                            v.from_outer.at[layer, lax.rem(outer - other + O, O), mats],
                            outer_device(other),
                        )
                        wait_bytes(
                            v.from_outer.at[layer, 0, mats], v.give_stage.at[layer, first, stage]
                        )

        elif stage == OUTER_BACK:

            def send_all():
                for step in range(1, O):
                    stage_copy(
                        layer,
                        first,
                        stage,
                        v.whole.at[layer, mats, piece_rows(outer)],
                        v.whole.at[layer, mats, piece_rows(outer)],
                        outer_device(lax.rem(outer + step, O)),
                    )

            if z.owners == O:
                send_all()
                stage_sent(layer, first, stage, v.from_outer.at[layer, pl.ds(1, O - 1), mats])
            else:

                @pl.when(outer < z.owners)
                def _():
                    send_all()
                    wait_bytes(
                        v.from_outer.at[layer, pl.ds(1, O - 1), mats],
                        v.give_stage.at[layer, first, stage],
                    )

        elif stage == SECTION_BACK:
            for step in range(1, S):
                stage_copy(
                    layer,
                    first,
                    stage,
                    v.whole.at[layer, mats, section_rows],
                    v.whole.at[layer, mats, section_rows],
                    {"section": lax.rem(sec + step, S)},
                )
            stage_sent(layer, first, stage, v.from_section.at[layer, :, mats])
        elif stage == CORE_BACK:
            columns = pl.ds(pl.multiple_of(core * half, LANES), half)
            for mat in range(first, first + count):
                source = v.whole.at[layer, mat]
                target = grads_out[mat].at[layer, :, columns]
                pltpu.make_async_remote_copy(
                    src_ref=source,
                    dst_ref=target,
                    send_sem=v.give_back.at[layer, mat],
                    recv_sem=v.take_back.at[layer, mat],
                    device_id={"nodes": mate},
                    device_id_type=MESH,
                ).start()
                pltpu.make_async_copy(source, target, v.store.at[layer * 3 + mat]).start()

    def end_stage(stage, layer, first, count):
        mats = pl.ds(first, count)
        taken = v.take_stage.at[layer, first, stage]
        each = range(first, first + count)
        if stage == CORE:
            wait_bytes(v.from_core.at[layer, mats], taken)
            for mat in each:
                v.sums[layer, mat, core] = v.sums[layer, mat, core] + v.from_core[layer, mat]
        elif stage == SECTION:
            wait_bytes(v.from_section.at[layer, :, mats], taken)
            for mat in each:
                value = v.sums[layer, mat, core, section_rows, :]
                for step in range(S - 1):
                    value = value + v.from_section[layer, step, mat]
                v.sums[layer, mat, core, section_rows, :] = value
        elif stage == OUTER:

            def add():
                wait_bytes(v.from_outer.at[layer, pl.ds(1, O - 1), mats], taken)
                for mat in each:
                    value = v.sums[layer, mat, core, piece_rows(outer), :]
                    for step in range(1, O):
                        value = value + v.from_outer[layer, step, mat]
                    v.whole[layer, mat, piece_rows(outer), :] = value

            if z.owners == O:
                add()
            else:
                pl.when(outer < z.owners)(add)
        elif stage == OUTER_BACK:
            if z.owners == O:
                wait_bytes(v.from_outer.at[layer, pl.ds(1, O - 1), mats], taken)
            else:
                wait_bytes(v.from_outer.at[layer, pl.ds(1, z.owners - 1), mats], taken)

                @pl.when(outer >= z.owners)
                def _():
                    wait_bytes(v.from_outer.at[layer, 0, mats], taken)

        elif stage == SECTION_BACK:
            wait_bytes(v.from_section.at[layer, :, mats], taken)
        elif stage == CORE_BACK:
            columns = pl.ds(pl.multiple_of(core * half, LANES), half)
            for mat in each:
                source = v.whole.at[layer, mat]
                target = grads_out[mat].at[layer, :, columns]
                wait_bytes(source, v.give_back.at[layer, mat])
                wait_bytes(source, v.take_back.at[layer, mat])
                pltpu.make_async_copy(source, target, v.store.at[layer * 3 + mat]).wait()

    loads[1].wait()
    v.listed_row[...] = jnp.zeros_like(v.listed_row)
    v.listed_row[0:1, : z.listed] = v.listed_in[pl.ds(sec, 1), :].astype(F32)
    spread_from = iota((v.listed_row.shape[1], z.halo_pad), 0)
    spread_to = iota((v.listed_row.shape[1], z.halo_pad), 1)
    spread = as_ones(
        (lax.div(spread_from, z.send) == lax.div(spread_to, TILE))
        & (lax.rem(spread_from, z.send) == lax.rem(spread_to, TILE))
        & (spread_from < z.listed)
    )
    listed = mm(v.listed_row[...].astype(BF16), spread)[0:1, :]
    place = iota((1, z.halo_pad), 1)
    real = (lax.rem(place, TILE) < z.send) & (place < z.halo)
    listed = jnp.where(real, listed, -1.0)
    list_t = jnp.where(iota((R, z.halo_pad), 0).astype(F32) == listed, 1.0, 0.0)
    v.list_t[...] = list_t.astype(BF16)
    v.list[...] = list_t.T[: z.halo, :].astype(BF16)

    loads[0].wait()
    own = v.features_in[...]
    v.h[pl.ds(0, R), :] = own
    high, low = halves(own)
    v.h_hi[pl.ds(0, R), :] = high
    v.h_lo[pl.ds(0, R), :] = low
    v.outgoing[FEATURES] = mm(v.list[...], high) + mm(v.list[...], low)
    pl.semaphore_wait(barrier, N - 1 + S - 1)
    start_exchange(FEATURES)

    for load in loads[2:5]:
        load.wait()
    for layer in range(2):
        for mat in range(3):
            high, low = halves(v.weights_in[mat, layer])
            v.weights_hi[layer, mat] = high
            v.weights_lo[layer, mat] = low

    def weight(layer, mat):
        return v.weights_hi[layer, mat], v.weights_lo[layer, mat]

    for load in loads[5:11]:
        load.wait()
    named = v.slots_in[...]
    offset = named - R
    remote = R + lax.div(offset, z.send) * TILE + lax.rem(offset, z.send)
    named = jnp.where(named < R, named, remote).astype(F32)
    v.prep[...] = jnp.zeros_like(v.prep)
    v.prep[pl.ds(0, K), :] = named
    v.prep[pl.ds(K, 1), :] = v.degree_in[pl.ds(sec, 1), :].astype(F32)
    v.prep[pl.ds(K + 1, 1), :] = v.mask_in[pl.ds(sec, 1), :].astype(F32)
    v.prep_t[...] = v.prep[...].T
    for slot in range(1, K):
        column = v.prep_t[:, slot : slot + 1]
        v.pick[slot - 1] = as_ones(iota((R, T), 1).astype(F32) == column)
        row = v.prep[slot : slot + 1, :]
        v.pick_t[:, (slot - 1) * R : slot * R] = as_ones(iota((z.picked, R), 0).astype(F32) == row)
    group = D // HEADS
    block_row = lax.div(lax.rem(iota((2 * D, D), 0), D), group)
    v.ones[...] = as_ones(block_row == lax.div(iota((2 * D, D), 1), group))

    def project(layer):
        rows = pl.ds(0, R)
        own = (v.h_hi[rows, :], v.h_lo[rows, :])
        left = mm3(own, weight(layer, 0))
        v.taken[layer, 0] = left
        high, low = halves(left)
        v.table_hi[rows, :] = high
        v.table_lo[rows, :] = low
        v.right[layer] = mm3(own, weight(layer, 1))
        v.skip[...] = mm3(own, weight(layer, 2))

    def project_halo(layer):
        rows = pl.ds(R, z.halo_pad)
        left = mm3((v.h_hi[rows, :], v.h_lo[rows, :]), weight(layer, 0))
        high, low = halves(left)
        v.table_hi[rows, :] = high
        v.table_lo[rows, :] = low

    def store_halo(values):
        if z.halo < z.halo_pad:
            rest = pl.ds(R + z.halo, z.halo_pad - z.halo)
            v.h[rest, :] = jnp.zeros((z.halo_pad - z.halo, D), F32)
            v.h_hi[rest, :] = jnp.zeros((z.halo_pad - z.halo, D), BF16)
            v.h_lo[rest, :] = jnp.zeros((z.halo_pad - z.halo, D), BF16)
        rows = pl.ds(R, z.halo)
        v.h[rows, :] = values
        high, low = halves(values)
        v.h_hi[rows, :] = high
        v.h_lo[rows, :] = low

    def keep_transposed(layer):
        high, low = halves(v.h[...].T)
        v.ht_hi[layer] = high
        v.ht_lo[layer] = low

    def head_sums():
        def one(slot, carry):
            v.score[slot] = mm(v.pair[slot], v.ones[...])
            return carry

        lax.fori_loop(0, K, one, 0)

    def store_pair(slot, rows, values):
        high, low = halves(values)
        v.pair[slot, rows, pl.ds(0, D)] = high
        v.pair[slot, rows, pl.ds(D, D)] = low

    def attend(layer):
        def gather(slot, carry):
            pick = v.pick[slot - 1]
            v.taken[layer, slot] = mm(pick, v.table_hi[...]) + mm(pick, v.table_lo[...])
            return carry

        lax.fori_loop(1, K, gather, 0)
        vector = v.vector_in[layer : layer + 1, :]

        def activate(i, carry):
            rows = chunk(i)
            right = v.right[layer, rows, :]
            for slot in range(K):
                u = v.taken[layer, slot, rows, :] + right
                sig = 1.0 / (1.0 + jnp.exp(-u))
                v.sig[layer, slot, rows, :] = sig
                store_pair(slot, rows, u * sig * vector)
            return carry

        rows_loop(activate, 0)
        head_sums()

        def mix(i, carry):
            rows = chunk(i)
            count = jnp.broadcast_to(v.prep_t[rows, K : K + 1], (CHUNK, D))
            scores = [
                jnp.where(count > slot, v.score[slot, rows, :], MASKED_SCORE) for slot in range(K)
            ]
            highest = functools.reduce(jnp.maximum, scores)
            powers = [jnp.exp(score - highest) for score in scores]
            scale = 1.0 / functools.reduce(jnp.add, powers)
            joined = jnp.zeros((CHUNK, D), F32)
            for slot in range(K):
                alpha = powers[slot] * scale
                v.alpha[layer, slot, rows, :] = alpha
                joined = joined + alpha * v.taken[layer, slot, rows, :]
            v.joined[layer, rows, :] = joined
            mixed = joined + v.skip[rows, :]
            v.mixed[rows, :] = mixed
            return carry[0] + fold(mixed), carry[1] + fold(mixed * mixed)

        nothing = jnp.zeros((TILE, D), F32)
        first, second = rows_loop(mix, (nothing, nothing))
        return add_rows(first), add_rows(second)

    def moments(which):
        first, second = arrived_sums(which)
        mean = first / total_rows
        return mean, lax.rsqrt(second / total_rows - mean * mean + VARIANCE_EPS)

    def activation(layer, mixed, mean, inverse):
        normed = (mixed - mean) * inverse
        pre = v.gain_in[layer : layer + 1, :] * normed + v.shift_in[layer : layer + 1, :]
        power = jnp.exp(jnp.minimum(pre, 0.0))
        return normed, jnp.where(pre > 0, 1.0, power), jnp.where(pre > 0, pre, power - 1.0)

    def sums_tile(which, first, second):
        v.outgoing[which, pl.ds(0, TILE), :] = with_sums(jnp.zeros((TILE, D), F32), first, second)

    def list_rows(values):
        high, low = halves(values)
        return mm(v.list[...], high) + mm(v.list[...], low)

    project(0)
    end_exchange(FEATURES)
    store_halo(arrived_rows(FEATURES))
    project_halo(0)
    first, second = attend(0)
    v.outgoing[MIXED] = with_sums(list_rows(v.mixed[...]), first, second)
    start_exchange(MIXED)
    keep_transposed(0)
    end_exchange(MIXED)
    mean0, inverse0 = moments(MIXED)

    def finish0(i, carry):
        rows = chunk(i)
        normed, slope, hidden = activation(0, v.mixed[rows, :], mean0, inverse0)
        v.normed[0, rows, :] = normed
        v.slope[0, rows, :] = slope
        v.h[rows, :] = hidden
        high, low = halves(hidden)
        v.h_hi[rows, :] = high
        v.h_lo[rows, :] = low
        return carry

    rows_loop(finish0, 0)
    normed, slope, hidden = activation(0, arrived_rows(MIXED), mean0, inverse0)
    v.halo_normed[...] = normed
    v.halo_slope[...] = slope
    store_halo(jnp.where(row_in_tile(z.halo) < z.send, hidden, 0.0))

    project(1)
    project_halo(1)
    first, second = attend(1)
    sums_tile(SUMS, first, second)
    start_exchange(SUMS, True)
    keep_transposed(1)
    loads[11].wait()
    end_exchange(SUMS)
    mean1, inverse1 = moments(SUMS)

    def finish1(i, carry):
        rows = chunk(i)
        normed, slope, hidden = activation(1, v.mixed[rows, :], mean1, inverse1)
        v.normed[1, rows, :] = normed
        v.out_rows[rows, :] = hidden
        dpre = v.cotangent_in[rows, :] * v.prep_t[rows, K + 1 : K + 2] * slope
        v.dpre[rows, :] = dpre
        return carry[0] + fold(dpre), carry[1] + fold(dpre * normed)

    nothing = jnp.zeros((TILE, D), F32)
    first, second = rows_loop(finish1, (nothing, nothing))
    shift1, gain1 = add_rows(first), add_rows(second)
    sums_tile(BACK_SUMS, shift1, gain1)
    start_exchange(BACK_SUMS, True)
    out_copy = pltpu.make_async_copy(v.out_rows, out.at[0], v.store.at[6])
    out_copy.start()

    def normalization_back(layer, which, inverse):
        first, second = arrived_sums(which)
        first = first / total_rows
        second = second / total_rows
        scale = inverse * v.gain_in[layer : layer + 1, :]

        def one(i, carry):
            rows = chunk(i)
            dmixed = scale * (v.dpre[rows, :] - first - v.normed[layer, rows, :] * second)
            v.dmixed[rows, :] = dmixed
            high, low = halves(dmixed)
            v.dm_hi[rows, :] = high
            v.dm_lo[rows, :] = low
            return carry

        rows_loop(one, 0)

    def attend_back(layer, between=()):
        vector = v.vector_in[layer : layer + 1, :]

        def differences(i, carry):
            rows = chunk(i)
            joined = v.joined[layer, rows, :]
            dmixed = v.dmixed[rows, :]
            for slot in range(K):
                store_pair(slot, rows, (v.taken[layer, slot, rows, :] - joined) * dmixed)
            return carry

        rows_loop(differences, 0)
        head_sums()
        for step in between[:1]:
            step()

        def one(i, carry):
            rows = chunk(i)
            right = v.right[layer, rows, :]
            dmixed = v.dmixed[rows, :]
            dright = jnp.zeros((CHUNK, D), F32)
            for slot in range(K):
                u = v.taken[layer, slot, rows, :] + right
                sig = v.sig[layer, slot, rows, :]
                alpha = v.alpha[layer, slot, rows, :]
                dscore = alpha * v.score[slot, rows, :]
                carry = carry + fold(dscore * u * sig)
                du = dscore * vector * sig * (1.0 + u * (1.0 - sig))
                dright = dright + du
                dleft = du + alpha * dmixed
                if slot == 0:
                    v.dleft_self[rows, :] = dleft
                else:
                    high, low = halves(dleft)
                    place = pl.ds(pl.multiple_of((slot - 1) * R + i * CHUNK, CHUNK), CHUNK)
                    v.dleft_hi[place, :] = high
                    v.dleft_lo[place, :] = low
            high, low = halves(dright)
            v.dr_hi[rows, :] = high
            v.dr_lo[rows, :] = low
            return carry

        vector_sum = rows_loop(one, jnp.zeros((TILE, D), F32))
        for step in between[1:]:
            step()

        def scattered(rows):
            pick = v.pick_t[rows, :]
            return mm(pick, v.dleft_hi[...]) + mm(pick, v.dleft_lo[...])

        rows = pl.ds(0, R)
        high, low = halves(scattered(rows) + v.dleft_self[...])
        v.dl_hi[rows, :] = high
        v.dl_lo[rows, :] = low
        rows = pl.ds(R, z.halo)
        high, low = halves(scattered(rows))
        v.dl_hi[rows, :] = high
        v.dl_lo[rows, :] = low
        return add_rows(vector_sum)

    def dleft(rows):
        return v.dl_hi[rows, :], v.dl_lo[rows, :]

    def input_back(layer):
        own = pl.ds(0, R)
        v.dh[...] = (
            mm3(dleft(own), weight(layer, 0), mm_nt)
            + mm3((v.dr_hi[...], v.dr_lo[...]), weight(layer, 1), mm_nt)
            + mm3((v.dm_hi[...], v.dm_lo[...]), weight(layer, 2), mm_nt)
        )
        return mm3(dleft(pl.ds(R, z.halo)), weight(layer, 0), mm_nt)

    def weight_grad(layer, mat):
        if mat == 0:
            upstream = (v.dl_hi[...], v.dl_lo[...])
            inputs = (v.ht_hi[layer], v.ht_lo[layer])
        else:
            upstream = (v.dr_hi[...], v.dr_lo[...]) if mat == 1 else (v.dm_hi[...], v.dm_lo[...])
            inputs = (v.ht_hi[layer, :, pl.ds(0, R)], v.ht_lo[layer, :, pl.ds(0, R)])
        value = mm3(inputs, upstream)
        v.sums[layer, mat, 0] = value[:, :half]
        v.sums[layer, mat, 1] = value[:, half:]

    if z.halo < z.halo_pad:
        rest = pl.ds(R + z.halo, z.halo_pad - z.halo)
        v.dl_hi[rest, :] = jnp.zeros((z.halo_pad - z.halo, D), BF16)
        v.dl_lo[rest, :] = jnp.zeros((z.halo_pad - z.halo, D), BF16)

    end_exchange(BACK_SUMS)
    normalization_back(1, BACK_SUMS, inverse1)
    vector1 = attend_back(1)
    halo_back = input_back(1)
    dpre = v.dh[...] * v.slope[0]
    halo_dpre = halo_back * v.halo_slope[...]
    shift0 = add_rows(dpre) + add_rows(halo_dpre)
    gain0 = add_rows(dpre * v.normed[0]) + add_rows(halo_dpre * v.halo_normed[...])
    v.outgoing[BACK_ROWS] = with_sums(halo_back, shift0, gain0)
    start_exchange(BACK_ROWS)
    for mat in range(3):
        weight_grad(1, mat)
    start_stage(CORE, 1, 0, 3)
    end_exchange(BACK_ROWS)
    v.dpre[...] = (v.dh[...] + give_rows_back(BACK_ROWS)) * v.slope[0]

    normalization_back(0, BACK_ROWS, inverse0)
    end_stage(CORE, 1, 0, 3)
    start_stage(SECTION, 1, 0, 3)

    def step1():
        end_stage(SECTION, 1, 0, 3)
        start_stage(OUTER, 1, 0, 3)

    def step2():
        end_stage(OUTER, 1, 0, 3)
        start_stage(OUTER_BACK, 1, 0, 3)

    vector0 = attend_back(0, (step1, step2))
    for mat in range(3):
        weight_grad(0, mat)
    start_stage(CORE, 0, 0, 3)
    end_stage(OUTER_BACK, 1, 0, 3)
    start_stage(SECTION_BACK, 1, 0, 3)

    rows = (vector0, vector1, gain0, gain1, shift0, shift1)
    row = iota((TILE, D), 0)
    tile = jnp.zeros((TILE, D), F32)
    for place, value in enumerate(rows):
        tile = jnp.where(row == place, value, tile)
    v.outgoing[SMALL, pl.ds(0, TILE), :] = tile
    start_exchange(SMALL, True)

    halo_back = input_back(0)
    v.outgoing[INPUT_ROWS] = halo_back
    start_exchange(INPUT_ROWS)

    end_stage(CORE, 0, 0, 3)
    start_stage(SECTION, 0, 0, 3)
    end_exchange(SMALL)
    v.small[...] = jnp.sum(v.incoming[SMALL].reshape(N, TILE, D), axis=0)
    for step in range(1, S):
        pltpu.make_async_remote_copy(
            src_ref=v.small,
            dst_ref=v.small_in.at[step],
            send_sem=v.give_small.at[0],
            recv_sem=v.take_small.at[0],
            device_id={"section": lax.rem(sec + step, S)},
            device_id_type=MESH,
        ).start()
    end_stage(SECTION_BACK, 1, 0, 3)
    start_stage(CORE_BACK, 1, 0, 3)
    end_exchange(INPUT_ROWS)
    v.grad_rows[...] = v.dh[...] + give_rows_back(INPUT_ROWS)
    grad_copy = pltpu.make_async_copy(v.grad_rows, grad_in.at[0], v.store.at[7])
    grad_copy.start()
    end_stage(SECTION, 0, 0, 3)
    start_stage(OUTER, 0, 0, 3)
    wait_bytes(v.small_in.at[pl.ds(1, S - 1)], v.take_small.at[0])
    value = v.small[...]
    for step in range(1, S):
        value = value + v.small_in[step]
    last = []
    for place, (buffer, target) in enumerate(
        ((v.vector_out, g_vec), (v.gain_out, g_gain), (v.shift_out, g_shift))
    ):
        buffer[...] = value[2 * place : 2 * place + 2, :]
        copy = pltpu.make_async_copy(buffer, target, v.store.at[8 + place])
        copy.start()
        last.append(copy)
    end_stage(OUTER, 0, 0, 3)
    start_stage(OUTER_BACK, 0, 0, 3)
    end_stage(OUTER_BACK, 0, 0, 3)
    start_stage(SECTION_BACK, 0, 0, 3)
    end_stage(SECTION_BACK, 0, 0, 3)
    start_stage(CORE_BACK, 0, 0, 3)
    out_copy.wait()
    grad_copy.wait()
    for copy in last:
        copy.wait()
    for which in range(EXCHANGES):
        wait_bytes(v.outgoing.at[which, pl.ds(0, (N - 1) * TILE)], v.give.at[which])
    wait_bytes(v.small_in.at[pl.ds(1, S - 1)], v.give_small.at[0])
    for ref, semaphore in sends_to_end:
        wait_bytes(ref, semaphore)
    end_stage(CORE_BACK, 1, 0, 3)
    end_stage(CORE_BACK, 0, 0, 3)


def body(
    features,
    cotangent,
    train_mask,
    degree,
    neighbours,
    send_rows,
    w_left,
    w_right,
    w_res,
    attn_vec,
    bn_gain,
    bn_shift,
):
    batches, rows, width = features.shape
    sections = lax.axis_size("section")
    assert batches == sections
    z = sizes_of(
        sections, lax.axis_size("nodes"), rows, width, neighbours.shape[2], send_rows.shape[1]
    )
    shapes = scratch_of(z)
    shapes["mask_in"] = (train_mask.shape, jnp.int32)
    shapes["degree_in"] = (degree.shape, jnp.int32)
    shapes["listed_in"] = (send_rows.shape, jnp.int32)
    scratch = [pltpu.VMEM(shape, dtype) for shape, dtype in shapes.values()]
    scratch += [pltpu.SemaphoreType.DMA(shape) for shape in SEMAPHORES.values()]
    names = list(shapes) + list(SEMAPHORES)
    anywhere = pl.BlockSpec(memory_space=pl.ANY)
    square = jax.ShapeDtypeStruct((2, width, width), F32)
    columns = jax.ShapeDtypeStruct((2, width), F32)
    block = jax.ShapeDtypeStruct((1, rows, width), F32)
    return pl.pallas_call(
        functools.partial(kernel, z, names),
        out_shape=(block, block, square, square, square, columns, columns, columns),
        in_specs=[anywhere] * 12,
        out_specs=(anywhere,) * 8,
        scratch_shapes=scratch,
        compiler_params=pltpu.CompilerParams(
            collective_id=0, has_side_effects=True, vmem_limit_bytes=56 * 1024 * 1024
        ),
    )(
        features,
        cotangent,
        train_mask,
        degree,
        jnp.transpose(neighbours, (0, 2, 1)),
        send_rows,
        w_left,
        w_right,
        w_res,
        attn_vec,
        bn_gain,
        bn_shift,
    )


def solution(mesh):
    return jax.shard_map(
        body,
        mesh=mesh,
        in_specs=(
            P(None, "nodes", None),
            P(None, "nodes", None),
            P(None, "nodes"),
            P(None, "nodes"),
            P(None, "nodes", None),
            P(None, "nodes"),
            P(),
            P(),
            P(),
            P(),
            P(),
            P(),
        ),
        out_specs=(
            P("section", "nodes", None),
            P("section", "nodes", None),
            P(),
            P(),
            P(),
            P(),
            P(),
            P(),
        ),
        check_vma=False,
    )
```

```python
import functools
import types

import jax
import jax.numpy as jnp
from jax import lax
from jax.experimental import pallas as pl
from jax.experimental.pallas import tpu as pltpu
from jax.sharding import PartitionSpec as P

HEADS = 4
MASKED_SCORE = -1e30
VARIANCE_EPS = 1e-05
F32 = jnp.float32
BF16 = jnp.bfloat16
MESH = pl.DeviceIdType.MESH
UNROLL = 4
LANES = 128
TILE = 8
CHUNK = 16

FEATURES, MIXED, SUMS, BACK_SUMS, BACK_ROWS, INPUT_ROWS, SMALL = range(7)
EXCHANGES = 7
CORE, SECTION, OUTER, OUTER_BACK, SECTION_BACK, CORE_BACK = range(6)
STAGES = 6


def halves(values):
    high = values.astype(BF16)
    return high, (values - high.astype(F32)).astype(BF16)


def mm(lhs, rhs):
    return jnp.dot(lhs, rhs, preferred_element_type=F32)


def mm_nt(lhs, rhs):
    return lax.dot_general(lhs, rhs, (((1,), (1,)), ((), ())), preferred_element_type=F32)


def mm3(lhs, rhs, product=mm):
    return product(lhs[0], rhs[0]) + product(lhs[1], rhs[0]) + product(lhs[0], rhs[1])


def iota(shape, dim):
    return lax.broadcasted_iota(jnp.int32, shape, dim)


def as_ones(condition):
    return jnp.where(condition, 1.0, 0.0).astype(BF16)


def sizes_of(sections, partitions, rows, width, slots, listed):
    z = types.SimpleNamespace()
    z.sections, z.partitions, z.outer = sections, partitions, partitions // 2
    z.rows, z.width, z.slots, z.listed = rows, width, slots, listed
    z.send = listed // partitions
    z.halo = partitions * TILE
    z.halo_pad = -(-z.halo // LANES) * LANES
    z.table = rows + z.halo_pad
    z.picked = rows + z.halo
    z.share = rows // sections
    z.piece = max(TILE, z.share // z.outer)
    z.owners = z.share // z.piece
    return z


def scratch_of(z):
    R, D, K, T = z.rows, z.width, z.slots, z.table
    S, O = z.sections, z.outer
    half = D // 2
    vmem = {
        "features_in": ((R, D), F32),
        "cotangent_in": ((R, D), F32),
        "mask_in": (None, jnp.int32),
        "degree_in": (None, jnp.int32),
        "slots_in": ((K, R), jnp.int32),
        "listed_in": (None, jnp.int32),
        "weights_in": ((3, 2, D, D), F32),
        "vector_in": ((2, D), F32),
        "gain_in": ((2, D), F32),
        "shift_in": ((2, D), F32),
        "weights_hi": ((2, 3, D, D), BF16),
        "weights_lo": ((2, 3, D, D), BF16),
        "prep": ((LANES, R), F32),
        "prep_t": ((R, LANES), F32),
        "listed_row": ((TILE, max(LANES, z.listed)), F32),
        "pick": ((K - 1, R, T), BF16),
        "pick_t": ((z.picked, (K - 1) * R), BF16),
        "list": ((z.halo, R), BF16),
        "list_t": ((R, z.halo_pad), BF16),
        "ones": ((2 * D, D), BF16),
        "h": ((T, D), F32),
        "h_hi": ((T, D), BF16),
        "h_lo": ((T, D), BF16),
        "ht_hi": ((2, D, T), BF16),
        "ht_lo": ((2, D, T), BF16),
        "table_hi": ((T, D), BF16),
        "table_lo": ((T, D), BF16),
        "taken": ((2, K, R, D), F32),
        "sig": ((2, K, R, D), F32),
        "alpha": ((2, K, R, D), F32),
        "joined": ((2, R, D), F32),
        "right": ((2, R, D), F32),
        "skip": ((R, D), F32),
        "mixed": ((R, D), F32),
        "normed": ((2, R, D), F32),
        "slope": ((2, R, D), F32),
        "halo_normed": ((z.halo, D), F32),
        "halo_slope": ((z.halo, D), F32),
        "pair": ((K, R, 2 * D), BF16),
        "score": ((K, R, D), F32),
        "dpre": ((R, D), F32),
        "dmixed": ((R, D), F32),
        "dm_hi": ((R, D), BF16),
        "dm_lo": ((R, D), BF16),
        "dr_hi": ((R, D), BF16),
        "dr_lo": ((R, D), BF16),
        "dl_hi": ((T, D), BF16),
        "dl_lo": ((T, D), BF16),
        "dleft_self": ((R, D), F32),
        "dleft_hi": (((K - 1) * R, D), BF16),
        "dleft_lo": (((K - 1) * R, D), BF16),
        "dh": ((R, D), F32),
        "outgoing": ((EXCHANGES, z.halo, D), F32),
        "incoming": ((EXCHANGES, z.halo, D), F32),
        "small": ((TILE, D), F32),
        "small_in": ((S, TILE, D), F32),
        "vector_out": ((2, D), F32),
        "gain_out": ((2, D), F32),
        "shift_out": ((2, D), F32),
        "out_rows": ((R, D), F32),
        "grad_rows": ((R, D), F32),
        "sums": ((2, 3, 2, R, half), F32),
        "from_core": ((2, 3, R, half), F32),
        "from_section": ((2, S - 1, 3, z.share, half), F32),
        "from_outer": ((2, O, 3, z.piece, half), F32),
        "whole": ((2, 3, R, half), F32),
    }
    return vmem


SEMAPHORES = {
    "load": (12,),
    "give": (EXCHANGES,),
    "take": (EXCHANGES,),
    "give_small": (1,),
    "take_small": (1,),
    "give_stage": (2, 3, STAGES),
    "take_stage": (2, 3, STAGES),
    "give_back": (2, 3),
    "take_back": (2, 3),
    "store": (16,),
}


def kernel(z, names, *refs):
    features, cotangent, train_mask, degree, neighbours, send_rows = refs[:6]
    w_left, w_right, w_res, attn_vec, bn_gain, bn_shift = refs[6:12]
    out, grad_in, g_left, g_right, g_res, g_vec, g_gain, g_shift = refs[12:20]
    v = types.SimpleNamespace(**dict(zip(names, refs[20:])))
    grads_out = (g_left, g_right, g_res)
    R, D, K, T = z.rows, z.width, z.slots, z.table
    S, N, O = z.sections, z.partitions, z.outer
    half = D // 2
    total_rows = R * N
    sec = lax.axis_index("section")
    me = lax.axis_index("nodes")
    core = lax.rem(me, 2)
    outer = lax.div(me, 2)
    mate = me + 1 - 2 * core

    barrier = pltpu.get_barrier_semaphore()

    def greet(step, carry):
        pl.semaphore_signal(
            barrier, inc=1, device_id={"nodes": lax.rem(me + step, N)}, device_id_type=MESH
        )
        return carry

    lax.fori_loop(1, N, greet, 0)
    for step in range(1, S):
        pl.semaphore_signal(
            barrier, inc=1, device_id={"section": lax.rem(sec + step, S)}, device_id_type=MESH
        )

    loads = []
    for source, target in (
        (features.at[sec], v.features_in),
        (send_rows, v.listed_in),
        (w_left, v.weights_in.at[0]),
        (w_right, v.weights_in.at[1]),
        (w_res, v.weights_in.at[2]),
        (neighbours.at[sec], v.slots_in),
        (degree, v.degree_in),
        (train_mask, v.mask_in),
        (attn_vec, v.vector_in),
        (bn_gain, v.gain_in),
        (bn_shift, v.shift_in),
        (cotangent.at[sec], v.cotangent_in),
    ):
        copy = pltpu.make_async_copy(source, target, v.load.at[len(loads)])
        copy.start()
        loads.append(copy)

    def rows_loop(body, start):
        return lax.fori_loop(0, R // CHUNK, body, start, unroll=UNROLL)

    def chunk(i):
        return pl.ds(pl.multiple_of(i * CHUNK, CHUNK), CHUNK)

    def fold(values):
        return jnp.sum(values.reshape(values.shape[0] // TILE, TILE, values.shape[1]), axis=0)

    def add_rows(values):
        return jnp.sum(values, axis=0, keepdims=True)


    def start_exchange(which, one_tile=False):
        def send(step, carry):
            other = lax.rem(me + step, N)
            place = 0 if one_tile else pl.multiple_of(other * TILE, TILE)
            pltpu.make_async_remote_copy(
                src_ref=v.outgoing.at[which, pl.ds(place, TILE)],
                dst_ref=v.incoming.at[which, pl.ds(pl.multiple_of(me * TILE, TILE), TILE)],
                send_sem=v.give.at[which],
                recv_sem=v.take.at[which],
                device_id={"nodes": other},
                device_id_type=MESH,
            ).start()
            return carry

        lax.fori_loop(1, N, send, 0)
        own = pl.ds(pl.multiple_of(me * TILE, TILE), TILE)
        mine = pl.ds(0, TILE) if one_tile else own
        v.incoming[which, own, :] = v.outgoing[which, mine, :]

    def wait_bytes(ref, semaphore):
        pltpu.make_async_copy(ref, ref, semaphore).wait()

    def end_exchange(which):
        wait_bytes(v.incoming.at[which, pl.ds(0, (N - 1) * TILE)], v.take.at[which])

    def row_in_tile(rows):
        return lax.rem(iota((rows, D), 0), TILE)

    def with_sums(values, first, second):
        row = row_in_tile(values.shape[0])
        return values + jnp.where(row == z.send, first, 0.0) + jnp.where(row == z.send + 1, second, 0.0)

    def arrived_sums(which):
        tile = jnp.sum(v.incoming[which].reshape(N, TILE, D), axis=0)
        return tile[z.send : z.send + 1, :], tile[z.send + 1 : z.send + 2, :]

    def arrived_rows(which):
        values = v.incoming[which]
        return jnp.where(row_in_tile(z.halo) < z.send, values, 0.0)

    def give_rows_back(which):
        high, low = halves(arrived_rows(which))
        listed = v.list_t[:, : z.halo]
        return mm(listed, high) + mm(listed, low)

    def stage_copy(layer, first, stage, source, target, device):
        copy = pltpu.make_async_remote_copy(
            src_ref=source,
            dst_ref=target,
            send_sem=v.give_stage.at[layer, first, stage],
            recv_sem=v.take_stage.at[layer, first, stage],
            device_id=device,
            device_id_type=MESH,
        )
        copy.start()

    sends_to_end = []

    def stage_sent(layer, first, stage, ref):
        sends_to_end.append((ref, v.give_stage.at[layer, first, stage]))

    section_rows = pl.ds(pl.multiple_of(sec * z.share, TILE), z.share)

    def piece_rows(which):
        return pl.ds(pl.multiple_of(sec * z.share + which * z.piece, TILE), z.piece)

    def outer_device(which):
        return {"nodes": which * 2 + core}

    def start_stage(stage, layer, first, count):
        mats = pl.ds(first, count)
        if stage == CORE:
            stage_copy(
                layer,
                first,
                stage,
                v.sums.at[layer, mats, 1 - core],
                v.from_core.at[layer, mats],
                {"nodes": mate},
            )
            stage_sent(layer, first, stage, v.from_core.at[layer, mats])
        elif stage == SECTION:
            for step in range(1, S):
                other = lax.rem(sec + step, S)
                rows = pl.ds(pl.multiple_of(other * z.share, TILE), z.share)
                stage_copy(
                    layer,
                    first,
                    stage,
                    v.sums.at[layer, mats, core, rows],
                    v.from_section.at[layer, step - 1, mats],
                    {"section": other},
                )
            stage_sent(layer, first, stage, v.from_section.at[layer, :, mats])
        elif stage == OUTER:
            if z.owners == O:
                for step in range(1, O):
                    other = lax.rem(outer + step, O)
                    stage_copy(
                        layer,
                        first,
                        stage,
                        v.sums.at[layer, mats, core, piece_rows(other)],
                        v.from_outer.at[layer, step, mats],
                        outer_device(other),
                    )
                stage_sent(layer, first, stage, v.from_outer.at[layer, pl.ds(1, O - 1), mats])
            else:
                for other in range(z.owners):

                    @pl.when(outer != other)
                    def _():
                        stage_copy(
                            layer,
                            first,
                            stage,
                            v.sums.at[layer, mats, core, piece_rows(other)],
                            v.from_outer.at[layer, lax.rem(outer - other + O, O), mats],
                            outer_device(other),
                        )
                        wait_bytes(
                            v.from_outer.at[layer, 0, mats], v.give_stage.at[layer, first, stage]
                        )

        elif stage == OUTER_BACK:

            def send_all():
                for step in range(1, O):
                    stage_copy(
                        layer,
                        first,
                        stage,
                        v.whole.at[layer, mats, piece_rows(outer)],
                        v.whole.at[layer, mats, piece_rows(outer)],
                        outer_device(lax.rem(outer + step, O)),
                    )

            if z.owners == O:
                send_all()
                stage_sent(layer, first, stage, v.from_outer.at[layer, pl.ds(1, O - 1), mats])
            else:

                @pl.when(outer < z.owners)
                def _():
                    send_all()
                    wait_bytes(
                        v.from_outer.at[layer, pl.ds(1, O - 1), mats],
                        v.give_stage.at[layer, first, stage],
                    )

        elif stage == SECTION_BACK:
            for step in range(1, S):
                stage_copy(
                    layer,
                    first,
                    stage,
                    v.whole.at[layer, mats, section_rows],
                    v.whole.at[layer, mats, section_rows],
                    {"section": lax.rem(sec + step, S)},
                )
            stage_sent(layer, first, stage, v.from_section.at[layer, :, mats])
        elif stage == CORE_BACK:
            columns = pl.ds(pl.multiple_of(core * half, LANES), half)
            for mat in range(first, first + count):
                source = v.whole.at[layer, mat]
                target = grads_out[mat].at[layer, :, columns]
                pltpu.make_async_remote_copy(
                    src_ref=source,
                    dst_ref=target,
                    send_sem=v.give_back.at[layer, mat],
                    recv_sem=v.take_back.at[layer, mat],
                    device_id={"nodes": mate},
                    device_id_type=MESH,
                ).start()
                pltpu.make_async_copy(source, target, v.store.at[layer * 3 + mat]).start()

    def end_stage(stage, layer, first, count):
        mats = pl.ds(first, count)
        taken = v.take_stage.at[layer, first, stage]
        each = range(first, first + count)
        if stage == CORE:
            wait_bytes(v.from_core.at[layer, mats], taken)
            for mat in each:
                v.sums[layer, mat, core] = v.sums[layer, mat, core] + v.from_core[layer, mat]
        elif stage == SECTION:
            wait_bytes(v.from_section.at[layer, :, mats], taken)
            for mat in each:
                value = v.sums[layer, mat, core, section_rows, :]
                for step in range(S - 1):
                    value = value + v.from_section[layer, step, mat]
                v.sums[layer, mat, core, section_rows, :] = value
        elif stage == OUTER:

            def add():
                wait_bytes(v.from_outer.at[layer, pl.ds(1, O - 1), mats], taken)
                for mat in each:
                    value = v.sums[layer, mat, core, piece_rows(outer), :]
                    for step in range(1, O):
                        value = value + v.from_outer[layer, step, mat]
                    v.whole[layer, mat, piece_rows(outer), :] = value

            if z.owners == O:
                add()
            else:
                pl.when(outer < z.owners)(add)
        elif stage == OUTER_BACK:
            if z.owners == O:
                wait_bytes(v.from_outer.at[layer, pl.ds(1, O - 1), mats], taken)
            else:
                wait_bytes(v.from_outer.at[layer, pl.ds(1, z.owners - 1), mats], taken)

                @pl.when(outer >= z.owners)
                def _():
                    wait_bytes(v.from_outer.at[layer, 0, mats], taken)

        elif stage == SECTION_BACK:
            wait_bytes(v.from_section.at[layer, :, mats], taken)
        elif stage == CORE_BACK:
            columns = pl.ds(pl.multiple_of(core * half, LANES), half)
            for mat in each:
                source = v.whole.at[layer, mat]
                target = grads_out[mat].at[layer, :, columns]
                wait_bytes(source, v.give_back.at[layer, mat])
                wait_bytes(source, v.take_back.at[layer, mat])
                pltpu.make_async_copy(source, target, v.store.at[layer * 3 + mat]).wait()


    loads[1].wait()
    v.listed_row[...] = jnp.zeros_like(v.listed_row)
    v.listed_row[0:1, : z.listed] = v.listed_in[pl.ds(sec, 1), :].astype(F32)
    spread_from = iota((v.listed_row.shape[1], z.halo_pad), 0)
    spread_to = iota((v.listed_row.shape[1], z.halo_pad), 1)
    spread = as_ones(
        (lax.div(spread_from, z.send) == lax.div(spread_to, TILE))
        & (lax.rem(spread_from, z.send) == lax.rem(spread_to, TILE))
        & (spread_from < z.listed)
    )
    listed = mm(v.listed_row[...].astype(BF16), spread)[0:1, :]
    place = iota((1, z.halo_pad), 1)
    real = (lax.rem(place, TILE) < z.send) & (place < z.halo)
    listed = jnp.where(real, listed, -1.0)
    list_t = jnp.where(iota((R, z.halo_pad), 0).astype(F32) == listed, 1.0, 0.0)
    v.list_t[...] = list_t.astype(BF16)
    v.list[...] = list_t.T[: z.halo, :].astype(BF16)

    loads[0].wait()
    own = v.features_in[...]
    v.h[pl.ds(0, R), :] = own
    high, low = halves(own)
    v.h_hi[pl.ds(0, R), :] = high
    v.h_lo[pl.ds(0, R), :] = low
    v.outgoing[FEATURES] = mm(v.list[...], high) + mm(v.list[...], low)
    pl.semaphore_wait(barrier, N - 1 + S - 1)
    start_exchange(FEATURES)

    for load in loads[2:5]:
        load.wait()
    for layer in range(2):
        for mat in range(3):
            high, low = halves(v.weights_in[mat, layer])
            v.weights_hi[layer, mat] = high
            v.weights_lo[layer, mat] = low

    def weight(layer, mat):
        return v.weights_hi[layer, mat], v.weights_lo[layer, mat]

    for load in loads[5:11]:
        load.wait()
    named = v.slots_in[...]
    offset = named - R
    remote = R + lax.div(offset, z.send) * TILE + lax.rem(offset, z.send)
    named = jnp.where(named < R, named, remote).astype(F32)
    v.prep[...] = jnp.zeros_like(v.prep)
    v.prep[pl.ds(0, K), :] = named
    v.prep[pl.ds(K, 1), :] = v.degree_in[pl.ds(sec, 1), :].astype(F32)
    v.prep[pl.ds(K + 1, 1), :] = v.mask_in[pl.ds(sec, 1), :].astype(F32)
    v.prep_t[...] = v.prep[...].T
    for slot in range(1, K):
        column = v.prep_t[:, slot : slot + 1]
        v.pick[slot - 1] = as_ones(iota((R, T), 1).astype(F32) == column)
        row = v.prep[slot : slot + 1, :]
        v.pick_t[:, (slot - 1) * R : slot * R] = as_ones(iota((z.picked, R), 0).astype(F32) == row)
    group = D // HEADS
    block_row = lax.div(lax.rem(iota((2 * D, D), 0), D), group)
    v.ones[...] = as_ones(block_row == lax.div(iota((2 * D, D), 1), group))

    def project(layer):
        rows = pl.ds(0, R)
        own = (v.h_hi[rows, :], v.h_lo[rows, :])
        left = mm3(own, weight(layer, 0))
        v.taken[layer, 0] = left
        high, low = halves(left)
        v.table_hi[rows, :] = high
        v.table_lo[rows, :] = low
        v.right[layer] = mm3(own, weight(layer, 1))
        v.skip[...] = mm3(own, weight(layer, 2))

    def project_halo(layer):
        rows = pl.ds(R, z.halo_pad)
        left = mm3((v.h_hi[rows, :], v.h_lo[rows, :]), weight(layer, 0))
        high, low = halves(left)
        v.table_hi[rows, :] = high
        v.table_lo[rows, :] = low

    def store_halo(values):
        if z.halo < z.halo_pad:
            rest = pl.ds(R + z.halo, z.halo_pad - z.halo)
            v.h[rest, :] = jnp.zeros((z.halo_pad - z.halo, D), F32)
            v.h_hi[rest, :] = jnp.zeros((z.halo_pad - z.halo, D), BF16)
            v.h_lo[rest, :] = jnp.zeros((z.halo_pad - z.halo, D), BF16)
        rows = pl.ds(R, z.halo)
        v.h[rows, :] = values
        high, low = halves(values)
        v.h_hi[rows, :] = high
        v.h_lo[rows, :] = low

    def keep_transposed(layer):
        high, low = halves(v.h[...].T)
        v.ht_hi[layer] = high
        v.ht_lo[layer] = low

    def head_sums():
        def one(slot, carry):
            v.score[slot] = mm(v.pair[slot], v.ones[...])
            return carry

        lax.fori_loop(0, K, one, 0, unroll=True)

    def store_pair(slot, rows, values):
        high, low = halves(values)
        v.pair[slot, rows, pl.ds(0, D)] = high
        v.pair[slot, rows, pl.ds(D, D)] = low

    def attend(layer):
        def gather(slot, carry):
            pick = v.pick[slot - 1]
            v.taken[layer, slot] = mm(pick, v.table_hi[...]) + mm(pick, v.table_lo[...])
            return carry

        lax.fori_loop(1, K, gather, 0, unroll=True)
        vector = v.vector_in[layer : layer + 1, :]

        def activate(i, carry):
            rows = chunk(i)
            right = v.right[layer, rows, :]
            for slot in range(K):
                u = v.taken[layer, slot, rows, :] + right
                sig = 1.0 / (1.0 + jnp.exp(-u))
                v.sig[layer, slot, rows, :] = sig
                store_pair(slot, rows, u * sig * vector)
            return carry

        rows_loop(activate, 0)
        head_sums()

        def mix(i, carry):
            rows = chunk(i)
            count = jnp.broadcast_to(v.prep_t[rows, K : K + 1], (CHUNK, D))
            scores = [
                jnp.where(count > slot, v.score[slot, rows, :], MASKED_SCORE) for slot in range(K)
            ]
            highest = functools.reduce(jnp.maximum, scores)
            powers = [jnp.exp(score - highest) for score in scores]
            scale = 1.0 / functools.reduce(jnp.add, powers)
            joined = jnp.zeros((CHUNK, D), F32)
            for slot in range(K):
                alpha = powers[slot] * scale
                v.alpha[layer, slot, rows, :] = alpha
                joined = joined + alpha * v.taken[layer, slot, rows, :]
            v.joined[layer, rows, :] = joined
            mixed = joined + v.skip[rows, :]
            v.mixed[rows, :] = mixed
            return carry[0] + fold(mixed), carry[1] + fold(mixed * mixed)

        nothing = jnp.zeros((TILE, D), F32)
        first, second = rows_loop(mix, (nothing, nothing))
        return add_rows(first), add_rows(second)

    def moments(which):
        first, second = arrived_sums(which)
        mean = first / total_rows
        return mean, lax.rsqrt(second / total_rows - mean * mean + VARIANCE_EPS)

    def activation(layer, mixed, mean, inverse):
        normed = (mixed - mean) * inverse
        pre = v.gain_in[layer : layer + 1, :] * normed + v.shift_in[layer : layer + 1, :]
        power = jnp.exp(jnp.minimum(pre, 0.0))
        return normed, jnp.where(pre > 0, 1.0, power), jnp.where(pre > 0, pre, power - 1.0)

    def sums_tile(which, first, second):
        v.outgoing[which, pl.ds(0, TILE), :] = with_sums(jnp.zeros((TILE, D), F32), first, second)

    def list_rows(values):
        high, low = halves(values)
        return mm(v.list[...], high) + mm(v.list[...], low)

    project(0)
    end_exchange(FEATURES)
    store_halo(arrived_rows(FEATURES))
    project_halo(0)
    first, second = attend(0)
    v.outgoing[MIXED] = with_sums(list_rows(v.mixed[...]), first, second)
    start_exchange(MIXED)
    keep_transposed(0)
    end_exchange(MIXED)
    mean0, inverse0 = moments(MIXED)

    def finish0(i, carry):
        rows = chunk(i)
        normed, slope, hidden = activation(0, v.mixed[rows, :], mean0, inverse0)
        v.normed[0, rows, :] = normed
        v.slope[0, rows, :] = slope
        v.h[rows, :] = hidden
        high, low = halves(hidden)
        v.h_hi[rows, :] = high
        v.h_lo[rows, :] = low
        return carry

    rows_loop(finish0, 0)
    normed, slope, hidden = activation(0, arrived_rows(MIXED), mean0, inverse0)
    v.halo_normed[...] = normed
    v.halo_slope[...] = slope
    store_halo(jnp.where(row_in_tile(z.halo) < z.send, hidden, 0.0))

    project(1)
    project_halo(1)
    first, second = attend(1)
    sums_tile(SUMS, first, second)
    start_exchange(SUMS, True)
    keep_transposed(1)
    loads[11].wait()
    end_exchange(SUMS)
    mean1, inverse1 = moments(SUMS)

    def finish1(i, carry):
        rows = chunk(i)
        normed, slope, hidden = activation(1, v.mixed[rows, :], mean1, inverse1)
        v.normed[1, rows, :] = normed
        v.out_rows[rows, :] = hidden
        dpre = v.cotangent_in[rows, :] * v.prep_t[rows, K + 1 : K + 2] * slope
        v.dpre[rows, :] = dpre
        return carry[0] + fold(dpre), carry[1] + fold(dpre * normed)

    nothing = jnp.zeros((TILE, D), F32)
    first, second = rows_loop(finish1, (nothing, nothing))
    shift1, gain1 = add_rows(first), add_rows(second)
    sums_tile(BACK_SUMS, shift1, gain1)
    start_exchange(BACK_SUMS, True)
    out_copy = pltpu.make_async_copy(v.out_rows, out.at[0], v.store.at[6])
    out_copy.start()

    def normalization_back(layer, which, inverse):
        first, second = arrived_sums(which)
        first = first / total_rows
        second = second / total_rows
        scale = inverse * v.gain_in[layer : layer + 1, :]

        def one(i, carry):
            rows = chunk(i)
            dmixed = scale * (v.dpre[rows, :] - first - v.normed[layer, rows, :] * second)
            v.dmixed[rows, :] = dmixed
            high, low = halves(dmixed)
            v.dm_hi[rows, :] = high
            v.dm_lo[rows, :] = low
            return carry

        rows_loop(one, 0)

    def attend_back(layer, between=()):
        vector = v.vector_in[layer : layer + 1, :]

        def differences(i, carry):
            rows = chunk(i)
            joined = v.joined[layer, rows, :]
            dmixed = v.dmixed[rows, :]
            for slot in range(K):
                store_pair(slot, rows, (v.taken[layer, slot, rows, :] - joined) * dmixed)
            return carry

        rows_loop(differences, 0)
        head_sums()
        for step in between[:1]:
            step()

        def one(i, carry):
            rows = chunk(i)
            right = v.right[layer, rows, :]
            dmixed = v.dmixed[rows, :]
            dright = jnp.zeros((CHUNK, D), F32)
            for slot in range(K):
                u = v.taken[layer, slot, rows, :] + right
                sig = v.sig[layer, slot, rows, :]
                alpha = v.alpha[layer, slot, rows, :]
                dscore = alpha * v.score[slot, rows, :]
                carry = carry + fold(dscore * u * sig)
                du = dscore * vector * sig * (1.0 + u * (1.0 - sig))
                dright = dright + du
                dleft = du + alpha * dmixed
                if slot == 0:
                    v.dleft_self[rows, :] = dleft
                else:
                    high, low = halves(dleft)
                    place = pl.ds(pl.multiple_of((slot - 1) * R + i * CHUNK, CHUNK), CHUNK)
                    v.dleft_hi[place, :] = high
                    v.dleft_lo[place, :] = low
            high, low = halves(dright)
            v.dr_hi[rows, :] = high
            v.dr_lo[rows, :] = low
            return carry

        vector_sum = rows_loop(one, jnp.zeros((TILE, D), F32))
        for step in between[1:]:
            step()

        def scattered(rows):
            pick = v.pick_t[rows, :]
            return mm(pick, v.dleft_hi[...]) + mm(pick, v.dleft_lo[...])

        def scatter():
            rows = pl.ds(0, R)
            high, low = halves(scattered(rows) + v.dleft_self[...])
            v.dl_hi[rows, :] = high
            v.dl_lo[rows, :] = low
            rows = pl.ds(R, z.halo)
            high, low = halves(scattered(rows))
            v.dl_hi[rows, :] = high
            v.dl_lo[rows, :] = low

        scatter()
        return add_rows(vector_sum)

    def dleft(rows):
        return v.dl_hi[rows, :], v.dl_lo[rows, :]

    def input_back(layer):
        own = pl.ds(0, R)
        v.dh[...] = (
            mm3(dleft(own), weight(layer, 0), mm_nt)
            + mm3((v.dr_hi[...], v.dr_lo[...]), weight(layer, 1), mm_nt)
            + mm3((v.dm_hi[...], v.dm_lo[...]), weight(layer, 2), mm_nt)
        )
        return mm3(dleft(pl.ds(R, z.halo)), weight(layer, 0), mm_nt)

    def weight_grad(layer, mat):
        if mat == 0:
            upstream = (v.dl_hi[...], v.dl_lo[...])
            inputs = (v.ht_hi[layer], v.ht_lo[layer])
        else:
            upstream = (v.dr_hi[...], v.dr_lo[...]) if mat == 1 else (v.dm_hi[...], v.dm_lo[...])
            inputs = (v.ht_hi[layer, :, pl.ds(0, R)], v.ht_lo[layer, :, pl.ds(0, R)])
        value = mm3(inputs, upstream)
        v.sums[layer, mat, 0] = value[:, :half]
        v.sums[layer, mat, 1] = value[:, half:]

    if z.halo < z.halo_pad:
        rest = pl.ds(R + z.halo, z.halo_pad - z.halo)
        v.dl_hi[rest, :] = jnp.zeros((z.halo_pad - z.halo, D), BF16)
        v.dl_lo[rest, :] = jnp.zeros((z.halo_pad - z.halo, D), BF16)

    end_exchange(BACK_SUMS)
    normalization_back(1, BACK_SUMS, inverse1)
    vector1 = attend_back(1)
    halo_back = input_back(1)
    dpre = v.dh[...] * v.slope[0]
    halo_dpre = halo_back * v.halo_slope[...]
    shift0 = add_rows(dpre) + add_rows(halo_dpre)
    gain0 = add_rows(dpre * v.normed[0]) + add_rows(halo_dpre * v.halo_normed[...])
    v.outgoing[BACK_ROWS] = with_sums(halo_back, shift0, gain0)
    start_exchange(BACK_ROWS)
    for mat in range(3):
        weight_grad(1, mat)
    start_stage(CORE, 1, 0, 3)
    end_exchange(BACK_ROWS)
    v.dpre[...] = (v.dh[...] + give_rows_back(BACK_ROWS)) * v.slope[0]

    normalization_back(0, BACK_ROWS, inverse0)
    end_stage(CORE, 1, 0, 3)
    start_stage(SECTION, 1, 0, 3)

    def step1():
        end_stage(SECTION, 1, 0, 3)
        start_stage(OUTER, 1, 0, 3)

    def step2():
        end_stage(OUTER, 1, 0, 3)
        start_stage(OUTER_BACK, 1, 0, 3)

    vector0 = attend_back(0, (step1, step2))
    for mat in range(3):
        weight_grad(0, mat)
    start_stage(CORE, 0, 0, 3)
    end_stage(OUTER_BACK, 1, 0, 3)
    start_stage(SECTION_BACK, 1, 0, 3)

    rows = (vector0, vector1, gain0, gain1, shift0, shift1)
    row = iota((TILE, D), 0)
    tile = jnp.zeros((TILE, D), F32)
    for place, value in enumerate(rows):
        tile = jnp.where(row == place, value, tile)
    v.outgoing[SMALL, pl.ds(0, TILE), :] = tile
    start_exchange(SMALL, True)

    halo_back = input_back(0)
    v.outgoing[INPUT_ROWS] = halo_back
    start_exchange(INPUT_ROWS)

    end_stage(CORE, 0, 0, 3)
    start_stage(SECTION, 0, 0, 3)
    end_exchange(SMALL)
    v.small[...] = jnp.sum(v.incoming[SMALL].reshape(N, TILE, D), axis=0)
    for step in range(1, S):
        pltpu.make_async_remote_copy(
            src_ref=v.small,
            dst_ref=v.small_in.at[step],
            send_sem=v.give_small.at[0],
            recv_sem=v.take_small.at[0],
            device_id={"section": lax.rem(sec + step, S)},
            device_id_type=MESH,
        ).start()
    end_stage(SECTION_BACK, 1, 0, 3)
    start_stage(CORE_BACK, 1, 0, 3)
    end_exchange(INPUT_ROWS)
    v.grad_rows[...] = v.dh[...] + give_rows_back(INPUT_ROWS)
    grad_copy = pltpu.make_async_copy(v.grad_rows, grad_in.at[0], v.store.at[7])
    grad_copy.start()
    end_stage(SECTION, 0, 0, 3)
    start_stage(OUTER, 0, 0, 3)
    wait_bytes(v.small_in.at[pl.ds(1, S - 1)], v.take_small.at[0])
    value = v.small[...]
    for step in range(1, S):
        value = value + v.small_in[step]
    last = []
    for place, (buffer, target) in enumerate(
        ((v.vector_out, g_vec), (v.gain_out, g_gain), (v.shift_out, g_shift))
    ):
        buffer[...] = value[2 * place : 2 * place + 2, :]
        copy = pltpu.make_async_copy(buffer, target, v.store.at[8 + place])
        copy.start()
        last.append(copy)
    end_stage(OUTER, 0, 0, 3)
    start_stage(OUTER_BACK, 0, 0, 3)
    end_stage(OUTER_BACK, 0, 0, 3)
    start_stage(SECTION_BACK, 0, 0, 3)
    end_stage(SECTION_BACK, 0, 0, 3)
    start_stage(CORE_BACK, 0, 0, 3)
    out_copy.wait()
    grad_copy.wait()
    for copy in last:
        copy.wait()
    for which in range(EXCHANGES):
        wait_bytes(v.outgoing.at[which, pl.ds(0, (N - 1) * TILE)], v.give.at[which])
    wait_bytes(v.small_in.at[pl.ds(1, S - 1)], v.give_small.at[0])
    for ref, semaphore in sends_to_end:
        wait_bytes(ref, semaphore)
    end_stage(CORE_BACK, 1, 0, 3)
    end_stage(CORE_BACK, 0, 0, 3)


def store_kernel(*refs):
    copies = [pltpu.make_async_copy(refs[i], refs[8 + i], refs[16].at[i]) for i in range(8)]
    for copy in copies:
        copy.start()
    for copy in copies:
        copy.wait()


def body(
    features,
    cotangent,
    train_mask,
    degree,
    neighbours,
    send_rows,
    w_left,
    w_right,
    w_res,
    attn_vec,
    bn_gain,
    bn_shift,
):
    batches, rows, width = features.shape
    sections = lax.axis_size("section")
    assert batches == sections
    z = sizes_of(
        sections, lax.axis_size("nodes"), rows, width, neighbours.shape[2], send_rows.shape[1]
    )
    shapes = scratch_of(z)
    shapes["mask_in"] = (train_mask.shape, jnp.int32)
    shapes["degree_in"] = (degree.shape, jnp.int32)
    shapes["listed_in"] = (send_rows.shape, jnp.int32)
    scratch = [pltpu.VMEM(shape, dtype) for shape, dtype in shapes.values()]
    scratch += [pltpu.SemaphoreType.DMA(shape) for shape in SEMAPHORES.values()]
    names = list(shapes) + list(SEMAPHORES)
    anywhere = pl.BlockSpec(memory_space=pl.ANY)
    square = jax.ShapeDtypeStruct((2, width, width), F32)
    columns = jax.ShapeDtypeStruct((2, width), F32)
    block = jax.ShapeDtypeStruct((1, rows, width), F32)
    results = (block, block, square, square, square, columns, columns, columns)
    in_vmem = pl.BlockSpec(memory_space=pltpu.VMEM)
    found = pl.pallas_call(
        functools.partial(kernel, z, names),
        out_shape=tuple(pltpu.VMEM(x.shape, x.dtype) for x in results),
        in_specs=[pl.BlockSpec(memory_space=pltpu.HBM)] * 12,
        out_specs=(in_vmem,) * 8,
        scratch_shapes=scratch,
        compiler_params=pltpu.CompilerParams(
            collective_id=0, has_side_effects=True, vmem_limit_bytes=60 * 1024 * 1024
        ),
    )(
        features,
        cotangent,
        train_mask,
        degree,
        jnp.transpose(neighbours, (0, 2, 1)),
        send_rows,
        w_left,
        w_right,
        w_res,
        attn_vec,
        bn_gain,
        bn_shift,
    )
    return pl.pallas_call(
        store_kernel,
        out_shape=results,
        in_specs=[anywhere] * 8,
        out_specs=(anywhere,) * 8,
        scratch_shapes=[pltpu.SemaphoreType.DMA((8,))],
        compiler_params=pltpu.CompilerParams(vmem_limit_bytes=1024 * 1024),
    )(*found)


def solution(mesh):
    return jax.shard_map(
        body,
        mesh=mesh,
        in_specs=(
            P(None, "nodes", None),
            P(None, "nodes", None),
            P(None, "nodes"),
            P(None, "nodes"),
            P(None, "nodes", None),
            P(None, "nodes"),
            P(),
            P(),
            P(),
            P(),
            P(),
            P(),
        ),
        out_specs=(
            P("section", "nodes", None),
            P("section", "nodes", None),
            P(),
            P(),
            P(),
            P(),
            P(),
            P(),
        ),
        check_vma=False,
    )
```

```python
import functools
import types

import jax
import jax.numpy as jnp
from jax import lax
from jax.experimental import pallas as pl
from jax.experimental.pallas import tpu as pltpu
from jax.sharding import PartitionSpec as P

HEADS = 4
MASKED_SCORE = -1e30
VARIANCE_EPS = 1e-05
F32 = jnp.float32
BF16 = jnp.bfloat16
MESH = pl.DeviceIdType.MESH
UNROLL = 4
LANES = 128
TILE = 8
CHUNK = 16

FEATURES, MIXED, SUMS, BACK_SUMS, BACK_ROWS, INPUT_ROWS, SMALL = range(7)
EXCHANGES = 7
CORE, SECTION, OUTER, OUTER_BACK, SECTION_BACK, CORE_BACK = range(6)
STAGES = 6


def halves(values):
    high = values.astype(BF16)
    return high, (values - high.astype(F32)).astype(BF16)


def mm(lhs, rhs):
    return jnp.dot(lhs, rhs, preferred_element_type=F32)


def mm_nt(lhs, rhs):
    return lax.dot_general(lhs, rhs, (((1,), (1,)), ((), ())), preferred_element_type=F32)


def mm3(lhs, rhs, product=mm):
    return product(lhs[0], rhs[0]) + product(lhs[1], rhs[0]) + product(lhs[0], rhs[1])


def iota(shape, dim):
    return lax.broadcasted_iota(jnp.int32, shape, dim)


def as_ones(condition):
    return jnp.where(condition, 1.0, 0.0).astype(BF16)


def sizes_of(sections, partitions, rows, width, slots, listed):
    z = types.SimpleNamespace()
    z.sections, z.partitions, z.outer = sections, partitions, partitions // 2
    z.rows, z.width, z.slots, z.listed = rows, width, slots, listed
    z.send = listed // partitions
    z.halo = partitions * TILE
    z.halo_pad = -(-z.halo // LANES) * LANES
    z.table = rows + z.halo_pad
    z.picked = rows + z.halo
    z.share = rows // sections
    z.piece = max(TILE, z.share // z.outer)
    z.owners = z.share // z.piece
    return z


def scratch_of(z):
    R, D, K, T = z.rows, z.width, z.slots, z.table
    S, O = z.sections, z.outer
    vmem = {
        "features_in": ((R, D), F32),
        "cotangent_in": ((R, D), F32),
        "mask_in": (None, jnp.int32),
        "degree_in": (None, jnp.int32),
        "slots_in": ((K, R), jnp.int32),
        "listed_in": (None, jnp.int32),
        "weights_in": ((3, 2, D, D), F32),
        "vector_in": ((2, D), F32),
        "gain_in": ((2, D), F32),
        "shift_in": ((2, D), F32),
        "weights_hi": ((2, 3, D, D), BF16),
        "weights_lo": ((2, 3, D, D), BF16),
        "prep": ((LANES, R), F32),
        "prep_t": ((R, LANES), F32),
        "listed_row": ((TILE, max(LANES, z.listed)), F32),
        "pick": ((K - 1, R, T), BF16),
        "pick_t": ((z.picked, (K - 1) * R), BF16),
        "list": ((z.halo, R), BF16),
        "list_t": ((R, z.halo_pad), BF16),
        "ones": ((2 * D, D), BF16),
        "h": ((T, D), F32),
        "h_hi": ((T, D), BF16),
        "h_lo": ((T, D), BF16),
        "ht_hi": ((2, D, T), BF16),
        "ht_lo": ((2, D, T), BF16),
        "table_hi": ((T, D), BF16),
        "table_lo": ((T, D), BF16),
        "taken": ((2, K, R, D), F32),
        "sig": ((2, K, R, D), F32),
        "alpha": ((2, K, R, D), F32),
        "joined": ((2, R, D), F32),
        "right": ((2, R, D), F32),
        "skip": ((R, D), F32),
        "mixed": ((R, D), F32),
        "normed": ((2, R, D), F32),
        "slope": ((2, R, D), F32),
        "halo_normed": ((z.halo, D), F32),
        "halo_slope": ((z.halo, D), F32),
        "pair": ((K, R, 2 * D), BF16),
        "score": ((K, R, D), F32),
        "dpre": ((R, D), F32),
        "dmixed": ((R, D), F32),
        "dm_hi": ((R, D), BF16),
        "dm_lo": ((R, D), BF16),
        "dr_hi": ((R, D), BF16),
        "dr_lo": ((R, D), BF16),
        "dl_hi": ((T, D), BF16),
        "dl_lo": ((T, D), BF16),
        "dleft_self": ((R, D), F32),
        "dleft_hi": (((K - 1) * R, D), BF16),
        "dleft_lo": (((K - 1) * R, D), BF16),
        "dh": ((R, D), F32),
        "outgoing": ((EXCHANGES, z.halo, D), F32),
        "incoming": ((EXCHANGES, z.halo, D), F32),
        "small": ((TILE, D), F32),
        "small_in": ((S, TILE, D), F32),
        "sums": ((2, 3, R, D), F32),
        "from_core": ((2, 3, R, D), F32),
        "from_section": ((2, S - 1, 3, z.share, D), F32),
        "from_outer": ((2, O, 3, z.piece, D), F32),
    }
    return vmem


SEMAPHORES = {
    "load": (12,),
    "give": (EXCHANGES,),
    "take": (EXCHANGES,),
    "give_small": (1,),
    "take_small": (1,),
    "give_stage": (2, 3, STAGES),
    "take_stage": (2, 3, STAGES),
}


def kernel(z, names, *refs):
    features, cotangent, train_mask, degree, neighbours, send_rows = refs[:6]
    w_left, w_right, w_res, attn_vec, bn_gain, bn_shift = refs[6:12]
    out, grad_in, grads, g_vec, g_gain, g_shift = refs[12:18]
    v = types.SimpleNamespace(**dict(zip(names, refs[18:])))
    R, D, K, T = z.rows, z.width, z.slots, z.table
    S, N, O = z.sections, z.partitions, z.outer
    total_rows = R * N
    sec = lax.axis_index("section")
    me = lax.axis_index("nodes")
    core = lax.rem(me, 2)
    outer = lax.div(me, 2)
    mate = me + 1 - 2 * core

    barrier = pltpu.get_barrier_semaphore()

    def greet(step, carry):
        pl.semaphore_signal(
            barrier, inc=1, device_id={"nodes": lax.rem(me + step, N)}, device_id_type=MESH
        )
        return carry

    lax.fori_loop(1, N, greet, 0)
    for step in range(1, S):
        pl.semaphore_signal(
            barrier, inc=1, device_id={"section": lax.rem(sec + step, S)}, device_id_type=MESH
        )

    loads = []
    for source, target in (
        (features.at[sec], v.features_in),
        (send_rows, v.listed_in),
        (w_left, v.weights_in.at[0]),
        (w_right, v.weights_in.at[1]),
        (w_res, v.weights_in.at[2]),
        (neighbours.at[sec], v.slots_in),
        (degree, v.degree_in),
        (train_mask, v.mask_in),
        (attn_vec, v.vector_in),
        (bn_gain, v.gain_in),
        (bn_shift, v.shift_in),
        (cotangent.at[sec], v.cotangent_in),
    ):
        copy = pltpu.make_async_copy(source, target, v.load.at[len(loads)])
        copy.start()
        loads.append(copy)

    def rows_loop(body, start):
        return lax.fori_loop(0, R // CHUNK, body, start, unroll=UNROLL)

    def chunk(i):
        return pl.ds(pl.multiple_of(i * CHUNK, CHUNK), CHUNK)

    def fold(values):
        return jnp.sum(values.reshape(values.shape[0] // TILE, TILE, values.shape[1]), axis=0)

    def add_rows(values):
        return jnp.sum(values, axis=0, keepdims=True)


    def start_exchange(which, one_tile=False):
        def send(step, carry):
            other = lax.rem(me + step, N)
            place = 0 if one_tile else pl.multiple_of(other * TILE, TILE)
            pltpu.make_async_remote_copy(
                src_ref=v.outgoing.at[which, pl.ds(place, TILE)],
                dst_ref=v.incoming.at[which, pl.ds(pl.multiple_of(me * TILE, TILE), TILE)],
                send_sem=v.give.at[which],
                recv_sem=v.take.at[which],
                device_id={"nodes": other},
                device_id_type=MESH,
            ).start()
            return carry

        lax.fori_loop(1, N, send, 0)
        own = pl.ds(pl.multiple_of(me * TILE, TILE), TILE)
        mine = pl.ds(0, TILE) if one_tile else own
        v.incoming[which, own, :] = v.outgoing[which, mine, :]

    def wait_bytes(ref, semaphore):
        pltpu.make_async_copy(ref, ref, semaphore).wait()

    def end_exchange(which):
        wait_bytes(v.incoming.at[which, pl.ds(0, (N - 1) * TILE)], v.take.at[which])

    def row_in_tile(rows):
        return lax.rem(iota((rows, D), 0), TILE)

    def with_sums(values, first, second):
        row = row_in_tile(values.shape[0])
        return values + jnp.where(row == z.send, first, 0.0) + jnp.where(row == z.send + 1, second, 0.0)

    def arrived_sums(which):
        tile = jnp.sum(v.incoming[which].reshape(N, TILE, D), axis=0)
        return tile[z.send : z.send + 1, :], tile[z.send + 1 : z.send + 2, :]

    def arrived_rows(which):
        values = v.incoming[which]
        return jnp.where(row_in_tile(z.halo) < z.send, values, 0.0)

    def give_rows_back(which):
        high, low = halves(arrived_rows(which))
        listed = v.list_t[:, : z.halo]
        return mm(listed, high) + mm(listed, low)

    sends_to_end = []

    def on(which, body):
        pl.when(core == which)(body)

    def stage_copy(layer, first, stage, source, target, device):
        pltpu.make_async_remote_copy(
            src_ref=source,
            dst_ref=target,
            send_sem=v.give_stage.at[layer, first, stage],
            recv_sem=v.take_stage.at[layer, first, stage],
            device_id=device,
            device_id_type=MESH,
        ).start()

    def stage_sent(layer, first, stage, ref, which):
        sends_to_end.append((ref, lambda: v.give_stage.at[layer, first, stage], which))

    def share_rows(which):
        return pl.ds(pl.multiple_of(which * z.share, TILE), z.share)

    def piece_rows(which):
        return pl.ds(pl.multiple_of(sec * z.share + which * z.piece, TILE), z.piece)

    def outer_device(which):
        return {"nodes": which * 2 + core}

    def from_others(layer, mats, count):
        return v.from_outer.at[layer, pl.ds(1, count), mats]

    def start_core(layer, mat):
        on(
            0,
            lambda: stage_copy(
                layer, mat, CORE, v.sums.at[layer, mat], v.from_core.at[layer, mat], {"nodes": mate}
            ),
        )
        stage_sent(layer, mat, CORE, lambda: v.from_core.at[layer, mat], 0)

    def start_stage(stage, layer, first, count):
        mats = pl.ds(first, count)
        if stage == SECTION:
            for step in range(1, S):
                other = lax.rem(sec + step, S)
                stage_copy(
                    layer,
                    first,
                    stage,
                    v.sums.at[layer, mats, share_rows(other)],
                    v.from_section.at[layer, step - 1, mats],
                    {"section": other},
                )
            stage_sent(layer, first, stage, lambda: v.from_section.at[layer, :, mats], 1)
        elif stage == OUTER:
            if z.owners == O:
                for step in range(1, O):
                    other = lax.rem(outer + step, O)
                    stage_copy(
                        layer,
                        first,
                        stage,
                        v.sums.at[layer, mats, piece_rows(other)],
                        v.from_outer.at[layer, step, mats],
                        outer_device(other),
                    )
                stage_sent(layer, first, stage, lambda: from_others(layer, mats, O - 1), 1)
            else:
                for other in range(z.owners):

                    @pl.when(outer != other)
                    def _():
                        stage_copy(
                            layer,
                            first,
                            stage,
                            v.sums.at[layer, mats, piece_rows(other)],
                            v.from_outer.at[layer, lax.rem(outer - other + O, O), mats],
                            outer_device(other),
                        )
                        wait_bytes(
                            v.from_outer.at[layer, 0, mats], v.give_stage.at[layer, first, stage]
                        )

        elif stage == OUTER_BACK:

            def send_all():
                for step in range(1, O):
                    stage_copy(
                        layer,
                        first,
                        stage,
                        grads.at[layer, mats, piece_rows(outer)],
                        grads.at[layer, mats, piece_rows(outer)],
                        outer_device(lax.rem(outer + step, O)),
                    )

            if z.owners == O:
                send_all()
                stage_sent(layer, first, stage, lambda: from_others(layer, mats, O - 1), 1)
            else:

                @pl.when(outer < z.owners)
                def _():
                    send_all()
                    wait_bytes(
                        from_others(layer, mats, O - 1), v.give_stage.at[layer, first, stage]
                    )

        elif stage == SECTION_BACK:
            for step in range(1, S):
                stage_copy(
                    layer,
                    first,
                    stage,
                    grads.at[layer, mats, share_rows(sec)],
                    grads.at[layer, mats, share_rows(sec)],
                    {"section": lax.rem(sec + step, S)},
                )
            stage_sent(layer, first, stage, lambda: v.from_section.at[layer, :, mats], 1)
        elif stage == CORE_BACK:
            stage_copy(
                layer, first, stage, grads.at[layer, mats], grads.at[layer, mats], {"nodes": mate}
            )
            stage_sent(layer, first, stage, lambda: grads.at[layer, mats], 1)

    def end_stage(stage, layer, first, count):
        mats = pl.ds(first, count)
        taken = v.take_stage.at[layer, first, stage]
        each = range(first, first + count)
        if stage == CORE:
            wait_bytes(v.from_core.at[layer, first], taken)
            v.sums[layer, first] = v.sums[layer, first] + v.from_core[layer, first]
        elif stage == SECTION:
            wait_bytes(v.from_section.at[layer, :, mats], taken)
            for mat in each:
                value = v.sums[layer, mat, share_rows(sec), :]
                for step in range(S - 1):
                    value = value + v.from_section[layer, step, mat]
                v.sums[layer, mat, share_rows(sec), :] = value
        elif stage == OUTER:

            def add():
                wait_bytes(from_others(layer, mats, O - 1), taken)
                for mat in each:
                    value = v.sums[layer, mat, piece_rows(outer), :]
                    for step in range(1, O):
                        value = value + v.from_outer[layer, step, mat]
                    grads[layer, mat, piece_rows(outer), :] = value

            if z.owners == O:
                add()
            else:
                pl.when(outer < z.owners)(add)
        elif stage == OUTER_BACK:
            if z.owners == O:
                wait_bytes(from_others(layer, mats, O - 1), taken)
            else:
                wait_bytes(from_others(layer, mats, z.owners - 1), taken)

                @pl.when(outer >= z.owners)
                def _():
                    wait_bytes(v.from_outer.at[layer, 0, mats], taken)

        elif stage == SECTION_BACK:
            wait_bytes(v.from_section.at[layer, :, mats], taken)
        elif stage == CORE_BACK:
            wait_bytes(grads.at[layer, mats], taken)

    def advance(*moves):
        def run():
            for stage, layer, first, count in moves:
                if stage == CORE:
                    for mat in range(first, first + count):
                        end_stage(CORE, layer, mat, 1)
                else:
                    end_stage(stage, layer, first, count)
                start_stage(stage + 1, layer, first, count)

        on(1, run)


    loads[1].wait()
    v.listed_row[...] = jnp.zeros_like(v.listed_row)
    v.listed_row[0:1, : z.listed] = v.listed_in[pl.ds(sec, 1), :].astype(F32)
    spread_from = iota((v.listed_row.shape[1], z.halo_pad), 0)
    spread_to = iota((v.listed_row.shape[1], z.halo_pad), 1)
    spread = as_ones(
        (lax.div(spread_from, z.send) == lax.div(spread_to, TILE))
        & (lax.rem(spread_from, z.send) == lax.rem(spread_to, TILE))
        & (spread_from < z.listed)
    )
    listed = mm(v.listed_row[...].astype(BF16), spread)[0:1, :]
    place = iota((1, z.halo_pad), 1)
    real = (lax.rem(place, TILE) < z.send) & (place < z.halo)
    listed = jnp.where(real, listed, -1.0)
    list_t = jnp.where(iota((R, z.halo_pad), 0).astype(F32) == listed, 1.0, 0.0)
    v.list_t[...] = list_t.astype(BF16)
    v.list[...] = list_t.T[: z.halo, :].astype(BF16)

    loads[0].wait()
    own = v.features_in[...]
    v.h[pl.ds(0, R), :] = own
    high, low = halves(own)
    v.h_hi[pl.ds(0, R), :] = high
    v.h_lo[pl.ds(0, R), :] = low
    v.outgoing[FEATURES] = mm(v.list[...], high) + mm(v.list[...], low)
    pl.semaphore_wait(barrier, N - 1 + S - 1)
    start_exchange(FEATURES)

    for load in loads[2:5]:
        load.wait()
    for layer in range(2):
        for mat in range(3):
            high, low = halves(v.weights_in[mat, layer])
            v.weights_hi[layer, mat] = high
            v.weights_lo[layer, mat] = low

    def weight(layer, mat):
        return v.weights_hi[layer, mat], v.weights_lo[layer, mat]

    for load in loads[5:11]:
        load.wait()
    named = v.slots_in[...]
    offset = named - R
    remote = R + lax.div(offset, z.send) * TILE + lax.rem(offset, z.send)
    named = jnp.where(named < R, named, remote).astype(F32)
    v.prep[...] = jnp.zeros_like(v.prep)
    v.prep[pl.ds(0, K), :] = named
    v.prep[pl.ds(K, 1), :] = v.degree_in[pl.ds(sec, 1), :].astype(F32)
    v.prep[pl.ds(K + 1, 1), :] = v.mask_in[pl.ds(sec, 1), :].astype(F32)
    v.prep_t[...] = v.prep[...].T
    for slot in range(1, K):
        column = v.prep_t[:, slot : slot + 1]
        v.pick[slot - 1] = as_ones(iota((R, T), 1).astype(F32) == column)
        row = v.prep[slot : slot + 1, :]
        v.pick_t[:, (slot - 1) * R : slot * R] = as_ones(iota((z.picked, R), 0).astype(F32) == row)
    group = D // HEADS
    block_row = lax.div(lax.rem(iota((2 * D, D), 0), D), group)
    v.ones[...] = as_ones(block_row == lax.div(iota((2 * D, D), 1), group))

    def project(layer):
        rows = pl.ds(0, R)
        own = (v.h_hi[rows, :], v.h_lo[rows, :])
        left = mm3(own, weight(layer, 0))
        v.taken[layer, 0] = left
        high, low = halves(left)
        v.table_hi[rows, :] = high
        v.table_lo[rows, :] = low
        v.right[layer] = mm3(own, weight(layer, 1))
        v.skip[...] = mm3(own, weight(layer, 2))

    def project_halo(layer):
        rows = pl.ds(R, z.halo_pad)
        left = mm3((v.h_hi[rows, :], v.h_lo[rows, :]), weight(layer, 0))
        high, low = halves(left)
        v.table_hi[rows, :] = high
        v.table_lo[rows, :] = low

    def store_halo(values):
        if z.halo < z.halo_pad:
            rest = pl.ds(R + z.halo, z.halo_pad - z.halo)
            v.h[rest, :] = jnp.zeros((z.halo_pad - z.halo, D), F32)
            v.h_hi[rest, :] = jnp.zeros((z.halo_pad - z.halo, D), BF16)
            v.h_lo[rest, :] = jnp.zeros((z.halo_pad - z.halo, D), BF16)
        rows = pl.ds(R, z.halo)
        v.h[rows, :] = values
        high, low = halves(values)
        v.h_hi[rows, :] = high
        v.h_lo[rows, :] = low

    def keep_transposed(layer):
        high, low = halves(v.h[...].T)
        v.ht_hi[layer] = high
        v.ht_lo[layer] = low

    def head_sums():
        def one(slot, carry):
            v.score[slot] = mm(v.pair[slot], v.ones[...])
            return carry

        lax.fori_loop(0, K, one, 0, unroll=True)

    def store_pair(slot, rows, values):
        high, low = halves(values)
        v.pair[slot, rows, pl.ds(0, D)] = high
        v.pair[slot, rows, pl.ds(D, D)] = low

    def attend(layer):
        def gather(slot, carry):
            pick = v.pick[slot - 1]
            v.taken[layer, slot] = mm(pick, v.table_hi[...]) + mm(pick, v.table_lo[...])
            return carry

        lax.fori_loop(1, K, gather, 0, unroll=True)
        vector = v.vector_in[layer : layer + 1, :]

        def activate(i, carry):
            rows = chunk(i)
            right = v.right[layer, rows, :]
            for slot in range(K):
                u = v.taken[layer, slot, rows, :] + right
                sig = 1.0 / (1.0 + jnp.exp(-u))
                v.sig[layer, slot, rows, :] = sig
                store_pair(slot, rows, u * sig * vector)
            return carry

        rows_loop(activate, 0)
        head_sums()

        def mix(i, carry):
            rows = chunk(i)
            count = jnp.broadcast_to(v.prep_t[rows, K : K + 1], (CHUNK, D))
            scores = [
                jnp.where(count > slot, v.score[slot, rows, :], MASKED_SCORE) for slot in range(K)
            ]
            highest = functools.reduce(jnp.maximum, scores)
            powers = [jnp.exp(score - highest) for score in scores]
            scale = 1.0 / functools.reduce(jnp.add, powers)
            joined = jnp.zeros((CHUNK, D), F32)
            for slot in range(K):
                alpha = powers[slot] * scale
                v.alpha[layer, slot, rows, :] = alpha
                joined = joined + alpha * v.taken[layer, slot, rows, :]
            v.joined[layer, rows, :] = joined
            mixed = joined + v.skip[rows, :]
            v.mixed[rows, :] = mixed
            return carry[0] + fold(mixed), carry[1] + fold(mixed * mixed)

        nothing = jnp.zeros((TILE, D), F32)
        first, second = rows_loop(mix, (nothing, nothing))
        return add_rows(first), add_rows(second)

    def moments(which):
        first, second = arrived_sums(which)
        mean = first / total_rows
        return mean, lax.rsqrt(second / total_rows - mean * mean + VARIANCE_EPS)

    def activation(layer, mixed, mean, inverse):
        normed = (mixed - mean) * inverse
        pre = v.gain_in[layer : layer + 1, :] * normed + v.shift_in[layer : layer + 1, :]
        power = jnp.exp(jnp.minimum(pre, 0.0))
        return normed, jnp.where(pre > 0, 1.0, power), jnp.where(pre > 0, pre, power - 1.0)

    def sums_tile(which, first, second):
        v.outgoing[which, pl.ds(0, TILE), :] = with_sums(jnp.zeros((TILE, D), F32), first, second)

    def list_rows(values):
        high, low = halves(values)
        return mm(v.list[...], high) + mm(v.list[...], low)

    project(0)
    end_exchange(FEATURES)
    store_halo(arrived_rows(FEATURES))
    project_halo(0)
    first, second = attend(0)
    v.outgoing[MIXED] = with_sums(list_rows(v.mixed[...]), first, second)
    start_exchange(MIXED)
    keep_transposed(0)
    end_exchange(MIXED)
    mean0, inverse0 = moments(MIXED)

    def finish0(i, carry):
        rows = chunk(i)
        normed, slope, hidden = activation(0, v.mixed[rows, :], mean0, inverse0)
        v.normed[0, rows, :] = normed
        v.slope[0, rows, :] = slope
        v.h[rows, :] = hidden
        high, low = halves(hidden)
        v.h_hi[rows, :] = high
        v.h_lo[rows, :] = low
        return carry

    rows_loop(finish0, 0)
    normed, slope, hidden = activation(0, arrived_rows(MIXED), mean0, inverse0)
    v.halo_normed[...] = normed
    v.halo_slope[...] = slope
    store_halo(jnp.where(row_in_tile(z.halo) < z.send, hidden, 0.0))

    project(1)
    project_halo(1)
    first, second = attend(1)
    sums_tile(SUMS, first, second)
    start_exchange(SUMS, True)
    keep_transposed(1)
    loads[11].wait()
    end_exchange(SUMS)
    mean1, inverse1 = moments(SUMS)

    def finish1(i, carry):
        rows = chunk(i)
        normed, slope, hidden = activation(1, v.mixed[rows, :], mean1, inverse1)
        v.normed[1, rows, :] = normed
        out[0, rows, :] = hidden
        dpre = v.cotangent_in[rows, :] * v.prep_t[rows, K + 1 : K + 2] * slope
        v.dpre[rows, :] = dpre
        return carry[0] + fold(dpre), carry[1] + fold(dpre * normed)

    nothing = jnp.zeros((TILE, D), F32)
    first, second = rows_loop(finish1, (nothing, nothing))
    shift1, gain1 = add_rows(first), add_rows(second)
    sums_tile(BACK_SUMS, shift1, gain1)
    start_exchange(BACK_SUMS, True)

    def normalization_back(layer, which, inverse):
        first, second = arrived_sums(which)
        first = first / total_rows
        second = second / total_rows
        scale = inverse * v.gain_in[layer : layer + 1, :]

        def one(i, carry):
            rows = chunk(i)
            dmixed = scale * (v.dpre[rows, :] - first - v.normed[layer, rows, :] * second)
            v.dmixed[rows, :] = dmixed
            high, low = halves(dmixed)
            v.dm_hi[rows, :] = high
            v.dm_lo[rows, :] = low
            return carry

        rows_loop(one, 0)

    def attend_back(layer, between=None):
        vector = v.vector_in[layer : layer + 1, :]

        def differences(i, carry):
            rows = chunk(i)
            joined = v.joined[layer, rows, :]
            dmixed = v.dmixed[rows, :]
            for slot in range(K):
                store_pair(slot, rows, (v.taken[layer, slot, rows, :] - joined) * dmixed)
            return carry

        rows_loop(differences, 0)
        head_sums()

        def one(i, carry):
            rows = chunk(i)
            right = v.right[layer, rows, :]
            dmixed = v.dmixed[rows, :]
            dright = jnp.zeros((CHUNK, D), F32)
            for slot in range(K):
                u = v.taken[layer, slot, rows, :] + right
                sig = v.sig[layer, slot, rows, :]
                alpha = v.alpha[layer, slot, rows, :]
                dscore = alpha * v.score[slot, rows, :]
                carry = carry + fold(dscore * u * sig)
                du = dscore * vector * sig * (1.0 + u * (1.0 - sig))
                dright = dright + du
                dleft = du + alpha * dmixed
                if slot == 0:
                    v.dleft_self[rows, :] = dleft
                else:
                    high, low = halves(dleft)
                    place = pl.ds(pl.multiple_of((slot - 1) * R + i * CHUNK, CHUNK), CHUNK)
                    v.dleft_hi[place, :] = high
                    v.dleft_lo[place, :] = low
            high, low = halves(dright)
            v.dr_hi[rows, :] = high
            v.dr_lo[rows, :] = low
            return carry

        vector_sum = rows_loop(one, jnp.zeros((TILE, D), F32))
        if between is not None:
            between()

        def scattered(rows):
            pick = v.pick_t[rows, :]
            return mm(pick, v.dleft_hi[...]) + mm(pick, v.dleft_lo[...])

        def scatter():
            rows = pl.ds(0, R)
            high, low = halves(scattered(rows) + v.dleft_self[...])
            v.dl_hi[rows, :] = high
            v.dl_lo[rows, :] = low
            rows = pl.ds(R, z.halo)
            high, low = halves(scattered(rows))
            v.dl_hi[rows, :] = high
            v.dl_lo[rows, :] = low

        scatter()
        return add_rows(vector_sum)

    def dleft(rows):
        return v.dl_hi[rows, :], v.dl_lo[rows, :]

    def input_back(layer):
        own = pl.ds(0, R)
        v.dh[...] = (
            mm3(dleft(own), weight(layer, 0), mm_nt)
            + mm3((v.dr_hi[...], v.dr_lo[...]), weight(layer, 1), mm_nt)
            + mm3((v.dm_hi[...], v.dm_lo[...]), weight(layer, 2), mm_nt)
        )
        return mm3(dleft(pl.ds(R, z.halo)), weight(layer, 0), mm_nt)

    def weight_grad(layer, mat):
        if mat == 0:
            upstream = (v.dl_hi[...], v.dl_lo[...])
            inputs = (v.ht_hi[layer], v.ht_lo[layer])
        else:
            upstream = (v.dr_hi[...], v.dr_lo[...]) if mat == 1 else (v.dm_hi[...], v.dm_lo[...])
            inputs = (v.ht_hi[layer, :, pl.ds(0, R)], v.ht_lo[layer, :, pl.ds(0, R)])
        v.sums[layer, mat] = mm3(inputs, upstream)
        start_core(layer, mat)

    if z.halo < z.halo_pad:
        rest = pl.ds(R + z.halo, z.halo_pad - z.halo)
        v.dl_hi[rest, :] = jnp.zeros((z.halo_pad - z.halo, D), BF16)
        v.dl_lo[rest, :] = jnp.zeros((z.halo_pad - z.halo, D), BF16)

    end_exchange(BACK_SUMS)
    normalization_back(1, BACK_SUMS, inverse1)
    vector1 = attend_back(1)
    halo_back = input_back(1)
    dpre = v.dh[...] * v.slope[0]
    halo_dpre = halo_back * v.halo_slope[...]
    shift0 = add_rows(dpre) + add_rows(halo_dpre)
    gain0 = add_rows(dpre * v.normed[0]) + add_rows(halo_dpre * v.halo_normed[...])
    v.outgoing[BACK_ROWS] = with_sums(halo_back, shift0, gain0)
    start_exchange(BACK_ROWS)
    for mat in (2, 1, 0):
        weight_grad(1, mat)
    advance((CORE, 1, 0, 3))
    end_exchange(BACK_ROWS)
    v.dpre[...] = (v.dh[...] + give_rows_back(BACK_ROWS)) * v.slope[0]

    normalization_back(0, BACK_ROWS, inverse0)
    weight_grad(0, 2)
    vector0 = attend_back(0, lambda: weight_grad(0, 1))
    weight_grad(0, 0)

    row = iota((TILE, D), 0)
    tile = jnp.zeros((TILE, D), F32)
    for place, value in enumerate((vector0, vector1, gain0, gain1, shift0, shift1)):
        tile = jnp.where(row == place, value, tile)
    v.outgoing[SMALL, pl.ds(0, TILE), :] = tile
    start_exchange(SMALL, True)
    advance((CORE, 0, 1, 2))
    halo_back = input_back(0)
    v.outgoing[INPUT_ROWS] = halo_back
    start_exchange(INPUT_ROWS)
    advance((SECTION, 1, 0, 3), (CORE, 0, 0, 1), (SECTION, 0, 1, 2))
    end_exchange(SMALL)
    v.small[...] = jnp.sum(v.incoming[SMALL].reshape(N, TILE, D), axis=0)
    for step in range(1, S):
        pltpu.make_async_remote_copy(
            src_ref=v.small,
            dst_ref=v.small_in.at[step],
            send_sem=v.give_small.at[0],
            recv_sem=v.take_small.at[0],
            device_id={"section": lax.rem(sec + step, S)},
            device_id_type=MESH,
        ).start()
    advance((OUTER, 1, 0, 3), (SECTION, 0, 0, 1), (OUTER, 0, 1, 2))
    end_exchange(INPUT_ROWS)
    grad_in[0] = v.dh[...] + give_rows_back(INPUT_ROWS)
    advance((OUTER_BACK, 1, 0, 3), (OUTER, 0, 0, 1), (OUTER_BACK, 0, 1, 2))
    wait_bytes(v.small_in.at[pl.ds(1, S - 1)], v.take_small.at[0])
    value = v.small[...]
    for step in range(1, S):
        value = value + v.small_in[step]
    g_vec[...] = value[0:2, :]
    g_gain[...] = value[2:4, :]
    g_shift[...] = value[4:6, :]
    advance((SECTION_BACK, 1, 0, 3), (OUTER_BACK, 0, 0, 1), (SECTION_BACK, 0, 1, 2))
    advance((SECTION_BACK, 0, 0, 1))

    def receive():
        end_stage(CORE_BACK, 1, 0, 3)
        end_stage(CORE_BACK, 0, 1, 2)
        end_stage(CORE_BACK, 0, 0, 1)

    on(0, receive)
    for which in range(EXCHANGES):
        wait_bytes(v.outgoing.at[which, pl.ds(0, (N - 1) * TILE)], v.give.at[which])
    wait_bytes(v.small_in.at[pl.ds(1, S - 1)], v.give_small.at[0])

    def sent(which):
        for ref, semaphore, sender in sends_to_end:
            if sender == which:
                wait_bytes(ref(), semaphore())

    on(0, lambda: sent(0))
    on(1, lambda: sent(1))


def store_kernel(*refs):
    out, grad_in, grads, g_vec, g_gain, g_shift = refs[:6]
    pairs = [(out, refs[6]), (grad_in, refs[7])]
    for mat in range(3):
        pairs += [(grads.at[layer, mat], refs[8 + mat].at[layer]) for layer in range(2)]
    pairs += [(g_vec, refs[11]), (g_gain, refs[12]), (g_shift, refs[13])]
    copies = [pltpu.make_async_copy(*pair, refs[14].at[i]) for i, pair in enumerate(pairs)]
    for copy in copies:
        copy.start()
    for copy in copies:
        copy.wait()


def body(
    features,
    cotangent,
    train_mask,
    degree,
    neighbours,
    send_rows,
    w_left,
    w_right,
    w_res,
    attn_vec,
    bn_gain,
    bn_shift,
):
    batches, rows, width = features.shape
    sections = lax.axis_size("section")
    assert batches == sections
    z = sizes_of(
        sections, lax.axis_size("nodes"), rows, width, neighbours.shape[2], send_rows.shape[1]
    )
    shapes = scratch_of(z)
    shapes["mask_in"] = (train_mask.shape, jnp.int32)
    shapes["degree_in"] = (degree.shape, jnp.int32)
    shapes["listed_in"] = (send_rows.shape, jnp.int32)
    scratch = [pltpu.VMEM(shape, dtype) for shape, dtype in shapes.values()]
    scratch += [pltpu.SemaphoreType.DMA(shape) for shape in SEMAPHORES.values()]
    names = list(shapes) + list(SEMAPHORES)
    anywhere = pl.BlockSpec(memory_space=pl.ANY)
    square = jax.ShapeDtypeStruct((2, width, width), F32)
    columns = jax.ShapeDtypeStruct((2, width), F32)
    block = jax.ShapeDtypeStruct((1, rows, width), F32)
    results = (block, block, square, square, square, columns, columns, columns)
    in_vmem = pl.BlockSpec(memory_space=pltpu.VMEM)
    squares = jax.ShapeDtypeStruct((2, 3, width, width), F32)
    kept = (block, block, squares, columns, columns, columns)
    found = pl.pallas_call(
        functools.partial(kernel, z, names),
        out_shape=tuple(pltpu.VMEM(x.shape, x.dtype) for x in kept),
        in_specs=[pl.BlockSpec(memory_space=pltpu.HBM)] * 12,
        out_specs=(in_vmem,) * 6,
        scratch_shapes=scratch,
        compiler_params=pltpu.CompilerParams(
            collective_id=0, has_side_effects=True, vmem_limit_bytes=60 * 1024 * 1024
        ),
    )(
        features,
        cotangent,
        train_mask,
        degree,
        jnp.transpose(neighbours, (0, 2, 1)),
        send_rows,
        w_left,
        w_right,
        w_res,
        attn_vec,
        bn_gain,
        bn_shift,
    )
    return pl.pallas_call(
        store_kernel,
        out_shape=results,
        in_specs=[anywhere] * 6,
        out_specs=(anywhere,) * 8,
        scratch_shapes=[pltpu.SemaphoreType.DMA((11,))],
        compiler_params=pltpu.CompilerParams(vmem_limit_bytes=1024 * 1024),
    )(*found)


def solution(mesh):
    return jax.shard_map(
        body,
        mesh=mesh,
        in_specs=(
            P(None, "nodes", None),
            P(None, "nodes", None),
            P(None, "nodes"),
            P(None, "nodes"),
            P(None, "nodes", None),
            P(None, "nodes"),
            P(),
            P(),
            P(),
            P(),
            P(),
            P(),
        ),
        out_specs=(
            P("section", "nodes", None),
            P("section", "nodes", None),
            P(),
            P(),
            P(),
            P(),
            P(),
            P(),
        ),
        check_vma=False,
    )
```

```python
import functools
import types

import jax
import jax.numpy as jnp
from jax import lax
from jax.experimental import pallas as pl
from jax.experimental.pallas import tpu as pltpu
from jax.sharding import PartitionSpec as P

HEADS = 4
MASKED_SCORE = -1e30
VARIANCE_EPS = 1e-05
F32 = jnp.float32
BF16 = jnp.bfloat16
MESH = pl.DeviceIdType.MESH
UNROLL = 4
SHARED = ()
LANES = 128
GROUP = 64
TILE = 8
CHUNK = 16

FEATURES, MIXED, SUMS, BACK_SUMS, BACK_ROWS = range(5)
EXCHANGES = 5
CORE, SECTION, OUTER, OUTER_BACK, SECTION_BACK, CORE_BACK = range(6)
STAGES = 6


def halves(values):
    high = values.astype(BF16)
    return high, (values - high.astype(F32)).astype(BF16)


def mm(lhs, rhs):
    return jnp.dot(lhs, rhs, preferred_element_type=F32)


def mm_nt(lhs, rhs):
    return lax.dot_general(lhs, rhs, (((1,), (1,)), ((), ())), preferred_element_type=F32)


def mm3(lhs, rhs, product=mm):
    return product(lhs[0], rhs[0]) + product(lhs[1], rhs[0]) + product(lhs[0], rhs[1])


def iota(shape, dim):
    return lax.broadcasted_iota(jnp.int32, shape, dim)


def sigmoid(u):
    return 0.5 * jnp.tanh(0.5 * u) + 0.5


def as_ones(condition):
    return jnp.where(condition, 1.0, 0.0).astype(BF16)


def sizes_of(sections, partitions, rows, width, slots, listed):
    z = types.SimpleNamespace()
    z.sections, z.partitions, z.outer = sections, partitions, partitions // 2
    z.rows, z.width, z.slots, z.listed = rows, width, slots, listed
    z.send = listed // partitions
    z.halo = partitions * TILE
    z.halo_pad = -(-z.halo // LANES) * LANES
    z.table = rows + z.halo_pad
    z.picked = rows + z.halo
    z.share = rows // sections
    z.piece = max(TILE, z.share // z.outer)
    z.owners = z.share // z.piece
    return z


def scratch_of(z):
    R, D, K, T = z.rows, z.width, z.slots, z.table
    S, O = z.sections, z.outer
    vmem = {
        "features_in": ((R, D), F32),
        "cotangent_in": ((R, D), F32),
        "mask_in": (None, jnp.int32),
        "degree_in": (None, jnp.int32),
        "slots_in": ((K, R), jnp.int32),
        "listed_in": (None, jnp.int32),
        "weights_in": ((3, 2, D, D), F32),
        "vector_in": ((2, D), F32),
        "gain_in": ((2, D), F32),
        "shift_in": ((2, D), F32),
        "weights_hi": ((2, 3, D, D), BF16),
        "weights_lo": ((2, 3, D, D), BF16),
        "prep": ((LANES, R), F32),
        "prep_t": ((R, LANES), F32),
        "listed_row": ((TILE, max(LANES, z.listed)), F32),
        "pick": ((K - 1, R, R + 2 * z.halo_pad), BF16),
        "pick_t": ((z.picked, (K - 1) * R), BF16),
        "list": ((z.halo, R), BF16),
        "list_t": ((R, z.halo_pad), BF16),
        "ones": ((2 * D, D), BF16),
        "h": ((T, D), F32),
        "h_hi": ((T, D), BF16),
        "h_lo": ((T, D), BF16),
        "ht_hi": ((2, D, T), BF16),
        "ht_lo": ((2, D, T), BF16),
        "table_hi": ((R, D), BF16),
        "table_lo": ((R, D), BF16),
        "halo_table": ((2 * z.halo_pad, D), BF16),
        "taken": ((2, K, R, D), F32),
        "act": ((2, K, R, D), F32),
        "rise": ((2, K, R, D), F32),
        "alpha": ((2, K, R, D), F32),
        "joined": ((2, R, D), F32),
        "right": ((2, R, D), F32),
        "skip": ((R, D), F32),
        "mixed": ((R, D), F32),
        "normed": ((2, R, D), F32),
        "slope": ((2, R, D), F32),
        "halo_normed": ((z.halo, D), F32),
        "halo_slope": ((z.halo, D), F32),
        "pair": ((K, R, 2 * D), BF16),
        "score": ((K, R, D), F32),
        "dpre": ((R, D), F32),
        "dmixed": ((R, D), F32),
        "dm_hi": ((R, D), BF16),
        "dm_lo": ((R, D), BF16),
        "dr_hi": ((R, D), BF16),
        "dr_lo": ((R, D), BF16),
        "dl_hi": ((T, D), BF16),
        "dl_lo": ((T, D), BF16),
        "dleft_self": ((R, D), F32),
        "dleft_hi": (((K - 1) * R, D), BF16),
        "dleft_lo": (((K - 1) * R, D), BF16),
        "dh": ((R, D), F32),
        "outgoing": ((EXCHANGES, z.halo, D), F32),
        "incoming": ((EXCHANGES, z.halo, D), F32),
        "small": ((4, TILE, D), F32),
        "small_core": ((2, TILE, D), F32),
        "small_outer": ((O, TILE, D), F32),
        "small_section": ((S, TILE, D), F32),
        "returning": ((z.halo, LANES), F32),
        "returned": ((z.halo, LANES), F32),
        "sums": ((2, 3, R, D), F32),
        "from_core": ((2, 3, R, D), F32),
        "from_section": ((2, S - 1, 3, z.share, D), F32),
        "from_outer": ((2, O, 3, z.piece, D), F32),
        "shares": ((3, O, z.share, D), F32),
    }
    return vmem


SEMAPHORES = {
    "load": (12,),
    "give": (EXCHANGES,),
    "take": (EXCHANGES,),
    "give_small": (4,),
    "take_small": (4,),
    "give_rows": (1,),
    "take_rows": (1,),
    "give_stage": (2, 3, STAGES),
    "take_stage": (2, 3, STAGES),
}


def kernel(z, names, *refs):
    features, cotangent, train_mask, degree, neighbours, send_rows = refs[:6]
    w_left, w_right, w_res, attn_vec, bn_gain, bn_shift = refs[6:12]
    out, grad_in, grads, g_vec, g_gain, g_shift = refs[12:18]
    v = types.SimpleNamespace(**dict(zip(names, refs[18:])))
    R, D, K, T = z.rows, z.width, z.slots, z.table
    S, N, O = z.sections, z.partitions, z.outer
    total_rows = R * N
    sec = lax.axis_index("section")
    me = lax.axis_index("nodes")
    core = lax.rem(me, 2)
    outer = lax.div(me, 2)
    mate = me + 1 - 2 * core

    barrier = pltpu.get_barrier_semaphore()

    def greet(step, carry):
        pl.semaphore_signal(
            barrier, inc=1, device_id={"nodes": lax.rem(me + step, N)}, device_id_type=MESH
        )
        return carry

    lax.fori_loop(1, N, greet, 0)
    for step in range(1, S):
        pl.semaphore_signal(
            barrier, inc=1, device_id={"section": lax.rem(sec + step, S)}, device_id_type=MESH
        )

    loads = []
    for source, target in (
        (features.at[sec], v.features_in),
        (send_rows, v.listed_in),
        (w_left, v.weights_in.at[0]),
        (w_right, v.weights_in.at[1]),
        (w_res, v.weights_in.at[2]),
        (neighbours.at[sec], v.slots_in),
        (degree, v.degree_in),
        (train_mask, v.mask_in),
        (attn_vec, v.vector_in),
        (bn_gain, v.gain_in),
        (bn_shift, v.shift_in),
        (cotangent.at[sec], v.cotangent_in),
    ):
        copy = pltpu.make_async_copy(source, target, v.load.at[len(loads)])
        copy.start()
        loads.append(copy)

    def rows_loop(body, start):
        return lax.fori_loop(0, R // CHUNK, body, start, unroll=UNROLL)

    def chunk(i):
        return pl.ds(pl.multiple_of(i * CHUNK, CHUNK), CHUNK)

    def fold(values):
        return jnp.sum(values.reshape(values.shape[0] // TILE, TILE, values.shape[1]), axis=0)

    def add_rows(values):
        return jnp.sum(values, axis=0, keepdims=True)


    def start_exchange(which, one_tile=False):
        def send(step, carry):
            other = lax.rem(me + step, N)
            place = 0 if one_tile else pl.multiple_of(other * TILE, TILE)
            pltpu.make_async_remote_copy(
                src_ref=v.outgoing.at[which, pl.ds(place, TILE)],
                dst_ref=v.incoming.at[which, pl.ds(pl.multiple_of(me * TILE, TILE), TILE)],
                send_sem=v.give.at[which],
                recv_sem=v.take.at[which],
                device_id={"nodes": other},
                device_id_type=MESH,
            ).start()
            return carry

        lax.fori_loop(1, N, send, 0)
        own = pl.ds(pl.multiple_of(me * TILE, TILE), TILE)
        mine = pl.ds(0, TILE) if one_tile else own
        v.incoming[which, own, :] = v.outgoing[which, mine, :]

    def wait_bytes(ref, semaphore):
        pltpu.make_async_copy(ref, ref, semaphore).wait()

    def end_exchange(which):
        wait_exchange(which)

    def wait_exchange(which):
        wait_bytes(v.incoming.at[which, pl.ds(0, (N - 1) * TILE)], v.take.at[which])

    def row_in_tile(rows):
        return lax.rem(iota((rows, D), 0), TILE)

    def with_sums(values, first, second):
        row = row_in_tile(values.shape[0])
        return values + jnp.where(row == z.send, first, 0.0) + jnp.where(row == z.send + 1, second, 0.0)

    def arrived_sums(which):
        tile = jnp.sum(v.incoming[which].reshape(N, TILE, D), axis=0)
        return tile[z.send : z.send + 1, :], tile[z.send + 1 : z.send + 2, :]

    def arrived_rows(which):
        values = v.incoming[which]
        return jnp.where(row_in_tile(z.halo) < z.send, values, 0.0)

    def give_rows_back(which):
        high, low = halves(arrived_rows(which))
        listed = v.list_t[:, : z.halo]
        return mm(listed, high) + mm(listed, low)

    def owner(layer):
        return 1 - layer

    sends_to_end = []

    def on(which, body):
        pl.when(core == which)(body)

    def stage_copy(layer, first, stage, source, target, device):
        pltpu.make_async_remote_copy(
            src_ref=source,
            dst_ref=target,
            send_sem=v.give_stage.at[layer, first, stage],
            recv_sem=v.take_stage.at[layer, first, stage],
            device_id=device,
            device_id_type=MESH,
        ).start()

    def stage_sent(layer, first, stage, ref, which):
        sends_to_end.append((ref, lambda: v.give_stage.at[layer, first, stage], which))

    def share_rows(which):
        return pl.ds(pl.multiple_of(which * z.share, TILE), z.share)

    def piece_rows(which):
        return pl.ds(pl.multiple_of(sec * z.share + which * z.piece, TILE), z.piece)

    def outer_device(which):
        return {"nodes": which * 2 + core}

    def from_others(layer, mats, count):
        return v.from_outer.at[layer, pl.ds(1, count), mats]

    def start_core(layer, mat):
        on(
            1 - owner(layer),
            lambda: stage_copy(
                layer, mat, CORE, v.sums.at[layer, mat], v.from_core.at[layer, mat], {"nodes": mate}
            ),
        )
        stage_sent(layer, mat, CORE, lambda: v.from_core.at[layer, mat], 1 - owner(layer))

    def start_stage(stage, layer, first, count):
        mats = pl.ds(first, count)
        if stage == SECTION:
            for step in range(1, S):
                other = lax.rem(sec + step, S)
                stage_copy(
                    layer,
                    first,
                    stage,
                    v.sums.at[layer, mats, share_rows(other)],
                    v.from_section.at[layer, step - 1, mats],
                    {"section": other},
                )
            stage_sent(layer, first, stage, lambda: v.from_section.at[layer, :, mats], owner(layer))
        elif stage == OUTER and layer in SHARED:
            for step in range(1, O):
                stage_copy(
                    layer,
                    first,
                    stage,
                    v.sums.at[layer, first, share_rows(sec)],
                    v.shares.at[first, outer],
                    outer_device(lax.rem(outer + step, O)),
                )
            stage_sent(layer, first, stage, lambda: v.shares.at[first, pl.ds(1, O - 1)], owner(layer))
            v.shares[first, outer] = v.sums[layer, first, share_rows(sec), :]
        elif stage == OUTER:
            if z.owners == O:
                for step in range(1, O):
                    other = lax.rem(outer + step, O)
                    stage_copy(
                        layer,
                        first,
                        stage,
                        v.sums.at[layer, mats, piece_rows(other)],
                        v.from_outer.at[layer, step, mats],
                        outer_device(other),
                    )
                stage_sent(layer, first, stage, lambda: from_others(layer, mats, O - 1), owner(layer))
            else:
                for other in range(z.owners):

                    @pl.when(outer != other)
                    def _():
                        stage_copy(
                            layer,
                            first,
                            stage,
                            v.sums.at[layer, mats, piece_rows(other)],
                            v.from_outer.at[layer, lax.rem(outer - other + O, O), mats],
                            outer_device(other),
                        )
                        wait_bytes(
                            v.from_outer.at[layer, 0, mats], v.give_stage.at[layer, first, stage]
                        )

        elif stage == OUTER_BACK:

            def send_all():
                for step in range(1, O):
                    stage_copy(
                        layer,
                        first,
                        stage,
                        grads.at[layer, mats, piece_rows(outer)],
                        grads.at[layer, mats, piece_rows(outer)],
                        outer_device(lax.rem(outer + step, O)),
                    )

            if z.owners == O:
                send_all()
                stage_sent(layer, first, stage, lambda: from_others(layer, mats, O - 1), owner(layer))
            else:

                @pl.when(outer < z.owners)
                def _():
                    send_all()
                    wait_bytes(
                        from_others(layer, mats, O - 1), v.give_stage.at[layer, first, stage]
                    )

        elif stage == SECTION_BACK:
            for step in range(1, S):
                stage_copy(
                    layer,
                    first,
                    stage,
                    grads.at[layer, mats, share_rows(sec)],
                    grads.at[layer, mats, share_rows(sec)],
                    {"section": lax.rem(sec + step, S)},
                )
            stage_sent(layer, first, stage, lambda: v.from_section.at[layer, :, mats], owner(layer))
        elif stage == CORE_BACK:
            stage_copy(
                layer, first, stage, grads.at[layer, mats], grads.at[layer, mats], {"nodes": mate}
            )
            stage_sent(layer, first, stage, lambda: grads.at[layer, mats], owner(layer))

    def end_stage(stage, layer, first, count):
        mats = pl.ds(first, count)
        taken = v.take_stage.at[layer, first, stage]
        each = range(first, first + count)
        if stage == CORE:
            wait_bytes(v.from_core.at[layer, first], taken)
            v.sums[layer, first] = v.sums[layer, first] + v.from_core[layer, first]
        elif stage == SECTION:
            wait_bytes(v.from_section.at[layer, :, mats], taken)
            for mat in each:
                value = v.sums[layer, mat, share_rows(sec), :]
                for step in range(S - 1):
                    value = value + v.from_section[layer, step, mat]
                v.sums[layer, mat, share_rows(sec), :] = value
        elif stage == OUTER and layer in SHARED:
            wait_bytes(v.shares.at[first, pl.ds(1, O - 1)], taken)
            value = v.shares[first, 0]
            for other in range(1, O):
                value = value + v.shares[first, other]
            grads[layer, first, share_rows(sec), :] = value
        elif stage == OUTER:

            def add():
                wait_bytes(from_others(layer, mats, O - 1), taken)
                for mat in each:
                    value = v.sums[layer, mat, piece_rows(outer), :]
                    for step in range(1, O):
                        value = value + v.from_outer[layer, step, mat]
                    grads[layer, mat, piece_rows(outer), :] = value

            if z.owners == O:
                add()
            else:
                pl.when(outer < z.owners)(add)
        elif stage == OUTER_BACK:
            if z.owners == O:
                wait_bytes(from_others(layer, mats, O - 1), taken)
            else:
                wait_bytes(from_others(layer, mats, z.owners - 1), taken)

                @pl.when(outer >= z.owners)
                def _():
                    wait_bytes(v.from_outer.at[layer, 0, mats], taken)

        elif stage == SECTION_BACK:
            wait_bytes(v.from_section.at[layer, :, mats], taken)
        elif stage == CORE_BACK:
            wait_bytes(grads.at[layer, mats], taken)

    def stage_after(stage, layer):
        return SECTION_BACK if stage == OUTER and layer in SHARED else stage + 1

    def advance(layer, *moves):
        def run():
            for stage, mat in moves:
                end_stage(stage, layer, mat, 1)
                start_stage(stage_after(stage, layer), layer, mat, 1)

        on(owner(layer), run)


    loads[1].wait()
    v.listed_row[...] = jnp.zeros_like(v.listed_row)
    v.listed_row[0:1, : z.listed] = v.listed_in[pl.ds(sec, 1), :].astype(F32)
    spread_from = iota((v.listed_row.shape[1], z.halo_pad), 0)
    spread_to = iota((v.listed_row.shape[1], z.halo_pad), 1)
    spread = as_ones(
        (lax.div(spread_from, z.send) == lax.div(spread_to, TILE))
        & (lax.rem(spread_from, z.send) == lax.rem(spread_to, TILE))
        & (spread_from < z.listed)
    )
    listed = mm(v.listed_row[...].astype(BF16), spread)[0:1, :]
    place = iota((1, z.halo_pad), 1)
    real = (lax.rem(place, TILE) < z.send) & (place < z.halo)
    listed = jnp.where(real, listed, -1.0)
    list_t = jnp.where(iota((R, z.halo_pad), 0).astype(F32) == listed, 1.0, 0.0)
    v.list_t[...] = list_t.astype(BF16)
    v.list[...] = list_t.T[: z.halo, :].astype(BF16)

    loads[0].wait()
    own = v.features_in[...]
    v.h[pl.ds(0, R), :] = own
    high, low = halves(own)
    v.h_hi[pl.ds(0, R), :] = high
    v.h_lo[pl.ds(0, R), :] = low
    v.outgoing[FEATURES] = mm(v.list[...], high) + mm(v.list[...], low)
    pl.semaphore_wait(barrier, N - 1 + S - 1)
    start_exchange(FEATURES)

    for load in loads[2:5]:
        load.wait()
    for layer in range(2):
        for mat in range(3):
            high, low = halves(v.weights_in[mat, layer])
            v.weights_hi[layer, mat] = high
            v.weights_lo[layer, mat] = low

    def weight(layer, mat):
        return v.weights_hi[layer, mat], v.weights_lo[layer, mat]

    for load in loads[5:11]:
        load.wait()
    named = v.slots_in[...]
    offset = named - R
    remote = R + lax.div(offset, z.send) * TILE + lax.rem(offset, z.send)
    named = jnp.where(named < R, named, remote).astype(F32)
    v.prep[...] = jnp.zeros_like(v.prep)
    v.prep[pl.ds(0, K), :] = named
    v.prep[pl.ds(K, 1), :] = v.degree_in[pl.ds(sec, 1), :].astype(F32)
    v.prep[pl.ds(K + 1, 1), :] = v.mask_in[pl.ds(sec, 1), :].astype(F32)
    v.prep_t[...] = v.prep[...].T
    for slot in range(1, K):
        column = v.prep_t[:, slot : slot + 1]
        pick = as_ones(iota((R, T), 1).astype(F32) == column)
        v.pick[slot - 1, :, pl.ds(0, T)] = pick
        v.pick[slot - 1, :, pl.ds(T, z.halo_pad)] = pick[:, R:]
        row = v.prep[slot : slot + 1, :]
        v.pick_t[:, (slot - 1) * R : slot * R] = as_ones(iota((z.picked, R), 0).astype(F32) == row)
    block_row = lax.div(lax.rem(iota((2 * D, D), 0), D), GROUP)
    v.ones[...] = as_ones(block_row == lax.div(iota((2 * D, D), 1), GROUP))

    def project(layer):
        rows = pl.ds(0, R)
        own = (v.h_hi[rows, :], v.h_lo[rows, :])
        left = mm3(own, weight(layer, 0))
        v.taken[layer, 0] = left
        high, low = halves(left)
        v.table_hi[rows, :] = high
        v.table_lo[rows, :] = low
        v.right[layer] = mm3(own, weight(layer, 1))
        v.skip[...] = mm3(own, weight(layer, 2))

    def project_halo(layer):
        rows = pl.ds(R, z.halo_pad)
        left = mm3((v.h_hi[rows, :], v.h_lo[rows, :]), weight(layer, 0))
        high, low = halves(left)
        v.halo_table[pl.ds(0, z.halo_pad), :] = high
        v.halo_table[pl.ds(z.halo_pad, z.halo_pad), :] = low

    def store_halo(values):
        if z.halo < z.halo_pad:
            rest = pl.ds(R + z.halo, z.halo_pad - z.halo)
            v.h[rest, :] = jnp.zeros((z.halo_pad - z.halo, D), F32)
            v.h_hi[rest, :] = jnp.zeros((z.halo_pad - z.halo, D), BF16)
            v.h_lo[rest, :] = jnp.zeros((z.halo_pad - z.halo, D), BF16)
        rows = pl.ds(R, z.halo)
        v.h[rows, :] = values
        high, low = halves(values)
        v.h_hi[rows, :] = high
        v.h_lo[rows, :] = low

    def keep_transposed(layer):
        high, low = halves(v.h[...].T)
        v.ht_hi[layer] = high
        v.ht_lo[layer] = low

    def head_sums():
        def one(slot, carry):
            v.score[slot] = mm(v.pair[slot], v.ones[...])
            return carry

        lax.fori_loop(0, K, one, 0, unroll=True)

    def store_pair(slot, rows, values):
        high, low = halves(values)
        v.pair[slot, rows, pl.ds(0, D)] = high
        v.pair[slot, rows, pl.ds(D, D)] = low

    def gather_own(layer):
        def one(slot, carry):
            pick = v.pick[slot - 1, :, pl.ds(0, R)]
            v.taken[layer, slot] = mm(pick, v.table_hi[...]) + mm(pick, v.table_lo[...])
            return carry

        lax.fori_loop(1, K, one, 0, unroll=True)

    def gather_halo(layer):
        def one(slot, carry):
            pick = v.pick[slot - 1, :, pl.ds(R, 2 * z.halo_pad)]
            v.taken[layer, slot] = v.taken[layer, slot] + mm(pick, v.halo_table[...])
            return carry

        lax.fori_loop(1, K, one, 0, unroll=True)

    def gather_all(layer):
        def one(slot, carry):
            own = v.pick[slot - 1, :, pl.ds(0, R)]
            halo = v.pick[slot - 1, :, pl.ds(R, 2 * z.halo_pad)]
            v.taken[layer, slot] = (
                mm(own, v.table_hi[...]) + mm(own, v.table_lo[...]) + mm(halo, v.halo_table[...])
            )
            return carry

        lax.fori_loop(1, K, one, 0, unroll=True)

    def attend(layer):
        vector = v.vector_in[layer : layer + 1, :]

        def activate(i, carry):
            rows = chunk(i)
            right = v.right[layer, rows, :]
            for slot in range(K):
                u = v.taken[layer, slot, rows, :] + right
                store_pair(slot, rows, u * sigmoid(u) * vector)
            return carry

        rows_loop(activate, 0)
        head_sums()

        def mix(i, carry):
            rows = chunk(i)
            count = jnp.broadcast_to(v.prep_t[rows, K : K + 1], (CHUNK, D))
            scores = [
                jnp.where(count > slot, v.score[slot, rows, :], MASKED_SCORE) for slot in range(K)
            ]
            highest = functools.reduce(jnp.maximum, scores)
            powers = [jnp.exp(score - highest) for score in scores]
            scale = 1.0 / functools.reduce(jnp.add, powers)
            joined = jnp.zeros((CHUNK, D), F32)
            for slot in range(K):
                alpha = powers[slot] * scale
                v.alpha[layer, slot, rows, :] = alpha
                joined = joined + alpha * v.taken[layer, slot, rows, :]
            v.joined[layer, rows, :] = joined
            mixed = joined + v.skip[rows, :]
            v.mixed[rows, :] = mixed
            return carry[0] + fold(mixed), carry[1] + fold(mixed * mixed)

        nothing = jnp.zeros((TILE, D), F32)
        first, second = rows_loop(mix, (nothing, nothing))
        return add_rows(first), add_rows(second)

    def derive(layer):
        vector = v.vector_in[layer : layer + 1, :]

        def one(i, carry):
            rows = chunk(i)
            right = v.right[layer, rows, :]
            for slot in range(K):
                u = v.taken[layer, slot, rows, :] + right
                sig = sigmoid(u)
                act = u * sig
                v.act[layer, slot, rows, :] = act
                v.rise[layer, slot, rows, :] = vector * (sig + act * (1.0 - sig))
            return carry

        rows_loop(one, 0)

    def moments(which):
        first, second = arrived_sums(which)
        mean = first / total_rows
        return mean, lax.rsqrt(second / total_rows - mean * mean + VARIANCE_EPS)

    def activation(layer, mixed, mean, inverse):
        normed = (mixed - mean) * inverse
        pre = v.gain_in[layer : layer + 1, :] * normed + v.shift_in[layer : layer + 1, :]
        power = jnp.exp(jnp.minimum(pre, 0.0))
        return normed, jnp.where(pre > 0, 1.0, power), jnp.where(pre > 0, pre, power - 1.0)

    def sums_tile(which, first, second):
        v.outgoing[which, pl.ds(0, TILE), :] = with_sums(jnp.zeros((TILE, D), F32), first, second)

    def list_rows(values):
        high, low = halves(values)
        return mm(v.list[...], high) + mm(v.list[...], low)

    project(0)
    gather_own(0)
    end_exchange(FEATURES)
    store_halo(arrived_rows(FEATURES))
    project_halo(0)
    gather_halo(0)
    first, second = attend(0)
    v.outgoing[MIXED] = with_sums(list_rows(v.mixed[...]), first, second)
    start_exchange(MIXED)
    keep_transposed(0)
    derive(0)
    end_exchange(MIXED)
    mean0, inverse0 = moments(MIXED)

    def finish0(i, carry):
        rows = chunk(i)
        normed, slope, hidden = activation(0, v.mixed[rows, :], mean0, inverse0)
        v.normed[0, rows, :] = normed
        v.slope[0, rows, :] = slope
        v.h[rows, :] = hidden
        high, low = halves(hidden)
        v.h_hi[rows, :] = high
        v.h_lo[rows, :] = low
        return carry

    rows_loop(finish0, 0)
    normed, slope, hidden = activation(0, arrived_rows(MIXED), mean0, inverse0)
    v.halo_normed[...] = normed
    v.halo_slope[...] = slope
    store_halo(jnp.where(row_in_tile(z.halo) < z.send, hidden, 0.0))

    project(1)
    project_halo(1)
    gather_all(1)
    first, second = attend(1)
    sums_tile(SUMS, first, second)
    start_exchange(SUMS, True)
    keep_transposed(1)
    derive(1)
    loads[11].wait()
    end_exchange(SUMS)
    mean1, inverse1 = moments(SUMS)

    def finish1(i, carry):
        rows = chunk(i)
        normed, slope, hidden = activation(1, v.mixed[rows, :], mean1, inverse1)
        v.normed[1, rows, :] = normed
        out[0, rows, :] = hidden
        dpre = v.cotangent_in[rows, :] * v.prep_t[rows, K + 1 : K + 2] * slope
        v.dpre[rows, :] = dpre
        return carry[0] + fold(dpre), carry[1] + fold(dpre * normed)

    nothing = jnp.zeros((TILE, D), F32)
    first, second = rows_loop(finish1, (nothing, nothing))
    shift1, gain1 = add_rows(first), add_rows(second)
    sums_tile(BACK_SUMS, shift1, gain1)
    start_exchange(BACK_SUMS, True)

    def normalization_back(layer, which, inverse):
        first, second = arrived_sums(which)
        first = first / total_rows
        second = second / total_rows
        scale = inverse * v.gain_in[layer : layer + 1, :]

        def one(i, carry):
            rows = chunk(i)
            dmixed = scale * (v.dpre[rows, :] - first - v.normed[layer, rows, :] * second)
            v.dmixed[rows, :] = dmixed
            high, low = halves(dmixed)
            v.dm_hi[rows, :] = high
            v.dm_lo[rows, :] = low
            return carry

        rows_loop(one, 0)

    def attend_back(layer, between=None):
        def differences(i, carry):
            rows = chunk(i)
            joined = v.joined[layer, rows, :]
            dmixed = v.dmixed[rows, :]
            for slot in range(K):
                store_pair(slot, rows, (v.taken[layer, slot, rows, :] - joined) * dmixed)
            return carry

        rows_loop(differences, 0)
        head_sums()

        def one(i, carry):
            rows = chunk(i)
            dmixed = v.dmixed[rows, :]
            dright = jnp.zeros((CHUNK, D), F32)
            for slot in range(K):
                alpha = v.alpha[layer, slot, rows, :]
                dscore = alpha * v.score[slot, rows, :]
                carry = carry + fold(dscore * v.act[layer, slot, rows, :])
                du = dscore * v.rise[layer, slot, rows, :]
                dright = dright + du
                dleft = du + alpha * dmixed
                if slot == 0:
                    v.dleft_self[rows, :] = dleft
                else:
                    high, low = halves(dleft)
                    place = pl.ds(pl.multiple_of((slot - 1) * R + i * CHUNK, CHUNK), CHUNK)
                    v.dleft_hi[place, :] = high
                    v.dleft_lo[place, :] = low
            high, low = halves(dright)
            v.dr_hi[rows, :] = high
            v.dr_lo[rows, :] = low
            return carry

        vector_sum = rows_loop(one, jnp.zeros((TILE, D), F32))
        if between is not None:
            between()

        def scattered(rows):
            pick = v.pick_t[rows, :]
            return mm(pick, v.dleft_hi[...]) + mm(pick, v.dleft_lo[...])

        rows = pl.ds(0, R)
        own = scattered(rows) + v.dleft_self[...]
        v.dleft_self[...] = own
        high, low = halves(own)
        v.dl_hi[rows, :] = high
        v.dl_lo[rows, :] = low
        rows = pl.ds(R, z.halo)
        halo = scattered(rows)
        if layer == 0:
            start_return(halo)
        high, low = halves(halo)
        v.dl_hi[rows, :] = high
        v.dl_lo[rows, :] = low
        return add_rows(vector_sum)

    def start_return(halo):
        v.returning[...] = halo[:, :LANES] + pltpu.roll(halo[:, LANES:], z.send, 0)
        own = pl.ds(pl.multiple_of(me * TILE, TILE), TILE)

        def send(step, carry):
            other = lax.rem(me + step, N)
            pltpu.make_async_remote_copy(
                src_ref=v.returning.at[pl.ds(pl.multiple_of(other * TILE, TILE), TILE)],
                dst_ref=v.returned.at[own],
                send_sem=v.give_rows.at[0],
                recv_sem=v.take_rows.at[0],
                device_id={"nodes": other},
                device_id_type=MESH,
            ).start()
            return carry

        lax.fori_loop(1, N, send, 0)
        v.returned[own, :] = v.returning[own, :]

    def dleft(rows):
        return v.dl_hi[rows, :], v.dl_lo[rows, :]

    def input_back(layer):
        own = pl.ds(0, R)
        v.dh[...] = (
            mm3(dleft(own), weight(layer, 0), mm_nt)
            + mm3((v.dr_hi[...], v.dr_lo[...]), weight(layer, 1), mm_nt)
            + mm3((v.dm_hi[...], v.dm_lo[...]), weight(layer, 2), mm_nt)
        )
        return mm3(dleft(pl.ds(R, z.halo)), weight(layer, 0), mm_nt)

    def weight_grad(layer, mat):
        if mat == 0:
            upstream = (v.dl_hi[...], v.dl_lo[...])
            inputs = (v.ht_hi[layer], v.ht_lo[layer])
        else:
            upstream = (v.dr_hi[...], v.dr_lo[...]) if mat == 1 else (v.dm_hi[...], v.dm_lo[...])
            inputs = (v.ht_hi[layer, :, pl.ds(0, R)], v.ht_lo[layer, :, pl.ds(0, R)])
        v.sums[layer, mat] = mm3(inputs, upstream)
        start_core(layer, mat)

    if z.halo < z.halo_pad:
        rest = pl.ds(R + z.halo, z.halo_pad - z.halo)
        v.dl_hi[rest, :] = jnp.zeros((z.halo_pad - z.halo, D), BF16)
        v.dl_lo[rest, :] = jnp.zeros((z.halo_pad - z.halo, D), BF16)

    end_exchange(BACK_SUMS)
    normalization_back(1, BACK_SUMS, inverse1)
    vector1 = attend_back(1)
    halo_back = input_back(1)
    dpre = v.dh[...] * v.slope[0]
    halo_dpre = halo_back * v.halo_slope[...]
    shift0 = add_rows(dpre) + add_rows(halo_dpre)
    gain0 = add_rows(dpre * v.normed[0]) + add_rows(halo_dpre * v.halo_normed[...])
    v.outgoing[BACK_ROWS] = with_sums(halo_back, shift0, gain0)
    start_exchange(BACK_ROWS)
    for mat in (2, 1, 0):
        weight_grad(1, mat)
    advance(1, (CORE, 2), (CORE, 1), (CORE, 0))
    end_exchange(BACK_ROWS)
    v.dpre[...] = (v.dh[...] + give_rows_back(BACK_ROWS)) * v.slope[0]

    normalization_back(0, BACK_ROWS, inverse0)
    weight_grad(0, 2)

    def between():
        weight_grad(0, 1)
        advance(1, (SECTION, 2))
        advance(0, (CORE, 2))

    vector0 = attend_back(0, between)
    weight_grad(0, 0)

    row = iota((TILE, D), 0)
    tile = jnp.zeros((TILE, D), F32)
    for place, value in enumerate((vector0, vector1, gain0, gain1, shift0, shift1)):
        tile = jnp.where(row == place, value, tile)
    v.small[0] = tile

    def send_small(stage, source, target, device):
        pltpu.make_async_remote_copy(
            src_ref=source,
            dst_ref=target,
            send_sem=v.give_small.at[stage],
            recv_sem=v.take_small.at[stage],
            device_id=device,
            device_id_type=MESH,
        ).start()

    on(0, lambda: send_small(0, v.small.at[0], v.small_core.at[0], {"nodes": mate}))

    def small_outer():
        wait_bytes(v.small_core.at[0], v.take_small.at[0])
        value = v.small[0] + v.small_core[0]
        v.small[1] = value
        v.small_outer[outer] = value
        for step in range(1, O):
            send_small(
                1, v.small.at[1], v.small_outer.at[outer], outer_device(lax.rem(outer + step, O))
            )

    def small_section():
        wait_bytes(v.small_outer.at[pl.ds(1, O - 1)], v.take_small.at[1])
        value = jnp.sum(v.small_outer[...], axis=0)
        v.small[2] = value
        v.small_section[sec] = value
        for step in range(1, S):
            send_small(
                2, v.small.at[2], v.small_section.at[sec], {"section": lax.rem(sec + step, S)}
            )

    def put_small(value):
        g_vec[...] = value[0:2, :]
        g_gain[...] = value[2:4, :]
        g_shift[...] = value[4:6, :]

    def small_back():
        wait_bytes(v.small_section.at[pl.ds(1, S - 1)], v.take_small.at[2])
        value = jnp.sum(v.small_section[...], axis=0)
        v.small[3] = value
        send_small(3, v.small.at[3], v.small_core.at[1], {"nodes": mate})
        put_small(value)

    def small_end():
        wait_bytes(v.small_core.at[1], v.take_small.at[3])
        put_small(v.small_core[1])

    advance(1, (SECTION, 1))
    advance(0, (CORE, 1))
    def part_input():
        v.dh[...] = mm3((v.dr_hi[...], v.dr_lo[...]), weight(0, 1), mm_nt) + mm3(
            (v.dm_hi[...], v.dm_lo[...]), weight(0, 2), mm_nt
        )

    def store_input():
        wait_bytes(v.returned.at[pl.ds(0, (N - 1) * TILE)], v.take_rows.at[0])
        values = v.returned[...]
        values = jnp.concatenate([values, pltpu.roll(values, z.halo - z.send, 0)], axis=1)
        high, low = halves(jnp.where(row_in_tile(z.halo) < z.send, values, 0.0))
        listed = v.list_t[:, : z.halo]
        left = v.dleft_self[...] + (mm(listed, high) + mm(listed, low))
        grad_in[0] = v.dh[...] + mm3(halves(left), weight(0, 0), mm_nt)

    tails = {
        1: (
            (SECTION, 0),
            (OUTER, 2),
            part_input,
            (OUTER, 1),
            (OUTER, 0),
            store_input,
            (OUTER_BACK, 2),
            (OUTER_BACK, 1),
            (OUTER_BACK, 0),
            (SECTION_BACK, 2),
            (SECTION_BACK, 1),
            (SECTION_BACK, 0),
            small_end,
        ),
        0: (
            (CORE, 0),
            (SECTION, 2),
            small_outer,
            (SECTION, 1),
            (SECTION, 0),
            part_input,
            (OUTER, 2),
            (OUTER, 1),
            (OUTER, 0),
            store_input,
            small_section,
            (OUTER_BACK, 2),
            (OUTER_BACK, 1),
            (OUTER_BACK, 0),
            small_back,
            (SECTION_BACK, 2),
            (SECTION_BACK, 1),
            (SECTION_BACK, 0),
        ),
    }

    def finish(layer):
        for step in tails[layer]:
            if callable(step):
                step()
            else:
                end_stage(step[0], layer, step[1], 1)
                start_stage(stage_after(step[0], layer), layer, step[1], 1)

    on(owner(1), lambda: finish(1))
    on(owner(0), lambda: finish(0))

    def receive(layer):
        for mat in range(3):
            end_stage(CORE_BACK, layer, mat, 1)

    on(0, lambda: receive(0))
    on(1, lambda: receive(1))
    for which in range(EXCHANGES):
        wait_bytes(v.outgoing.at[which, pl.ds(0, (N - 1) * TILE)], v.give.at[which])
    wait_bytes(v.returned.at[pl.ds(0, (N - 1) * TILE)], v.give_rows.at[0])

    def sent(which):
        for ref, semaphore, sender in sends_to_end:
            if sender == which:
                wait_bytes(ref(), semaphore())

    def sent_small(stage, count):
        wait_bytes(v.small_outer.at[pl.ds(0, count)], v.give_small.at[stage])

    def sent0():
        sent(0)
        sent_small(0, 1)

    def sent1():
        sent(1)
        sent_small(1, O - 1)
        wait_bytes(v.small_section.at[pl.ds(1, S - 1)], v.give_small.at[2])
        sent_small(3, 1)

    on(0, sent0)
    on(1, sent1)


def store_kernel(*refs):
    out, grad_in, grads, g_vec, g_gain, g_shift = refs[:6]
    pairs = [(out, refs[6]), (grad_in, refs[7])]
    for mat in range(3):
        pairs += [(grads.at[layer, mat], refs[8 + mat].at[layer]) for layer in range(2)]
    pairs += [(g_vec, refs[11]), (g_gain, refs[12]), (g_shift, refs[13])]
    copies = [pltpu.make_async_copy(*pair, refs[14].at[i]) for i, pair in enumerate(pairs)]
    for copy in copies:
        copy.start()
    for copy in copies:
        copy.wait()


def body(
    features,
    cotangent,
    train_mask,
    degree,
    neighbours,
    send_rows,
    w_left,
    w_right,
    w_res,
    attn_vec,
    bn_gain,
    bn_shift,
):
    batches, rows, width = features.shape
    sections = lax.axis_size("section")
    assert batches == sections and width == HEADS * GROUP
    z = sizes_of(
        sections, lax.axis_size("nodes"), rows, width, neighbours.shape[2], send_rows.shape[1]
    )
    shapes = scratch_of(z)
    shapes["mask_in"] = (train_mask.shape, jnp.int32)
    shapes["degree_in"] = (degree.shape, jnp.int32)
    shapes["listed_in"] = (send_rows.shape, jnp.int32)
    scratch = [pltpu.VMEM(shape, dtype) for shape, dtype in shapes.values()]
    scratch += [pltpu.SemaphoreType.DMA(shape) for shape in SEMAPHORES.values()]
    names = list(shapes) + list(SEMAPHORES)
    anywhere = pl.BlockSpec(memory_space=pl.ANY)
    square = jax.ShapeDtypeStruct((2, width, width), F32)
    columns = jax.ShapeDtypeStruct((2, width), F32)
    block = jax.ShapeDtypeStruct((1, rows, width), F32)
    results = (block, block, square, square, square, columns, columns, columns)
    in_vmem = pl.BlockSpec(memory_space=pltpu.VMEM)
    squares = jax.ShapeDtypeStruct((2, 3, width, width), F32)
    kept = (block, block, squares, columns, columns, columns)
    found = pl.pallas_call(
        functools.partial(kernel, z, names),
        out_shape=tuple(pltpu.VMEM(x.shape, x.dtype) for x in kept),
        in_specs=[pl.BlockSpec(memory_space=pltpu.HBM)] * 12,
        out_specs=(in_vmem,) * 6,
        scratch_shapes=scratch,
        compiler_params=pltpu.CompilerParams(
            collective_id=0, has_side_effects=True, vmem_limit_bytes=60 * 1024 * 1024
        ),
    )(
        features,
        cotangent,
        train_mask,
        degree,
        jnp.transpose(neighbours, (0, 2, 1)),
        send_rows,
        w_left,
        w_right,
        w_res,
        attn_vec,
        bn_gain,
        bn_shift,
    )
    return pl.pallas_call(
        store_kernel,
        out_shape=results,
        in_specs=[anywhere] * 6,
        out_specs=(anywhere,) * 8,
        scratch_shapes=[pltpu.SemaphoreType.DMA((11,))],
        compiler_params=pltpu.CompilerParams(vmem_limit_bytes=1024 * 1024),
    )(*found)


def solution(mesh):
    return jax.shard_map(
        body,
        mesh=mesh,
        in_specs=(
            P(None, "nodes", None),
            P(None, "nodes", None),
            P(None, "nodes"),
            P(None, "nodes"),
            P(None, "nodes", None),
            P(None, "nodes"),
            P(),
            P(),
            P(),
            P(),
            P(),
            P(),
        ),
        out_specs=(
            P("section", "nodes", None),
            P("section", "nodes", None),
            P(),
            P(),
            P(),
            P(),
            P(),
            P(),
        ),
        check_vma=False,
    )
```

```python
import functools
import types

import jax
import jax.numpy as jnp
from jax import lax
from jax.experimental import pallas as pl
from jax.experimental.pallas import tpu as pltpu
from jax.sharding import PartitionSpec as P

HEADS = 4
MASKED_SCORE = -1e30
VARIANCE_EPS = 1e-05
F32 = jnp.float32
BF16 = jnp.bfloat16
MESH = pl.DeviceIdType.MESH
UNROLL = 16
BLOCK = 32
OUTER_FIRST = ()
LANES = 128
GROUP = 64
TILE = 8
CHUNK = 16

FEATURES, MIXED, SUMS, BACK_SUMS, BACK_ROWS = range(5)
EXCHANGES = 5
CORE, FIRST, SECOND, SECOND_BACK, FIRST_BACK, CORE_BACK = range(6)
STAGES = 6


def halves(values):
    high = values.astype(BF16)
    return high, (values - high.astype(F32)).astype(BF16)


def mm(lhs, rhs):
    return jnp.dot(lhs, rhs, preferred_element_type=F32)


def mm_nt(lhs, rhs):
    return lax.dot_general(lhs, rhs, (((1,), (1,)), ((), ())), preferred_element_type=F32)


def mm3(lhs, rhs, product=mm):
    return product(lhs[0], rhs[0]) + product(lhs[1], rhs[0]) + product(lhs[0], rhs[1])


def iota(shape, dim):
    return lax.broadcasted_iota(jnp.int32, shape, dim)


def sigmoid(u):
    return 0.5 * jnp.tanh(0.5 * u) + 0.5


def as_ones(condition):
    return jnp.where(condition, 1.0, 0.0).astype(BF16)


def sizes_of(sections, partitions, rows, width, slots, listed):
    z = types.SimpleNamespace()
    z.sections, z.partitions, z.outer = sections, partitions, partitions // 2
    z.rows, z.width, z.slots, z.listed = rows, width, slots, listed
    z.send = listed // partitions
    z.halo = partitions * TILE
    z.halo_pad = -(-z.halo // LANES) * LANES
    z.table = rows + z.halo_pad
    z.picked = rows + z.halo
    return z


def shares_of(rows, first, second):
    share = rows // first
    piece = max(TILE, share // second)
    return share, piece, share // piece


def scratch_of(z):
    R, D, K, T = z.rows, z.width, z.slots, z.table
    S, O = z.sections, z.outer
    vmem = {
        "features_in": ((R, D), F32),
        "cotangent_in": ((R, D), F32),
        "mask_in": (None, jnp.int32),
        "degree_in": (None, jnp.int32),
        "slots_in": ((K, R), jnp.int32),
        "listed_in": (None, jnp.int32),
        "weights_in": ((3, 2, D, D), F32),
        "vector_in": ((2, D), F32),
        "gain_in": ((2, D), F32),
        "shift_in": ((2, D), F32),
        "weights_hi": ((2, 3, D, D), BF16),
        "weights_lo": ((2, 3, D, D), BF16),
        "prep": ((LANES, R), F32),
        "prep_t": ((R, LANES), F32),
        "listed_row": ((TILE, max(LANES, z.listed)), F32),
        "pick": ((K - 1, R, R + 2 * z.halo_pad), BF16),
        "pick_t": ((z.picked, (K - 1) * R), BF16),
        "list": ((z.halo, R), BF16),
        "list_t": ((R, z.halo_pad), BF16),
        "ones": ((2 * D, D), BF16),
        "h": ((T, D), F32),
        "h_hi": ((T, D), BF16),
        "h_lo": ((T, D), BF16),
        "ht_hi": ((2, D, T), BF16),
        "ht_lo": ((2, D, T), BF16),
        "table_hi": ((R, D), BF16),
        "table_lo": ((R, D), BF16),
        "halo_table": ((2 * z.halo_pad, D), BF16),
        "taken": ((2, K, R, D), F32),
        "act": ((2, K, R, D), F32),
        "rise": ((2, K, R, D), F32),
        "alpha": ((2, K, R, D), F32),
        "joined": ((2, R, D), F32),
        "right": ((2, R, D), F32),
        "skip": ((R, D), F32),
        "mixed": ((R, D), F32),
        "normed": ((2, R, D), F32),
        "slope": ((2, R, D), F32),
        "halo_normed": ((z.halo, D), F32),
        "halo_slope": ((z.halo, D), F32),
        "pair": ((K, R, 2 * D), BF16),
        "score": ((K, R, D), F32),
        "dpre": ((R, D), F32),
        "dmixed": ((R, D), F32),
        "dm_hi": ((R, D), BF16),
        "dm_lo": ((R, D), BF16),
        "dr_hi": ((R, D), BF16),
        "dr_lo": ((R, D), BF16),
        "dl_hi": ((T, D), BF16),
        "dl_lo": ((T, D), BF16),
        "dleft_self": ((R, D), F32),
        "dleft_hi": (((K - 1) * R, D), BF16),
        "dleft_lo": (((K - 1) * R, D), BF16),
        "dh": ((R, D), F32),
        "outgoing": ((EXCHANGES, z.halo, D), F32),
        "incoming": ((EXCHANGES, z.halo, D), F32),
        "small": ((4, TILE, D), F32),
        "small_core": ((2, TILE, D), F32),
        "small_outer": ((O, TILE, D), F32),
        "small_section": ((S, TILE, D), F32),
        "returning": ((z.halo, LANES), F32),
        "returned": ((z.halo, LANES), F32),
        "sums": ((2, 3, R, D), F32),
        "from_core": ((2, 3, R, D), F32),
    }
    for layer in range(2):
        for mat in range(3):
            first, second = (O, S) if (layer, mat) in OUTER_FIRST else (S, O)
            share, piece, _ = shares_of(R, first, second)
            vmem[f"first_{layer}{mat}"] = ((first - 1, share, D), F32)
            vmem[f"second_{layer}{mat}"] = ((second, piece, D), F32)
    return vmem


SEMAPHORES = {
    "load": (12,),
    "give": (EXCHANGES,),
    "take": (EXCHANGES,),
    "give_small": (4,),
    "take_small": (4,),
    "give_rows": (1,),
    "take_rows": (1,),
    "give_stage": (2, 3, STAGES),
    "take_stage": (2, 3, STAGES),
}


def kernel(z, names, *refs):
    features, cotangent, train_mask, degree, neighbours, send_rows = refs[:6]
    w_left, w_right, w_res, attn_vec, bn_gain, bn_shift = refs[6:12]
    out, grad_in, grads, g_vec, g_gain, g_shift = refs[12:18]
    v = types.SimpleNamespace(**dict(zip(names, refs[18:])))
    R, D, K, T = z.rows, z.width, z.slots, z.table
    S, N, O = z.sections, z.partitions, z.outer
    total_rows = R * N
    sec = lax.axis_index("section")
    me = lax.axis_index("nodes")
    core = lax.rem(me, 2)
    outer = lax.div(me, 2)
    mate = me + 1 - 2 * core

    barrier = pltpu.get_barrier_semaphore()

    def greet(step, carry):
        pl.semaphore_signal(
            barrier, inc=1, device_id={"nodes": lax.rem(me + step, N)}, device_id_type=MESH
        )
        return carry

    lax.fori_loop(1, N, greet, 0)
    for step in range(1, S):
        pl.semaphore_signal(
            barrier, inc=1, device_id={"section": lax.rem(sec + step, S)}, device_id_type=MESH
        )

    loads = []
    for source, target in (
        (features.at[sec], v.features_in),
        (send_rows, v.listed_in),
        (w_left, v.weights_in.at[0]),
        (w_right, v.weights_in.at[1]),
        (w_res, v.weights_in.at[2]),
        (neighbours.at[sec], v.slots_in),
        (degree, v.degree_in),
        (train_mask, v.mask_in),
        (attn_vec, v.vector_in),
        (bn_gain, v.gain_in),
        (bn_shift, v.shift_in),
        (cotangent.at[sec], v.cotangent_in),
    ):
        copy = pltpu.make_async_copy(source, target, v.load.at[len(loads)])
        copy.start()
        loads.append(copy)

    def rows_loop(body, start):
        return lax.fori_loop(0, R // CHUNK, body, start, unroll=UNROLL)

    def chunk(i):
        return pl.ds(pl.multiple_of(i * CHUNK, CHUNK), CHUNK)

    def fold(values):
        return jnp.sum(values.reshape(values.shape[0] // TILE, TILE, values.shape[1]), axis=0)

    def add_rows(values):
        return jnp.sum(values, axis=0, keepdims=True)


    def start_exchange(which, one_tile=False):
        def send(step, carry):
            other = lax.rem(me + step, N)
            place = 0 if one_tile else pl.multiple_of(other * TILE, TILE)
            pltpu.make_async_remote_copy(
                src_ref=v.outgoing.at[which, pl.ds(place, TILE)],
                dst_ref=v.incoming.at[which, pl.ds(pl.multiple_of(me * TILE, TILE), TILE)],
                send_sem=v.give.at[which],
                recv_sem=v.take.at[which],
                device_id={"nodes": other},
                device_id_type=MESH,
            ).start()
            return carry

        lax.fori_loop(1, N, send, 0)
        own = pl.ds(pl.multiple_of(me * TILE, TILE), TILE)
        mine = pl.ds(0, TILE) if one_tile else own
        v.incoming[which, own, :] = v.outgoing[which, mine, :]

    def wait_bytes(ref, semaphore):
        pltpu.make_async_copy(ref, ref, semaphore).wait()

    def end_exchange(which):
        wait_exchange(which)

    def wait_exchange(which):
        wait_bytes(v.incoming.at[which, pl.ds(0, (N - 1) * TILE)], v.take.at[which])

    def row_in_tile(rows):
        return lax.rem(iota((rows, D), 0), TILE)

    def with_sums(values, first, second):
        row = row_in_tile(values.shape[0])
        return values + jnp.where(row == z.send, first, 0.0) + jnp.where(row == z.send + 1, second, 0.0)

    def arrived_sums(which):
        tile = jnp.sum(v.incoming[which].reshape(N, TILE, D), axis=0)
        return tile[z.send : z.send + 1, :], tile[z.send + 1 : z.send + 2, :]

    def arrived_rows(which):
        values = v.incoming[which]
        return jnp.where(row_in_tile(z.halo) < z.send, values, 0.0)

    def give_rows_back(which):
        high, low = halves(arrived_rows(which))
        listed = v.list_t[:, : z.halo]
        return mm(listed, high) + mm(listed, low)

    def owner(layer):
        return 1 - layer

    sends_to_end = []

    def on(which, body):
        pl.when(core == which)(body)

    def stage_copy(layer, first, stage, source, target, device):
        pltpu.make_async_remote_copy(
            src_ref=source,
            dst_ref=target,
            send_sem=v.give_stage.at[layer, first, stage],
            recv_sem=v.take_stage.at[layer, first, stage],
            device_id=device,
            device_id_type=MESH,
        ).start()

    def stage_sent(layer, first, stage, ref, which):
        sends_to_end.append((ref, lambda: v.give_stage.at[layer, first, stage], which))

    def lane_of(layer, mat):
        lane = types.SimpleNamespace()
        over_section = (S, sec, lambda which: {"section": which})
        over_outer = (O, outer, lambda which: {"nodes": which * 2 + core})
        axes = (over_outer, over_section) if (layer, mat) in OUTER_FIRST else (over_section, over_outer)
        (lane.first, lane.first_me, lane.first_device), (lane.second, lane.second_me, lane.second_device) = axes
        lane.share, lane.piece, lane.owners = shares_of(R, lane.first, lane.second)
        lane.sums = v.sums.at[layer, mat]
        lane.result = grads.at[layer, mat]
        lane.from_first = getattr(v, f"first_{layer}{mat}")
        lane.from_second = getattr(v, f"second_{layer}{mat}")
        lane.share_rows = lambda which: pl.ds(pl.multiple_of(which * lane.share, TILE), lane.share)
        lane.piece_rows = lambda which: pl.ds(
            pl.multiple_of(lane.first_me * lane.share + which * lane.piece, TILE), lane.piece
        )
        return lane

    def start_core(layer, mat):
        on(
            1 - owner(layer),
            lambda: stage_copy(
                layer, mat, CORE, v.sums.at[layer, mat], v.from_core.at[layer, mat], {"nodes": mate}
            ),
        )
        stage_sent(layer, mat, CORE, lambda: v.from_core.at[layer, mat], 1 - owner(layer))

    def start_stage(stage, layer, mat):
        lane = lane_of(layer, mat)
        copy = functools.partial(stage_copy, layer, mat, stage)

        def sent(ref):
            stage_sent(layer, mat, stage, ref, owner(layer))

        if stage == FIRST:
            for step in range(1, lane.first):
                other = lax.rem(lane.first_me + step, lane.first)
                copy(
                    lane.sums.at[lane.share_rows(other)],
                    lane.from_first.at[step - 1],
                    lane.first_device(other),
                )
            sent(lambda: lane_of(layer, mat).from_first)
        elif stage == SECOND:
            if lane.owners == lane.second:
                for step in range(1, lane.second):
                    other = lax.rem(lane.second_me + step, lane.second)
                    copy(
                        lane.sums.at[lane.piece_rows(other)],
                        lane.from_second.at[step],
                        lane.second_device(other),
                    )
                sent(lambda: lane_of(layer, mat).from_second.at[pl.ds(1, lane.second - 1)])
            else:
                for other in range(lane.owners):

                    @pl.when(lane.second_me != other)
                    def _():
                        copy(
                            lane.sums.at[lane.piece_rows(other)],
                            lane.from_second.at[
                                lax.rem(lane.second_me - other + lane.second, lane.second)
                            ],
                            lane.second_device(other),
                        )
                        wait_bytes(lane.from_second.at[0], v.give_stage.at[layer, mat, stage])

        elif stage == SECOND_BACK:

            def send_all():
                rows = lane.piece_rows(lane.second_me)
                for step in range(1, lane.second):
                    copy(
                        lane.result.at[rows],
                        lane.result.at[rows],
                        lane.second_device(lax.rem(lane.second_me + step, lane.second)),
                    )

            if lane.owners == lane.second:
                send_all()
                sent(lambda: lane_of(layer, mat).from_second.at[pl.ds(1, lane.second - 1)])
            else:

                @pl.when(lane.second_me < lane.owners)
                def _():
                    send_all()
                    wait_bytes(
                        lane.from_second.at[pl.ds(1, lane.second - 1)],
                        v.give_stage.at[layer, mat, stage],
                    )

        elif stage == FIRST_BACK:
            rows = lane.share_rows(lane.first_me)
            for step in range(1, lane.first):
                copy(
                    lane.result.at[rows],
                    lane.result.at[rows],
                    lane.first_device(lax.rem(lane.first_me + step, lane.first)),
                )
            sent(lambda: lane_of(layer, mat).from_first)
        elif stage == CORE_BACK:
            copy(lane.result, lane.result, {"nodes": mate})
            sent(lambda: grads.at[layer, mat])

    def end_stage(stage, layer, mat):
        lane = lane_of(layer, mat)
        taken = v.take_stage.at[layer, mat, stage]
        if stage == CORE:
            wait_bytes(v.from_core.at[layer, mat], taken)
            v.sums[layer, mat] = v.sums[layer, mat] + v.from_core[layer, mat]
        elif stage == FIRST:
            wait_bytes(lane.from_first, taken)
            rows = lane.share_rows(lane.first_me)
            value = v.sums[layer, mat, rows, :]
            for step in range(lane.first - 1):
                value = value + lane.from_first[step]
            v.sums[layer, mat, rows, :] = value
        elif stage == SECOND:

            def add():
                wait_bytes(lane.from_second.at[pl.ds(1, lane.second - 1)], taken)
                rows = lane.piece_rows(lane.second_me)
                value = v.sums[layer, mat, rows, :]
                for step in range(1, lane.second):
                    value = value + lane.from_second[step]
                grads[layer, mat, rows, :] = value

            if lane.owners == lane.second:
                add()
            else:
                pl.when(lane.second_me < lane.owners)(add)
        elif stage == SECOND_BACK:
            if lane.owners == lane.second:
                wait_bytes(lane.from_second.at[pl.ds(1, lane.second - 1)], taken)
            else:
                if lane.owners > 1:
                    wait_bytes(lane.from_second.at[pl.ds(1, lane.owners - 1)], taken)

                @pl.when(lane.second_me >= lane.owners)
                def _():
                    wait_bytes(lane.from_second.at[0], taken)

        elif stage == FIRST_BACK:
            wait_bytes(lane.from_first, taken)
        elif stage == CORE_BACK:
            wait_bytes(grads.at[layer, mat], taken)

    def advance(layer, *moves):
        def run():
            for stage, mat in moves:
                end_stage(stage, layer, mat)
                start_stage(stage + 1, layer, mat)

        on(owner(layer), run)


    loads[1].wait()
    v.listed_row[...] = jnp.zeros_like(v.listed_row)
    v.listed_row[0:1, : z.listed] = v.listed_in[pl.ds(sec, 1), :].astype(F32)
    spread_from = iota((v.listed_row.shape[1], z.halo_pad), 0)
    spread_to = iota((v.listed_row.shape[1], z.halo_pad), 1)
    spread = as_ones(
        (lax.div(spread_from, z.send) == lax.div(spread_to, TILE))
        & (lax.rem(spread_from, z.send) == lax.rem(spread_to, TILE))
        & (spread_from < z.listed)
    )
    listed = mm(v.listed_row[...].astype(BF16), spread)[0:1, :]
    place = iota((1, z.halo_pad), 1)
    real = (lax.rem(place, TILE) < z.send) & (place < z.halo)
    listed = jnp.where(real, listed, -1.0)
    list_t = jnp.where(iota((R, z.halo_pad), 0).astype(F32) == listed, 1.0, 0.0)
    v.list_t[...] = list_t.astype(BF16)
    v.list[...] = list_t.T[: z.halo, :].astype(BF16)

    loads[0].wait()
    own = v.features_in[...]
    v.h[pl.ds(0, R), :] = own
    high, low = halves(own)
    v.h_hi[pl.ds(0, R), :] = high
    v.h_lo[pl.ds(0, R), :] = low
    v.outgoing[FEATURES] = mm(v.list[...], high) + mm(v.list[...], low)
    pl.semaphore_wait(barrier, N - 1 + S - 1)
    start_exchange(FEATURES)

    for load in loads[2:5]:
        load.wait()
    for layer in range(2):
        for mat in range(3):
            high, low = halves(v.weights_in[mat, layer])
            v.weights_hi[layer, mat] = high
            v.weights_lo[layer, mat] = low

    def weight(layer, mat):
        return v.weights_hi[layer, mat], v.weights_lo[layer, mat]

    for load in loads[5:11]:
        load.wait()
    named = v.slots_in[...]
    offset = named - R
    remote = R + lax.div(offset, z.send) * TILE + lax.rem(offset, z.send)
    named = jnp.where(named < R, named, remote).astype(F32)
    v.prep[...] = jnp.zeros_like(v.prep)
    v.prep[pl.ds(0, K), :] = named
    v.prep[pl.ds(K, 1), :] = v.degree_in[pl.ds(sec, 1), :].astype(F32)
    v.prep[pl.ds(K + 1, 1), :] = v.mask_in[pl.ds(sec, 1), :].astype(F32)
    v.prep_t[...] = v.prep[...].T
    for slot in range(1, K):
        column = v.prep_t[:, slot : slot + 1]
        pick = as_ones(iota((R, T), 1).astype(F32) == column)
        v.pick[slot - 1, :, pl.ds(0, T)] = pick
        v.pick[slot - 1, :, pl.ds(T, z.halo_pad)] = pick[:, R:]
        row = v.prep[slot : slot + 1, :]
        v.pick_t[:, (slot - 1) * R : slot * R] = as_ones(iota((z.picked, R), 0).astype(F32) == row)
    block_row = lax.div(lax.rem(iota((2 * D, D), 0), D), GROUP)
    v.ones[...] = as_ones(block_row == lax.div(iota((2 * D, D), 1), GROUP))

    def project(layer):
        rows = pl.ds(0, R)
        own = (v.h_hi[rows, :], v.h_lo[rows, :])
        left = mm3(own, weight(layer, 0))
        v.taken[layer, 0] = left
        high, low = halves(left)
        v.table_hi[rows, :] = high
        v.table_lo[rows, :] = low
        v.right[layer] = mm3(own, weight(layer, 1))
        v.skip[...] = mm3(own, weight(layer, 2))

    def project_halo(layer):
        rows = pl.ds(R, z.halo_pad)
        left = mm3((v.h_hi[rows, :], v.h_lo[rows, :]), weight(layer, 0))
        high, low = halves(left)
        v.halo_table[pl.ds(0, z.halo_pad), :] = high
        v.halo_table[pl.ds(z.halo_pad, z.halo_pad), :] = low

    def store_halo(values):
        if z.halo < z.halo_pad:
            rest = pl.ds(R + z.halo, z.halo_pad - z.halo)
            v.h[rest, :] = jnp.zeros((z.halo_pad - z.halo, D), F32)
            v.h_hi[rest, :] = jnp.zeros((z.halo_pad - z.halo, D), BF16)
            v.h_lo[rest, :] = jnp.zeros((z.halo_pad - z.halo, D), BF16)
        rows = pl.ds(R, z.halo)
        v.h[rows, :] = values
        high, low = halves(values)
        v.h_hi[rows, :] = high
        v.h_lo[rows, :] = low

    def keep_transposed(layer):
        high, low = halves(v.h[...].T)
        v.ht_hi[layer] = high
        v.ht_lo[layer] = low

    def store_pair(slot, rows, values):
        high, low = halves(values)
        v.pair[slot, rows, pl.ds(0, D)] = high
        v.pair[slot, rows, pl.ds(D, D)] = low

    def gather_own(layer):
        def one(slot, carry):
            pick = v.pick[slot - 1, :, pl.ds(0, R)]
            v.taken[layer, slot] = mm(pick, v.table_hi[...]) + mm(pick, v.table_lo[...])
            return carry

        lax.fori_loop(1, K, one, 0, unroll=True)

    def head_sum(slot):
        v.score[slot] = mm(v.pair[slot], v.ones[...])

    def attend(layer):
        vector = v.vector_in[layer : layer + 1, :]

        def gather(slot):
            pick = v.pick[slot - 1, :, pl.ds(R, 2 * z.halo_pad)]
            value = mm(pick, v.halo_table[...])
            if layer == 0:
                value = v.taken[layer, slot] + value
            else:
                pick = v.pick[slot - 1, :, pl.ds(0, R)]
                value = mm(pick, v.table_hi[...]) + mm(pick, v.table_lo[...]) + value
            v.taken[layer, slot] = value

        def activate(slot):
            for place in range(0, R, BLOCK):
                rows = pl.ds(place, BLOCK)
                u = v.taken[layer, slot, rows, :] + v.right[layer, rows, :]
                store_pair(slot, rows, u * sigmoid(u) * vector)

        for slot in range(1, K + 3):
            if slot < K:
                gather(slot)
            if slot <= K:
                activate(slot - 1)
            if slot >= 3:
                head_sum(slot - 3)

        def mix(i, carry):
            rows = chunk(i)
            count = jnp.broadcast_to(v.prep_t[rows, K : K + 1], (CHUNK, D))
            scores = [
                jnp.where(count > slot, v.score[slot, rows, :], MASKED_SCORE) for slot in range(K)
            ]
            highest = functools.reduce(jnp.maximum, scores)
            powers = [jnp.exp(score - highest) for score in scores]
            scale = 1.0 / functools.reduce(jnp.add, powers)
            joined = jnp.zeros((CHUNK, D), F32)
            for slot in range(K):
                alpha = powers[slot] * scale
                v.alpha[layer, slot, rows, :] = alpha
                joined = joined + alpha * v.taken[layer, slot, rows, :]
            v.joined[layer, rows, :] = joined
            mixed = joined + v.skip[rows, :]
            v.mixed[rows, :] = mixed
            return carry[0] + fold(mixed), carry[1] + fold(mixed * mixed)

        nothing = jnp.zeros((TILE, D), F32)
        first, second = rows_loop(mix, (nothing, nothing))
        return add_rows(first), add_rows(second)

    def derive(layer):
        vector = v.vector_in[layer : layer + 1, :]

        def one(i, carry):
            rows = chunk(i)
            right = v.right[layer, rows, :]
            for slot in range(K):
                u = v.taken[layer, slot, rows, :] + right
                sig = sigmoid(u)
                act = u * sig
                v.act[layer, slot, rows, :] = act
                v.rise[layer, slot, rows, :] = vector * (sig + act * (1.0 - sig))
            return carry

        rows_loop(one, 0)

    def moments(which):
        first, second = arrived_sums(which)
        mean = first / total_rows
        return mean, lax.rsqrt(second / total_rows - mean * mean + VARIANCE_EPS)

    def activation(layer, mixed, mean, inverse):
        normed = (mixed - mean) * inverse
        pre = v.gain_in[layer : layer + 1, :] * normed + v.shift_in[layer : layer + 1, :]
        power = jnp.exp(jnp.minimum(pre, 0.0))
        return normed, jnp.where(pre > 0, 1.0, power), jnp.where(pre > 0, pre, power - 1.0)

    def sums_tile(which, first, second):
        v.outgoing[which, pl.ds(0, TILE), :] = with_sums(jnp.zeros((TILE, D), F32), first, second)

    def list_rows(values):
        high, low = halves(values)
        return mm(v.list[...], high) + mm(v.list[...], low)

    project(0)
    gather_own(0)
    end_exchange(FEATURES)
    store_halo(arrived_rows(FEATURES))
    project_halo(0)
    first, second = attend(0)
    v.outgoing[MIXED] = with_sums(list_rows(v.mixed[...]), first, second)
    start_exchange(MIXED)
    keep_transposed(0)
    derive(0)
    end_exchange(MIXED)
    mean0, inverse0 = moments(MIXED)

    def finish0(i, carry):
        rows = chunk(i)
        normed, slope, hidden = activation(0, v.mixed[rows, :], mean0, inverse0)
        v.normed[0, rows, :] = normed
        v.slope[0, rows, :] = slope
        v.h[rows, :] = hidden
        high, low = halves(hidden)
        v.h_hi[rows, :] = high
        v.h_lo[rows, :] = low
        return carry

    rows_loop(finish0, 0)
    normed, slope, hidden = activation(0, arrived_rows(MIXED), mean0, inverse0)
    v.halo_normed[...] = normed
    v.halo_slope[...] = slope
    store_halo(jnp.where(row_in_tile(z.halo) < z.send, hidden, 0.0))

    project(1)
    project_halo(1)
    first, second = attend(1)
    sums_tile(SUMS, first, second)
    start_exchange(SUMS, True)
    keep_transposed(1)
    derive(1)
    loads[11].wait()
    end_exchange(SUMS)
    mean1, inverse1 = moments(SUMS)

    def finish1(i, carry):
        rows = chunk(i)
        normed, slope, hidden = activation(1, v.mixed[rows, :], mean1, inverse1)
        v.normed[1, rows, :] = normed
        out[0, rows, :] = hidden
        dpre = v.cotangent_in[rows, :] * v.prep_t[rows, K + 1 : K + 2] * slope
        v.dpre[rows, :] = dpre
        return carry[0] + fold(dpre), carry[1] + fold(dpre * normed)

    nothing = jnp.zeros((TILE, D), F32)
    first, second = rows_loop(finish1, (nothing, nothing))
    shift1, gain1 = add_rows(first), add_rows(second)
    sums_tile(BACK_SUMS, shift1, gain1)
    start_exchange(BACK_SUMS, True)

    def normalization_back(layer, which, inverse):
        first, second = arrived_sums(which)
        first = first / total_rows
        second = second / total_rows
        scale = inverse * v.gain_in[layer : layer + 1, :]

        def one(i, carry):
            rows = chunk(i)
            dmixed = scale * (v.dpre[rows, :] - first - v.normed[layer, rows, :] * second)
            v.dmixed[rows, :] = dmixed
            high, low = halves(dmixed)
            v.dm_hi[rows, :] = high
            v.dm_lo[rows, :] = low
            return carry

        rows_loop(one, 0)

    def attend_back(layer, between=None):
        def differences(slot):
            for place in range(0, R, BLOCK):
                rows = pl.ds(place, BLOCK)
                value = (v.taken[layer, slot, rows, :] - v.joined[layer, rows, :]) * v.dmixed[rows, :]
                store_pair(slot, rows, value)

        for slot in range(K + 1):
            if slot < K:
                differences(slot)
            if slot >= 1:
                head_sum(slot - 1)

        def one(i, carry):
            rows = chunk(i)
            dmixed = v.dmixed[rows, :]
            dright = jnp.zeros((CHUNK, D), F32)
            for slot in range(K):
                alpha = v.alpha[layer, slot, rows, :]
                dscore = alpha * v.score[slot, rows, :]
                carry = carry + fold(dscore * v.act[layer, slot, rows, :])
                du = dscore * v.rise[layer, slot, rows, :]
                dright = dright + du
                dleft = du + alpha * dmixed
                if slot == 0:
                    v.dleft_self[rows, :] = dleft
                else:
                    high, low = halves(dleft)
                    place = pl.ds(pl.multiple_of((slot - 1) * R + i * CHUNK, CHUNK), CHUNK)
                    v.dleft_hi[place, :] = high
                    v.dleft_lo[place, :] = low
            high, low = halves(dright)
            v.dr_hi[rows, :] = high
            v.dr_lo[rows, :] = low
            return carry

        vector_sum = rows_loop(one, jnp.zeros((TILE, D), F32))
        if between is not None:
            between()

        def scattered(rows):
            pick = v.pick_t[rows, :]
            return mm(pick, v.dleft_hi[...]) + mm(pick, v.dleft_lo[...])

        rows = pl.ds(0, R)
        own = scattered(rows) + v.dleft_self[...]
        v.dleft_self[...] = own
        high, low = halves(own)
        v.dl_hi[rows, :] = high
        v.dl_lo[rows, :] = low
        rows = pl.ds(R, z.halo)
        halo = scattered(rows)
        if layer == 0:
            start_return(halo)
        high, low = halves(halo)
        v.dl_hi[rows, :] = high
        v.dl_lo[rows, :] = low
        return add_rows(vector_sum)

    def start_return(halo):
        v.returning[...] = halo[:, :LANES] + pltpu.roll(halo[:, LANES:], z.send, 0)
        own = pl.ds(pl.multiple_of(me * TILE, TILE), TILE)

        def send(step, carry):
            other = lax.rem(me + step, N)
            pltpu.make_async_remote_copy(
                src_ref=v.returning.at[pl.ds(pl.multiple_of(other * TILE, TILE), TILE)],
                dst_ref=v.returned.at[own],
                send_sem=v.give_rows.at[0],
                recv_sem=v.take_rows.at[0],
                device_id={"nodes": other},
                device_id_type=MESH,
            ).start()
            return carry

        lax.fori_loop(1, N, send, 0)
        v.returned[own, :] = v.returning[own, :]

    def dleft(rows):
        return v.dl_hi[rows, :], v.dl_lo[rows, :]

    def input_back(layer):
        own = pl.ds(0, R)
        v.dh[...] = (
            mm3(dleft(own), weight(layer, 0), mm_nt)
            + mm3((v.dr_hi[...], v.dr_lo[...]), weight(layer, 1), mm_nt)
            + mm3((v.dm_hi[...], v.dm_lo[...]), weight(layer, 2), mm_nt)
        )
        return mm3(dleft(pl.ds(R, z.halo)), weight(layer, 0), mm_nt)

    def weight_grad(layer, mat):
        if mat == 0:
            upstream = (v.dl_hi[...], v.dl_lo[...])
            inputs = (v.ht_hi[layer], v.ht_lo[layer])
        else:
            upstream = (v.dr_hi[...], v.dr_lo[...]) if mat == 1 else (v.dm_hi[...], v.dm_lo[...])
            inputs = (v.ht_hi[layer, :, pl.ds(0, R)], v.ht_lo[layer, :, pl.ds(0, R)])
        v.sums[layer, mat] = mm3(inputs, upstream)
        start_core(layer, mat)

    if z.halo < z.halo_pad:
        rest = pl.ds(R + z.halo, z.halo_pad - z.halo)
        v.dl_hi[rest, :] = jnp.zeros((z.halo_pad - z.halo, D), BF16)
        v.dl_lo[rest, :] = jnp.zeros((z.halo_pad - z.halo, D), BF16)

    end_exchange(BACK_SUMS)
    normalization_back(1, BACK_SUMS, inverse1)
    vector1 = attend_back(1)
    halo_back = input_back(1)
    dpre = v.dh[...] * v.slope[0]
    halo_dpre = halo_back * v.halo_slope[...]
    shift0 = add_rows(dpre) + add_rows(halo_dpre)
    gain0 = add_rows(dpre * v.normed[0]) + add_rows(halo_dpre * v.halo_normed[...])
    v.outgoing[BACK_ROWS] = with_sums(halo_back, shift0, gain0)
    start_exchange(BACK_ROWS)
    for mat in (2, 1, 0):
        weight_grad(1, mat)
    advance(1, (CORE, 2), (CORE, 1), (CORE, 0))
    end_exchange(BACK_ROWS)
    v.dpre[...] = (v.dh[...] + give_rows_back(BACK_ROWS)) * v.slope[0]

    normalization_back(0, BACK_ROWS, inverse0)
    weight_grad(0, 2)

    def between():
        weight_grad(0, 1)
        advance(1, (FIRST, 2))
        advance(0, (CORE, 2))

    vector0 = attend_back(0, between)
    weight_grad(0, 0)

    row = iota((TILE, D), 0)
    tile = jnp.zeros((TILE, D), F32)
    for place, value in enumerate((vector0, vector1, gain0, gain1, shift0, shift1)):
        tile = jnp.where(row == place, value, tile)
    v.small[0] = tile

    def send_small(stage, source, target, device):
        pltpu.make_async_remote_copy(
            src_ref=source,
            dst_ref=target,
            send_sem=v.give_small.at[stage],
            recv_sem=v.take_small.at[stage],
            device_id=device,
            device_id_type=MESH,
        ).start()

    on(0, lambda: send_small(0, v.small.at[0], v.small_core.at[0], {"nodes": mate}))

    def small_outer():
        wait_bytes(v.small_core.at[0], v.take_small.at[0])
        value = v.small[0] + v.small_core[0]
        v.small[1] = value
        v.small_outer[outer] = value
        for step in range(1, O):
            send_small(
                1, v.small.at[1], v.small_outer.at[outer], {"nodes": lax.rem(outer + step, O) * 2 + core}
            )

    def small_section():
        wait_bytes(v.small_outer.at[pl.ds(1, O - 1)], v.take_small.at[1])
        value = jnp.sum(v.small_outer[...], axis=0)
        v.small[2] = value
        v.small_section[sec] = value
        for step in range(1, S):
            send_small(
                2, v.small.at[2], v.small_section.at[sec], {"section": lax.rem(sec + step, S)}
            )

    def put_small(value):
        g_vec[...] = value[0:2, :]
        g_gain[...] = value[2:4, :]
        g_shift[...] = value[4:6, :]

    def small_back():
        wait_bytes(v.small_section.at[pl.ds(1, S - 1)], v.take_small.at[2])
        value = jnp.sum(v.small_section[...], axis=0)
        v.small[3] = value
        send_small(3, v.small.at[3], v.small_core.at[1], {"nodes": mate})
        put_small(value)

    def small_end():
        wait_bytes(v.small_core.at[1], v.take_small.at[3])
        put_small(v.small_core[1])

    advance(1, (FIRST, 1))
    advance(0, (CORE, 1))
    def part_input():
        v.dh[...] = mm3((v.dr_hi[...], v.dr_lo[...]), weight(0, 1), mm_nt) + mm3(
            (v.dm_hi[...], v.dm_lo[...]), weight(0, 2), mm_nt
        )

    def store_input():
        wait_bytes(v.returned.at[pl.ds(0, (N - 1) * TILE)], v.take_rows.at[0])
        values = v.returned[...]
        values = jnp.concatenate([values, pltpu.roll(values, z.halo - z.send, 0)], axis=1)
        high, low = halves(jnp.where(row_in_tile(z.halo) < z.send, values, 0.0))
        listed = v.list_t[:, : z.halo]
        left = v.dleft_self[...] + (mm(listed, high) + mm(listed, low))
        grad_in[0] = v.dh[...] + mm3(halves(left), weight(0, 0), mm_nt)

    tails = {
        1: (
            (FIRST, 0),
            (SECOND, 2),
            part_input,
            (SECOND, 1),
            (SECOND, 0),
            store_input,
            (SECOND_BACK, 2),
            (SECOND_BACK, 1),
            (SECOND_BACK, 0),
            (FIRST_BACK, 2),
            (FIRST_BACK, 1),
            (FIRST_BACK, 0),
            small_end,
        ),
        0: (
            (CORE, 0),
            (FIRST, 2),
            small_outer,
            (FIRST, 1),
            (FIRST, 0),
            part_input,
            (SECOND, 2),
            (SECOND, 1),
            (SECOND, 0),
            store_input,
            small_section,
            (SECOND_BACK, 2),
            (SECOND_BACK, 1),
            (SECOND_BACK, 0),
            small_back,
            (FIRST_BACK, 2),
            (FIRST_BACK, 1),
            (FIRST_BACK, 0),
        ),
    }

    def finish(layer):
        for step in tails[layer]:
            if callable(step):
                step()
            else:
                end_stage(step[0], layer, step[1])
                start_stage(step[0] + 1, layer, step[1])

    on(owner(1), lambda: finish(1))
    on(owner(0), lambda: finish(0))

    def receive(layer):
        for mat in range(3):
            end_stage(CORE_BACK, layer, mat)

    on(0, lambda: receive(0))
    on(1, lambda: receive(1))
    for which in range(EXCHANGES):
        wait_bytes(v.outgoing.at[which, pl.ds(0, (N - 1) * TILE)], v.give.at[which])
    wait_bytes(v.returned.at[pl.ds(0, (N - 1) * TILE)], v.give_rows.at[0])

    def sent(which):
        for ref, semaphore, sender in sends_to_end:
            if sender == which:
                wait_bytes(ref(), semaphore())

    def sent_small(stage, count):
        wait_bytes(v.small_outer.at[pl.ds(0, count)], v.give_small.at[stage])

    def sent0():
        sent(0)
        sent_small(0, 1)

    def sent1():
        sent(1)
        sent_small(1, O - 1)
        wait_bytes(v.small_section.at[pl.ds(1, S - 1)], v.give_small.at[2])
        sent_small(3, 1)

    on(0, sent0)
    on(1, sent1)


def store_kernel(*refs):
    out, grad_in, grads, g_vec, g_gain, g_shift = refs[:6]
    pairs = [(out, refs[6]), (grad_in, refs[7])]
    for mat in range(3):
        pairs += [(grads.at[layer, mat], refs[8 + mat].at[layer]) for layer in range(2)]
    pairs += [(g_vec, refs[11]), (g_gain, refs[12]), (g_shift, refs[13])]
    copies = [pltpu.make_async_copy(*pair, refs[14].at[i]) for i, pair in enumerate(pairs)]
    for copy in copies:
        copy.start()
    for copy in copies:
        copy.wait()


def body(
    features,
    cotangent,
    train_mask,
    degree,
    neighbours,
    send_rows,
    w_left,
    w_right,
    w_res,
    attn_vec,
    bn_gain,
    bn_shift,
):
    batches, rows, width = features.shape
    sections = lax.axis_size("section")
    assert batches == sections and width == HEADS * GROUP
    z = sizes_of(
        sections, lax.axis_size("nodes"), rows, width, neighbours.shape[2], send_rows.shape[1]
    )
    shapes = scratch_of(z)
    shapes["mask_in"] = (train_mask.shape, jnp.int32)
    shapes["degree_in"] = (degree.shape, jnp.int32)
    shapes["listed_in"] = (send_rows.shape, jnp.int32)
    scratch = [pltpu.VMEM(shape, dtype) for shape, dtype in shapes.values()]
    scratch += [pltpu.SemaphoreType.DMA(shape) for shape in SEMAPHORES.values()]
    names = list(shapes) + list(SEMAPHORES)
    anywhere = pl.BlockSpec(memory_space=pl.ANY)
    square = jax.ShapeDtypeStruct((2, width, width), F32)
    columns = jax.ShapeDtypeStruct((2, width), F32)
    block = jax.ShapeDtypeStruct((1, rows, width), F32)
    results = (block, block, square, square, square, columns, columns, columns)
    in_vmem = pl.BlockSpec(memory_space=pltpu.VMEM)
    squares = jax.ShapeDtypeStruct((2, 3, width, width), F32)
    kept = (block, block, squares, columns, columns, columns)
    found = pl.pallas_call(
        functools.partial(kernel, z, names),
        out_shape=tuple(pltpu.VMEM(x.shape, x.dtype) for x in kept),
        in_specs=[pl.BlockSpec(memory_space=pltpu.HBM)] * 12,
        out_specs=(in_vmem,) * 6,
        scratch_shapes=scratch,
        compiler_params=pltpu.CompilerParams(
            collective_id=0, has_side_effects=True, vmem_limit_bytes=60 * 1024 * 1024
        ),
    )(
        features,
        cotangent,
        train_mask,
        degree,
        jnp.transpose(neighbours, (0, 2, 1)),
        send_rows,
        w_left,
        w_right,
        w_res,
        attn_vec,
        bn_gain,
        bn_shift,
    )
    return pl.pallas_call(
        store_kernel,
        out_shape=results,
        in_specs=[anywhere] * 6,
        out_specs=(anywhere,) * 8,
        scratch_shapes=[pltpu.SemaphoreType.DMA((11,))],
        compiler_params=pltpu.CompilerParams(vmem_limit_bytes=1024 * 1024),
    )(*found)


def solution(mesh):
    return jax.shard_map(
        body,
        mesh=mesh,
        in_specs=(
            P(None, "nodes", None),
            P(None, "nodes", None),
            P(None, "nodes"),
            P(None, "nodes"),
            P(None, "nodes", None),
            P(None, "nodes"),
            P(),
            P(),
            P(),
            P(),
            P(),
            P(),
        ),
        out_specs=(
            P("section", "nodes", None),
            P("section", "nodes", None),
            P(),
            P(),
            P(),
            P(),
            P(),
            P(),
        ),
        check_vma=False,
    )
```

```python
import functools
import types

import jax
import jax.numpy as jnp
from jax import lax
from jax.experimental import pallas as pl
from jax.experimental.pallas import tpu as pltpu
from jax.sharding import PartitionSpec as P

HEADS = 4
MASKED_SCORE = -1e30
VARIANCE_EPS = 1e-05
F32 = jnp.float32
BF16 = jnp.bfloat16
MESH = pl.DeviceIdType.MESH
UNROLL = 16
BLOCK = 32
OUTER_FIRST = ()
LANES = 128
GROUP = 64
TILE = 8
CHUNK = 16

FEATURES, MIXED, SUMS, BACK_SUMS, BACK_ROWS = range(5)
EXCHANGES = 5
CORE, FIRST, SECOND, SECOND_BACK, FIRST_BACK, CORE_BACK = range(6)
STAGES = 6
ON_CORE_0 = ((1, 2), (1, 1))
BETWEEN = ((FIRST, 1, 2), (FIRST, 1, 0), (CORE, 0, 2))
AFTER = ((FIRST, 1, 1), (CORE, 0, 1))
TAILS = (
    (
        (SECOND, 1, 2),
        (SECOND, 1, 1),
        (SECOND_BACK, 1, 2),
        (SECOND_BACK, 1, 1),
        (FIRST_BACK, 1, 2),
        (FIRST_BACK, 1, 1),
        "part",
        "input",
        "end",
    ),
    (
        (CORE, 0, 0),
        (SECOND, 1, 0),
        (FIRST, 0, 2),
        "outer",
        (FIRST, 0, 1),
        (FIRST, 0, 0),
        (SECOND_BACK, 1, 0),
        (SECOND, 0, 2),
        (SECOND, 0, 1),
        "section",
        (SECOND, 0, 0),
        (FIRST_BACK, 1, 0),
        (SECOND_BACK, 0, 2),
        (SECOND_BACK, 0, 1),
        "back",
        (SECOND_BACK, 0, 0),
        (FIRST_BACK, 0, 2),
        (FIRST_BACK, 0, 1),
        (FIRST_BACK, 0, 0),
        "part",
        "input",
    ),
)


def halves(values):
    high = values.astype(BF16)
    return high, (values - high.astype(F32)).astype(BF16)


def mm(lhs, rhs):
    return jnp.dot(lhs, rhs, preferred_element_type=F32)


def mm_nt(lhs, rhs):
    return lax.dot_general(lhs, rhs, (((1,), (1,)), ((), ())), preferred_element_type=F32)


def mm3(lhs, rhs, product=mm):
    return product(lhs[0], rhs[0]) + product(lhs[1], rhs[0]) + product(lhs[0], rhs[1])


def iota(shape, dim):
    return lax.broadcasted_iota(jnp.int32, shape, dim)


def sigmoid(u):
    return 0.5 * jnp.tanh(0.5 * u) + 0.5


def as_ones(condition):
    return jnp.where(condition, 1.0, 0.0).astype(BF16)


def sizes_of(sections, partitions, rows, width, slots, listed):
    z = types.SimpleNamespace()
    z.sections, z.partitions, z.outer = sections, partitions, partitions // 2
    z.rows, z.width, z.slots, z.listed = rows, width, slots, listed
    z.send = listed // partitions
    z.halo = partitions * TILE
    z.halo_pad = -(-z.halo // LANES) * LANES
    z.table = rows + z.halo_pad
    z.picked = rows + z.halo
    return z


def shares_of(rows, first, second):
    share = rows // first
    piece = max(TILE, share // second)
    return share, piece, share // piece


def scratch_of(z):
    R, D, K, T = z.rows, z.width, z.slots, z.table
    S, O = z.sections, z.outer
    vmem = {
        "features_in": ((R, D), F32),
        "cotangent_in": ((R, D), F32),
        "mask_in": (None, jnp.int32),
        "degree_in": (None, jnp.int32),
        "slots_in": ((K, R), jnp.int32),
        "listed_in": (None, jnp.int32),
        "weights_in": ((3, 2, D, D), F32),
        "vector_in": ((2, D), F32),
        "gain_in": ((2, D), F32),
        "shift_in": ((2, D), F32),
        "weights_hi": ((2, 3, D, D), BF16),
        "weights_lo": ((2, 3, D, D), BF16),
        "prep": ((LANES, R), F32),
        "prep_t": ((R, LANES), F32),
        "listed_row": ((TILE, max(LANES, z.listed)), F32),
        "pick": ((K - 1, R, R + 2 * z.halo_pad), BF16),
        "pick_t": ((z.picked, (K - 1) * R), BF16),
        "list": ((z.halo, R), BF16),
        "list_t": ((R, z.halo_pad), BF16),
        "ones": ((2 * D, D), BF16),
        "h": ((T, D), F32),
        "h_hi": ((T, D), BF16),
        "h_lo": ((T, D), BF16),
        "ht_hi": ((2, D, T), BF16),
        "ht_lo": ((2, D, T), BF16),
        "table_hi": ((R, D), BF16),
        "table_lo": ((R, D), BF16),
        "halo_table": ((2 * z.halo_pad, D), BF16),
        "taken": ((2, K, R, D), F32),
        "act": ((2, K, R, D), F32),
        "rise": ((2, K, R, D), F32),
        "alpha": ((2, K, R, D), F32),
        "joined": ((2, R, D), F32),
        "right": ((2, R, D), F32),
        "skip": ((R, D), F32),
        "mixed": ((R, D), F32),
        "normed": ((2, R, D), F32),
        "slope": ((2, R, D), F32),
        "halo_normed": ((z.halo, D), F32),
        "halo_slope": ((z.halo, D), F32),
        "pair": ((K, R, 2 * D), BF16),
        "score": ((K, R, D), F32),
        "dpre": ((R, D), F32),
        "dmixed": ((R, D), F32),
        "dm_hi": ((R, D), BF16),
        "dm_lo": ((R, D), BF16),
        "dr_hi": ((R, D), BF16),
        "dr_lo": ((R, D), BF16),
        "dl_hi": ((T, D), BF16),
        "dl_lo": ((T, D), BF16),
        "dleft_self": ((R, D), F32),
        "dleft_hi": (((K - 1) * R, D), BF16),
        "dleft_lo": (((K - 1) * R, D), BF16),
        "dh": ((R, D), F32),
        "outgoing": ((EXCHANGES, z.halo, D), F32),
        "incoming": ((EXCHANGES, z.halo, D), F32),
        "small": ((4, TILE, D), F32),
        "small_core": ((2, TILE, D), F32),
        "small_outer": ((O, TILE, D), F32),
        "small_section": ((S, TILE, D), F32),
        "returning": ((z.halo, LANES), F32),
        "returned": ((z.halo, LANES), F32),
        "sums": ((2, 3, R, D), F32),
        "from_core": ((2, 3, R, D), F32),
    }
    for layer in range(2):
        for mat in range(3):
            first, second = (O, S) if (layer, mat) in OUTER_FIRST else (S, O)
            share, piece, _ = shares_of(R, first, second)
            vmem[f"first_{layer}{mat}"] = ((first - 1, share, D), F32)
            vmem[f"second_{layer}{mat}"] = ((second, piece, D), F32)
    return vmem


SEMAPHORES = {
    "load": (12,),
    "give": (EXCHANGES,),
    "take": (EXCHANGES,),
    "give_small": (4,),
    "take_small": (4,),
    "give_rows": (1,),
    "take_rows": (1,),
    "give_stage": (2, 3, STAGES),
    "take_stage": (2, 3, STAGES),
}


def kernel(z, names, *refs):
    features, cotangent, train_mask, degree, neighbours, send_rows = refs[:6]
    w_left, w_right, w_res, attn_vec, bn_gain, bn_shift = refs[6:12]
    out, grad_in, grads, g_vec, g_gain, g_shift = refs[12:18]
    v = types.SimpleNamespace(**dict(zip(names, refs[18:])))
    R, D, K, T = z.rows, z.width, z.slots, z.table
    S, N, O = z.sections, z.partitions, z.outer
    total_rows = R * N
    sec = lax.axis_index("section")
    me = lax.axis_index("nodes")
    core = lax.rem(me, 2)
    outer = lax.div(me, 2)
    mate = me + 1 - 2 * core

    barrier = pltpu.get_barrier_semaphore()

    def greet(step, carry):
        pl.semaphore_signal(
            barrier, inc=1, device_id={"nodes": lax.rem(me + step, N)}, device_id_type=MESH
        )
        return carry

    lax.fori_loop(1, N, greet, 0)
    for step in range(1, S):
        pl.semaphore_signal(
            barrier, inc=1, device_id={"section": lax.rem(sec + step, S)}, device_id_type=MESH
        )

    loads = []
    for source, target in (
        (features.at[sec], v.features_in),
        (send_rows, v.listed_in),
        (w_left, v.weights_in.at[0]),
        (w_right, v.weights_in.at[1]),
        (w_res, v.weights_in.at[2]),
        (neighbours.at[sec], v.slots_in),
        (degree, v.degree_in),
        (train_mask, v.mask_in),
        (attn_vec, v.vector_in),
        (bn_gain, v.gain_in),
        (bn_shift, v.shift_in),
        (cotangent.at[sec], v.cotangent_in),
    ):
        copy = pltpu.make_async_copy(source, target, v.load.at[len(loads)])
        copy.start()
        loads.append(copy)

    def rows_loop(body, start):
        return lax.fori_loop(0, R // CHUNK, body, start, unroll=UNROLL)

    def chunk(i):
        return pl.ds(pl.multiple_of(i * CHUNK, CHUNK), CHUNK)

    def fold(values):
        return jnp.sum(values.reshape(values.shape[0] // TILE, TILE, values.shape[1]), axis=0)

    def add_rows(values):
        return jnp.sum(values, axis=0, keepdims=True)


    def start_exchange(which, one_tile=False):
        def send(step, carry):
            other = lax.rem(me + step, N)
            place = 0 if one_tile else pl.multiple_of(other * TILE, TILE)
            pltpu.make_async_remote_copy(
                src_ref=v.outgoing.at[which, pl.ds(place, TILE)],
                dst_ref=v.incoming.at[which, pl.ds(pl.multiple_of(me * TILE, TILE), TILE)],
                send_sem=v.give.at[which],
                recv_sem=v.take.at[which],
                device_id={"nodes": other},
                device_id_type=MESH,
            ).start()
            return carry

        lax.fori_loop(1, N, send, 0)
        own = pl.ds(pl.multiple_of(me * TILE, TILE), TILE)
        mine = pl.ds(0, TILE) if one_tile else own
        v.incoming[which, own, :] = v.outgoing[which, mine, :]

    def wait_bytes(ref, semaphore):
        pltpu.make_async_copy(ref, ref, semaphore).wait()

    def end_exchange(which):
        wait_exchange(which)

    def wait_exchange(which):
        wait_bytes(v.incoming.at[which, pl.ds(0, (N - 1) * TILE)], v.take.at[which])

    def row_in_tile(rows):
        return lax.rem(iota((rows, D), 0), TILE)

    def with_sums(values, first, second):
        row = row_in_tile(values.shape[0])
        return values + jnp.where(row == z.send, first, 0.0) + jnp.where(row == z.send + 1, second, 0.0)

    def arrived_sums(which):
        tile = jnp.sum(v.incoming[which].reshape(N, TILE, D), axis=0)
        return tile[z.send : z.send + 1, :], tile[z.send + 1 : z.send + 2, :]

    def arrived_rows(which):
        values = v.incoming[which]
        return jnp.where(row_in_tile(z.halo) < z.send, values, 0.0)

    def give_rows_back(which):
        high, low = halves(arrived_rows(which))
        listed = v.list_t[:, : z.halo]
        return mm(listed, high) + mm(listed, low)

    def owner(layer, mat):
        return 0 if (layer, mat) in ON_CORE_0 else 1

    sends_to_end = []

    def on(which, body):
        pl.when(core == which)(body)

    def stage_copy(layer, first, stage, source, target, device):
        pltpu.make_async_remote_copy(
            src_ref=source,
            dst_ref=target,
            send_sem=v.give_stage.at[layer, first, stage],
            recv_sem=v.take_stage.at[layer, first, stage],
            device_id=device,
            device_id_type=MESH,
        ).start()

    def stage_sent(layer, first, stage, ref, which):
        sends_to_end.append((ref, lambda: v.give_stage.at[layer, first, stage], which))

    def lane_of(layer, mat):
        lane = types.SimpleNamespace()
        over_section = (S, sec, lambda which: {"section": which})
        over_outer = (O, outer, lambda which: {"nodes": which * 2 + core})
        axes = (over_outer, over_section) if (layer, mat) in OUTER_FIRST else (over_section, over_outer)
        (lane.first, lane.first_me, lane.first_device), (lane.second, lane.second_me, lane.second_device) = axes
        lane.share, lane.piece, lane.owners = shares_of(R, lane.first, lane.second)
        lane.sums = v.sums.at[layer, mat]
        lane.result = grads.at[layer, mat]
        lane.from_first = getattr(v, f"first_{layer}{mat}")
        lane.from_second = getattr(v, f"second_{layer}{mat}")
        lane.share_rows = lambda which: pl.ds(pl.multiple_of(which * lane.share, TILE), lane.share)
        lane.piece_rows = lambda which: pl.ds(
            pl.multiple_of(lane.first_me * lane.share + which * lane.piece, TILE), lane.piece
        )
        return lane

    def start_core(layer, mat):
        on(
            1 - owner(layer, mat),
            lambda: stage_copy(
                layer, mat, CORE, v.sums.at[layer, mat], v.from_core.at[layer, mat], {"nodes": mate}
            ),
        )
        stage_sent(layer, mat, CORE, lambda: v.from_core.at[layer, mat], 1 - owner(layer, mat))

    def start_stage(stage, layer, mat):
        lane = lane_of(layer, mat)
        copy = functools.partial(stage_copy, layer, mat, stage)

        def sent(ref):
            stage_sent(layer, mat, stage, ref, owner(layer, mat))

        if stage == FIRST:
            for step in range(1, lane.first):
                other = lax.rem(lane.first_me + step, lane.first)
                copy(
                    lane.sums.at[lane.share_rows(other)],
                    lane.from_first.at[step - 1],
                    lane.first_device(other),
                )
            sent(lambda: lane_of(layer, mat).from_first)
        elif stage == SECOND:
            if lane.owners == lane.second:
                for step in range(1, lane.second):
                    other = lax.rem(lane.second_me + step, lane.second)
                    copy(
                        lane.sums.at[lane.piece_rows(other)],
                        lane.from_second.at[step],
                        lane.second_device(other),
                    )
                sent(lambda: lane_of(layer, mat).from_second.at[pl.ds(1, lane.second - 1)])
            else:
                for other in range(lane.owners):

                    @pl.when(lane.second_me != other)
                    def _():
                        copy(
                            lane.sums.at[lane.piece_rows(other)],
                            lane.from_second.at[
                                lax.rem(lane.second_me - other + lane.second, lane.second)
                            ],
                            lane.second_device(other),
                        )
                        wait_bytes(lane.from_second.at[0], v.give_stage.at[layer, mat, stage])

        elif stage == SECOND_BACK:

            def send_all():
                rows = lane.piece_rows(lane.second_me)
                for step in range(1, lane.second):
                    copy(
                        lane.result.at[rows],
                        lane.result.at[rows],
                        lane.second_device(lax.rem(lane.second_me + step, lane.second)),
                    )

            if lane.owners == lane.second:
                send_all()
                sent(lambda: lane_of(layer, mat).from_second.at[pl.ds(1, lane.second - 1)])
            else:

                @pl.when(lane.second_me < lane.owners)
                def _():
                    send_all()
                    wait_bytes(
                        lane.from_second.at[pl.ds(1, lane.second - 1)],
                        v.give_stage.at[layer, mat, stage],
                    )

        elif stage == FIRST_BACK:
            rows = lane.share_rows(lane.first_me)
            for step in range(1, lane.first):
                copy(
                    lane.result.at[rows],
                    lane.result.at[rows],
                    lane.first_device(lax.rem(lane.first_me + step, lane.first)),
                )
            sent(lambda: lane_of(layer, mat).from_first)
        elif stage == CORE_BACK:
            copy(lane.result, lane.result, {"nodes": mate})
            sent(lambda: grads.at[layer, mat])

    def end_stage(stage, layer, mat):
        lane = lane_of(layer, mat)
        taken = v.take_stage.at[layer, mat, stage]
        if stage == CORE:
            wait_bytes(v.from_core.at[layer, mat], taken)
            v.sums[layer, mat] = v.sums[layer, mat] + v.from_core[layer, mat]
        elif stage == FIRST:
            wait_bytes(lane.from_first, taken)
            rows = lane.share_rows(lane.first_me)
            value = v.sums[layer, mat, rows, :]
            for step in range(lane.first - 1):
                value = value + lane.from_first[step]
            v.sums[layer, mat, rows, :] = value
        elif stage == SECOND:

            def add():
                wait_bytes(lane.from_second.at[pl.ds(1, lane.second - 1)], taken)
                rows = lane.piece_rows(lane.second_me)
                value = v.sums[layer, mat, rows, :]
                for step in range(1, lane.second):
                    value = value + lane.from_second[step]
                grads[layer, mat, rows, :] = value

            if lane.owners == lane.second:
                add()
            else:
                pl.when(lane.second_me < lane.owners)(add)
        elif stage == SECOND_BACK:
            if lane.owners == lane.second:
                wait_bytes(lane.from_second.at[pl.ds(1, lane.second - 1)], taken)
            else:
                if lane.owners > 1:
                    wait_bytes(lane.from_second.at[pl.ds(1, lane.owners - 1)], taken)

                @pl.when(lane.second_me >= lane.owners)
                def _():
                    wait_bytes(lane.from_second.at[0], taken)

        elif stage == FIRST_BACK:
            wait_bytes(lane.from_first, taken)
        elif stage == CORE_BACK:
            wait_bytes(grads.at[layer, mat], taken)

    def advance(*moves):
        def run(which):
            for stage, layer, mat in moves:
                if owner(layer, mat) == which:
                    end_stage(stage, layer, mat)
                    start_stage(stage + 1, layer, mat)

        for which in range(2):
            if any(owner(layer, mat) == which for _, layer, mat in moves):
                on(which, functools.partial(run, which))


    loads[1].wait()
    v.listed_row[...] = jnp.zeros_like(v.listed_row)
    v.listed_row[0:1, : z.listed] = v.listed_in[pl.ds(sec, 1), :].astype(F32)
    spread_from = iota((v.listed_row.shape[1], z.halo_pad), 0)
    spread_to = iota((v.listed_row.shape[1], z.halo_pad), 1)
    spread = as_ones(
        (lax.div(spread_from, z.send) == lax.div(spread_to, TILE))
        & (lax.rem(spread_from, z.send) == lax.rem(spread_to, TILE))
        & (spread_from < z.listed)
    )
    listed = mm(v.listed_row[...].astype(BF16), spread)[0:1, :]
    place = iota((1, z.halo_pad), 1)
    real = (lax.rem(place, TILE) < z.send) & (place < z.halo)
    listed = jnp.where(real, listed, -1.0)
    list_t = jnp.where(iota((R, z.halo_pad), 0).astype(F32) == listed, 1.0, 0.0)
    v.list_t[...] = list_t.astype(BF16)
    v.list[...] = list_t.T[: z.halo, :].astype(BF16)

    loads[0].wait()
    own = v.features_in[...]
    v.h[pl.ds(0, R), :] = own
    high, low = halves(own)
    v.h_hi[pl.ds(0, R), :] = high
    v.h_lo[pl.ds(0, R), :] = low
    v.outgoing[FEATURES] = mm(v.list[...], high) + mm(v.list[...], low)
    pl.semaphore_wait(barrier, N - 1 + S - 1)
    start_exchange(FEATURES)

    for load in loads[2:5]:
        load.wait()
    for layer in range(2):
        for mat in range(3):
            high, low = halves(v.weights_in[mat, layer])
            v.weights_hi[layer, mat] = high
            v.weights_lo[layer, mat] = low

    def weight(layer, mat):
        return v.weights_hi[layer, mat], v.weights_lo[layer, mat]

    for load in loads[5:11]:
        load.wait()
    named = v.slots_in[...]
    offset = named - R
    remote = R + lax.div(offset, z.send) * TILE + lax.rem(offset, z.send)
    named = jnp.where(named < R, named, remote).astype(F32)
    v.prep[...] = jnp.zeros_like(v.prep)
    v.prep[pl.ds(0, K), :] = named
    v.prep[pl.ds(K, 1), :] = v.degree_in[pl.ds(sec, 1), :].astype(F32)
    v.prep[pl.ds(K + 1, 1), :] = v.mask_in[pl.ds(sec, 1), :].astype(F32)
    v.prep_t[...] = v.prep[...].T
    for slot in range(1, K):
        column = v.prep_t[:, slot : slot + 1]
        pick = as_ones(iota((R, T), 1).astype(F32) == column)
        v.pick[slot - 1, :, pl.ds(0, T)] = pick
        v.pick[slot - 1, :, pl.ds(T, z.halo_pad)] = pick[:, R:]
        row = v.prep[slot : slot + 1, :]
        v.pick_t[:, (slot - 1) * R : slot * R] = as_ones(iota((z.picked, R), 0).astype(F32) == row)
    block_row = lax.div(lax.rem(iota((2 * D, D), 0), D), GROUP)
    v.ones[...] = as_ones(block_row == lax.div(iota((2 * D, D), 1), GROUP))

    def project(layer):
        rows = pl.ds(0, R)
        own = (v.h_hi[rows, :], v.h_lo[rows, :])
        left = mm3(own, weight(layer, 0))
        v.taken[layer, 0] = left
        high, low = halves(left)
        v.table_hi[rows, :] = high
        v.table_lo[rows, :] = low
        v.right[layer] = mm3(own, weight(layer, 1))
        v.skip[...] = mm3(own, weight(layer, 2))

    def project_halo(layer):
        rows = pl.ds(R, z.halo_pad)
        left = mm3((v.h_hi[rows, :], v.h_lo[rows, :]), weight(layer, 0))
        high, low = halves(left)
        v.halo_table[pl.ds(0, z.halo_pad), :] = high
        v.halo_table[pl.ds(z.halo_pad, z.halo_pad), :] = low

    def store_halo(values):
        if z.halo < z.halo_pad:
            rest = pl.ds(R + z.halo, z.halo_pad - z.halo)
            v.h[rest, :] = jnp.zeros((z.halo_pad - z.halo, D), F32)
            v.h_hi[rest, :] = jnp.zeros((z.halo_pad - z.halo, D), BF16)
            v.h_lo[rest, :] = jnp.zeros((z.halo_pad - z.halo, D), BF16)
        rows = pl.ds(R, z.halo)
        v.h[rows, :] = values
        high, low = halves(values)
        v.h_hi[rows, :] = high
        v.h_lo[rows, :] = low

    def keep_transposed(layer):
        high, low = halves(v.h[...].T)
        v.ht_hi[layer] = high
        v.ht_lo[layer] = low

    def store_pair(slot, rows, values):
        high, low = halves(values)
        v.pair[slot, rows, pl.ds(0, D)] = high
        v.pair[slot, rows, pl.ds(D, D)] = low

    def gather_own(layer):
        def one(slot, carry):
            pick = v.pick[slot - 1, :, pl.ds(0, R)]
            v.taken[layer, slot] = mm(pick, v.table_hi[...]) + mm(pick, v.table_lo[...])
            return carry

        lax.fori_loop(1, K, one, 0, unroll=True)

    def head_sum(slot):
        v.score[slot] = mm(v.pair[slot], v.ones[...])

    def attend(layer):
        vector = v.vector_in[layer : layer + 1, :]

        def gather(slot):
            pick = v.pick[slot - 1, :, pl.ds(R, 2 * z.halo_pad)]
            value = mm(pick, v.halo_table[...])
            if layer == 0:
                value = v.taken[layer, slot] + value
            else:
                pick = v.pick[slot - 1, :, pl.ds(0, R)]
                value = mm(pick, v.table_hi[...]) + mm(pick, v.table_lo[...]) + value
            v.taken[layer, slot] = value

        def activate(slot):
            for place in range(0, R, BLOCK):
                rows = pl.ds(place, BLOCK)
                u = v.taken[layer, slot, rows, :] + v.right[layer, rows, :]
                store_pair(slot, rows, u * sigmoid(u) * vector)

        for slot in range(1, K + 3):
            if slot < K:
                gather(slot)
            if slot <= K:
                activate(slot - 1)
            if slot >= 3:
                head_sum(slot - 3)

        def mix(i, carry):
            rows = chunk(i)
            count = jnp.broadcast_to(v.prep_t[rows, K : K + 1], (CHUNK, D))
            scores = [
                jnp.where(count > slot, v.score[slot, rows, :], MASKED_SCORE) for slot in range(K)
            ]
            highest = functools.reduce(jnp.maximum, scores)
            powers = [jnp.exp(score - highest) for score in scores]
            scale = 1.0 / functools.reduce(jnp.add, powers)
            joined = jnp.zeros((CHUNK, D), F32)
            for slot in range(K):
                alpha = powers[slot] * scale
                v.alpha[layer, slot, rows, :] = alpha
                joined = joined + alpha * v.taken[layer, slot, rows, :]
            v.joined[layer, rows, :] = joined
            mixed = joined + v.skip[rows, :]
            v.mixed[rows, :] = mixed
            return carry[0] + fold(mixed), carry[1] + fold(mixed * mixed)

        nothing = jnp.zeros((TILE, D), F32)
        first, second = rows_loop(mix, (nothing, nothing))
        return add_rows(first), add_rows(second)

    def derive(layer):
        vector = v.vector_in[layer : layer + 1, :]

        def one(i, carry):
            rows = chunk(i)
            right = v.right[layer, rows, :]
            for slot in range(K):
                u = v.taken[layer, slot, rows, :] + right
                sig = sigmoid(u)
                act = u * sig
                v.act[layer, slot, rows, :] = act
                v.rise[layer, slot, rows, :] = vector * (sig + act * (1.0 - sig))
            return carry

        rows_loop(one, 0)

    def moments(which):
        first, second = arrived_sums(which)
        mean = first / total_rows
        return mean, lax.rsqrt(second / total_rows - mean * mean + VARIANCE_EPS)

    def activation(layer, mixed, mean, inverse):
        normed = (mixed - mean) * inverse
        pre = v.gain_in[layer : layer + 1, :] * normed + v.shift_in[layer : layer + 1, :]
        power = jnp.exp(jnp.minimum(pre, 0.0))
        return normed, jnp.where(pre > 0, 1.0, power), jnp.where(pre > 0, pre, power - 1.0)

    def sums_tile(which, first, second):
        v.outgoing[which, pl.ds(0, TILE), :] = with_sums(jnp.zeros((TILE, D), F32), first, second)

    def list_rows(values):
        high, low = halves(values)
        return mm(v.list[...], high) + mm(v.list[...], low)

    project(0)
    gather_own(0)
    end_exchange(FEATURES)
    store_halo(arrived_rows(FEATURES))
    project_halo(0)
    first, second = attend(0)
    v.outgoing[MIXED] = with_sums(list_rows(v.mixed[...]), first, second)
    start_exchange(MIXED)
    keep_transposed(0)
    derive(0)
    end_exchange(MIXED)
    mean0, inverse0 = moments(MIXED)

    def finish0(i, carry):
        rows = chunk(i)
        normed, slope, hidden = activation(0, v.mixed[rows, :], mean0, inverse0)
        v.normed[0, rows, :] = normed
        v.slope[0, rows, :] = slope
        v.h[rows, :] = hidden
        high, low = halves(hidden)
        v.h_hi[rows, :] = high
        v.h_lo[rows, :] = low
        return carry

    rows_loop(finish0, 0)
    normed, slope, hidden = activation(0, arrived_rows(MIXED), mean0, inverse0)
    v.halo_normed[...] = normed
    v.halo_slope[...] = slope
    store_halo(jnp.where(row_in_tile(z.halo) < z.send, hidden, 0.0))

    project(1)
    project_halo(1)
    first, second = attend(1)
    sums_tile(SUMS, first, second)
    start_exchange(SUMS, True)
    keep_transposed(1)
    derive(1)
    loads[11].wait()
    end_exchange(SUMS)
    mean1, inverse1 = moments(SUMS)

    def finish1(i, carry):
        rows = chunk(i)
        normed, slope, hidden = activation(1, v.mixed[rows, :], mean1, inverse1)
        v.normed[1, rows, :] = normed
        out[0, rows, :] = hidden
        dpre = v.cotangent_in[rows, :] * v.prep_t[rows, K + 1 : K + 2] * slope
        v.dpre[rows, :] = dpre
        return carry[0] + fold(dpre), carry[1] + fold(dpre * normed)

    nothing = jnp.zeros((TILE, D), F32)
    first, second = rows_loop(finish1, (nothing, nothing))
    shift1, gain1 = add_rows(first), add_rows(second)
    sums_tile(BACK_SUMS, shift1, gain1)
    start_exchange(BACK_SUMS, True)

    def normalization_back(layer, which, inverse):
        first, second = arrived_sums(which)
        first = first / total_rows
        second = second / total_rows
        scale = inverse * v.gain_in[layer : layer + 1, :]

        def one(i, carry):
            rows = chunk(i)
            dmixed = scale * (v.dpre[rows, :] - first - v.normed[layer, rows, :] * second)
            v.dmixed[rows, :] = dmixed
            high, low = halves(dmixed)
            v.dm_hi[rows, :] = high
            v.dm_lo[rows, :] = low
            return carry

        rows_loop(one, 0)

    def attend_back(layer, between=None):
        def differences(slot):
            for place in range(0, R, BLOCK):
                rows = pl.ds(place, BLOCK)
                value = (v.taken[layer, slot, rows, :] - v.joined[layer, rows, :]) * v.dmixed[rows, :]
                store_pair(slot, rows, value)

        weight_grad(layer, 2)
        for slot in range(K + 1):
            if slot < K:
                differences(slot)
            if slot >= 1:
                head_sum(slot - 1)
        start_core(layer, 2)

        def one(i, carry):
            rows = chunk(i)
            dmixed = v.dmixed[rows, :]
            dright = jnp.zeros((CHUNK, D), F32)
            for slot in range(K):
                alpha = v.alpha[layer, slot, rows, :]
                dscore = alpha * v.score[slot, rows, :]
                carry = carry + fold(dscore * v.act[layer, slot, rows, :])
                du = dscore * v.rise[layer, slot, rows, :]
                dright = dright + du
                dleft = du + alpha * dmixed
                if slot == 0:
                    v.dleft_self[rows, :] = dleft
                else:
                    high, low = halves(dleft)
                    place = pl.ds(pl.multiple_of((slot - 1) * R + i * CHUNK, CHUNK), CHUNK)
                    v.dleft_hi[place, :] = high
                    v.dleft_lo[place, :] = low
            high, low = halves(dright)
            v.dr_hi[rows, :] = high
            v.dr_lo[rows, :] = low
            return carry

        vector_sum = rows_loop(one, jnp.zeros((TILE, D), F32))
        if between is not None:
            between()

        def scattered(rows):
            pick = v.pick_t[rows, :]
            return mm(pick, v.dleft_hi[...]) + mm(pick, v.dleft_lo[...])

        rows = pl.ds(0, R)
        own = scattered(rows) + v.dleft_self[...]
        v.dleft_self[...] = own
        high, low = halves(own)
        v.dl_hi[rows, :] = high
        v.dl_lo[rows, :] = low
        rows = pl.ds(R, z.halo)
        halo = scattered(rows)
        if layer == 0:
            start_return(halo)
        high, low = halves(halo)
        v.dl_hi[rows, :] = high
        v.dl_lo[rows, :] = low
        return add_rows(vector_sum)

    def start_return(halo):
        v.returning[...] = halo[:, :LANES] + pltpu.roll(halo[:, LANES:], z.send, 0)
        own = pl.ds(pl.multiple_of(me * TILE, TILE), TILE)

        def send(step, carry):
            other = lax.rem(me + step, N)
            pltpu.make_async_remote_copy(
                src_ref=v.returning.at[pl.ds(pl.multiple_of(other * TILE, TILE), TILE)],
                dst_ref=v.returned.at[own],
                send_sem=v.give_rows.at[0],
                recv_sem=v.take_rows.at[0],
                device_id={"nodes": other},
                device_id_type=MESH,
            ).start()
            return carry

        lax.fori_loop(1, N, send, 0)
        v.returned[own, :] = v.returning[own, :]

    def dleft(rows):
        return v.dl_hi[rows, :], v.dl_lo[rows, :]

    def input_back(layer):
        own = pl.ds(0, R)
        v.dh[...] = (
            mm3(dleft(own), weight(layer, 0), mm_nt)
            + mm3((v.dr_hi[...], v.dr_lo[...]), weight(layer, 1), mm_nt)
            + mm3((v.dm_hi[...], v.dm_lo[...]), weight(layer, 2), mm_nt)
        )
        return mm3(dleft(pl.ds(R, z.halo)), weight(layer, 0), mm_nt)

    def weight_grad(layer, mat):
        if mat == 0:
            upstream = (v.dl_hi[...], v.dl_lo[...])
            inputs = (v.ht_hi[layer], v.ht_lo[layer])
        else:
            upstream = (v.dr_hi[...], v.dr_lo[...]) if mat == 1 else (v.dm_hi[...], v.dm_lo[...])
            inputs = (v.ht_hi[layer, :, pl.ds(0, R)], v.ht_lo[layer, :, pl.ds(0, R)])
        v.sums[layer, mat] = mm3(inputs, upstream)

    if z.halo < z.halo_pad:
        rest = pl.ds(R + z.halo, z.halo_pad - z.halo)
        v.dl_hi[rest, :] = jnp.zeros((z.halo_pad - z.halo, D), BF16)
        v.dl_lo[rest, :] = jnp.zeros((z.halo_pad - z.halo, D), BF16)

    end_exchange(BACK_SUMS)
    normalization_back(1, BACK_SUMS, inverse1)
    vector1 = attend_back(1)
    halo_back = input_back(1)
    dpre = v.dh[...] * v.slope[0]
    halo_dpre = halo_back * v.halo_slope[...]
    shift0 = add_rows(dpre) + add_rows(halo_dpre)
    gain0 = add_rows(dpre * v.normed[0]) + add_rows(halo_dpre * v.halo_normed[...])
    v.outgoing[BACK_ROWS] = with_sums(halo_back, shift0, gain0)
    start_exchange(BACK_ROWS)
    advance((CORE, 1, 2))
    weight_grad(1, 1)
    start_core(1, 1)
    weight_grad(1, 0)
    start_core(1, 0)
    advance((CORE, 1, 1), (CORE, 1, 0))
    end_exchange(BACK_ROWS)
    v.dpre[...] = (v.dh[...] + give_rows_back(BACK_ROWS)) * v.slope[0]

    normalization_back(0, BACK_ROWS, inverse0)

    def between():
        weight_grad(0, 1)
        start_core(0, 1)
        advance(*BETWEEN)

    vector0 = attend_back(0, between)
    weight_grad(0, 0)
    start_core(0, 0)

    row = iota((TILE, D), 0)
    tile = jnp.zeros((TILE, D), F32)
    for place, value in enumerate((vector0, vector1, gain0, gain1, shift0, shift1)):
        tile = jnp.where(row == place, value, tile)
    v.small[0] = tile

    def send_small(stage, source, target, device):
        pltpu.make_async_remote_copy(
            src_ref=source,
            dst_ref=target,
            send_sem=v.give_small.at[stage],
            recv_sem=v.take_small.at[stage],
            device_id=device,
            device_id_type=MESH,
        ).start()

    on(0, lambda: send_small(0, v.small.at[0], v.small_core.at[0], {"nodes": mate}))

    def small_outer():
        wait_bytes(v.small_core.at[0], v.take_small.at[0])
        value = v.small[0] + v.small_core[0]
        v.small[1] = value
        v.small_outer[outer] = value
        for step in range(1, O):
            send_small(
                1, v.small.at[1], v.small_outer.at[outer], {"nodes": lax.rem(outer + step, O) * 2 + core}
            )

    def small_section():
        wait_bytes(v.small_outer.at[pl.ds(1, O - 1)], v.take_small.at[1])
        value = jnp.sum(v.small_outer[...], axis=0)
        v.small[2] = value
        v.small_section[sec] = value
        for step in range(1, S):
            send_small(
                2, v.small.at[2], v.small_section.at[sec], {"section": lax.rem(sec + step, S)}
            )

    def put_small(value):
        g_vec[...] = value[0:2, :]
        g_gain[...] = value[2:4, :]
        g_shift[...] = value[4:6, :]

    def small_back():
        wait_bytes(v.small_section.at[pl.ds(1, S - 1)], v.take_small.at[2])
        value = jnp.sum(v.small_section[...], axis=0)
        v.small[3] = value
        send_small(3, v.small.at[3], v.small_core.at[1], {"nodes": mate})
        put_small(value)

    def small_end():
        wait_bytes(v.small_core.at[1], v.take_small.at[3])
        put_small(v.small_core[1])

    advance(*AFTER)
    def part_input():
        v.dh[...] = mm3((v.dr_hi[...], v.dr_lo[...]), weight(0, 1), mm_nt) + mm3(
            (v.dm_hi[...], v.dm_lo[...]), weight(0, 2), mm_nt
        )

    def store_input():
        wait_bytes(v.returned.at[pl.ds(0, (N - 1) * TILE)], v.take_rows.at[0])
        values = v.returned[...]
        values = jnp.concatenate([values, pltpu.roll(values, z.halo - z.send, 0)], axis=1)
        high, low = halves(jnp.where(row_in_tile(z.halo) < z.send, values, 0.0))
        listed = v.list_t[:, : z.halo]
        left = v.dleft_self[...] + (mm(listed, high) + mm(listed, low))
        grad_in[0] = v.dh[...] + mm3(halves(left), weight(0, 0), mm_nt)

    steps = {
        "outer": small_outer,
        "section": small_section,
        "back": small_back,
        "end": small_end,
        "part": part_input,
        "input": store_input,
    }

    def finish(which):
        for step in TAILS[which]:
            if isinstance(step, str):
                steps[step]()
            else:
                end_stage(*step)
                start_stage(step[0] + 1, *step[1:])

    on(0, lambda: finish(0))
    on(1, lambda: finish(1))

    def receive(which):
        for layer in (1, 0):
            for mat in (2, 1, 0):
                if owner(layer, mat) != which:
                    end_stage(CORE_BACK, layer, mat)

    for which in range(EXCHANGES):
        wait_bytes(v.outgoing.at[which, pl.ds(0, (N - 1) * TILE)], v.give.at[which])
    wait_bytes(v.returned.at[pl.ds(0, (N - 1) * TILE)], v.give_rows.at[0])

    def sent(which):
        for ref, semaphore, sender in sends_to_end:
            if sender == which:
                wait_bytes(ref(), semaphore())

    def sent_small(stage, count):
        wait_bytes(v.small_outer.at[pl.ds(0, count)], v.give_small.at[stage])

    def sent0():
        sent(0)
        sent_small(0, 1)
        receive(0)

    def sent1():
        sent(1)
        sent_small(1, O - 1)
        wait_bytes(v.small_section.at[pl.ds(1, S - 1)], v.give_small.at[2])
        sent_small(3, 1)
        receive(1)

    on(0, sent0)
    on(1, sent1)


def store_kernel(*refs):
    out, grad_in, grads, g_vec, g_gain, g_shift = refs[:6]
    pairs = [(out, refs[6]), (grad_in, refs[7])]
    for mat in range(3):
        pairs += [(grads.at[layer, mat], refs[8 + mat].at[layer]) for layer in range(2)]
    pairs += [(g_vec, refs[11]), (g_gain, refs[12]), (g_shift, refs[13])]
    copies = [pltpu.make_async_copy(*pair, refs[14].at[i]) for i, pair in enumerate(pairs)]
    for copy in copies:
        copy.start()
    for copy in copies:
        copy.wait()


def body(
    features,
    cotangent,
    train_mask,
    degree,
    neighbours,
    send_rows,
    w_left,
    w_right,
    w_res,
    attn_vec,
    bn_gain,
    bn_shift,
):
    batches, rows, width = features.shape
    sections = lax.axis_size("section")
    assert batches == sections and width == HEADS * GROUP
    z = sizes_of(
        sections, lax.axis_size("nodes"), rows, width, neighbours.shape[2], send_rows.shape[1]
    )
    shapes = scratch_of(z)
    shapes["mask_in"] = (train_mask.shape, jnp.int32)
    shapes["degree_in"] = (degree.shape, jnp.int32)
    shapes["listed_in"] = (send_rows.shape, jnp.int32)
    scratch = [pltpu.VMEM(shape, dtype) for shape, dtype in shapes.values()]
    scratch += [pltpu.SemaphoreType.DMA(shape) for shape in SEMAPHORES.values()]
    names = list(shapes) + list(SEMAPHORES)
    anywhere = pl.BlockSpec(memory_space=pl.ANY)
    square = jax.ShapeDtypeStruct((2, width, width), F32)
    columns = jax.ShapeDtypeStruct((2, width), F32)
    block = jax.ShapeDtypeStruct((1, rows, width), F32)
    results = (block, block, square, square, square, columns, columns, columns)
    in_vmem = pl.BlockSpec(memory_space=pltpu.VMEM)
    squares = jax.ShapeDtypeStruct((2, 3, width, width), F32)
    kept = (block, block, squares, columns, columns, columns)
    found = pl.pallas_call(
        functools.partial(kernel, z, names),
        out_shape=tuple(pltpu.VMEM(x.shape, x.dtype) for x in kept),
        in_specs=[pl.BlockSpec(memory_space=pltpu.HBM)] * 12,
        out_specs=(in_vmem,) * 6,
        scratch_shapes=scratch,
        compiler_params=pltpu.CompilerParams(
            collective_id=0, has_side_effects=True, vmem_limit_bytes=60 * 1024 * 1024
        ),
    )(
        features,
        cotangent,
        train_mask,
        degree,
        jnp.transpose(neighbours, (0, 2, 1)),
        send_rows,
        w_left,
        w_right,
        w_res,
        attn_vec,
        bn_gain,
        bn_shift,
    )
    return pl.pallas_call(
        store_kernel,
        out_shape=results,
        in_specs=[anywhere] * 6,
        out_specs=(anywhere,) * 8,
        scratch_shapes=[pltpu.SemaphoreType.DMA((11,))],
        compiler_params=pltpu.CompilerParams(vmem_limit_bytes=1024 * 1024),
    )(*found)


def solution(mesh):
    return jax.shard_map(
        body,
        mesh=mesh,
        in_specs=(
            P(None, "nodes", None),
            P(None, "nodes", None),
            P(None, "nodes"),
            P(None, "nodes"),
            P(None, "nodes", None),
            P(None, "nodes"),
            P(),
            P(),
            P(),
            P(),
            P(),
            P(),
        ),
        out_specs=(
            P("section", "nodes", None),
            P("section", "nodes", None),
            P(),
            P(),
            P(),
            P(),
            P(),
            P(),
        ),
        check_vma=False,
    )
```

```python
import functools
import types

import jax
import jax.numpy as jnp
from jax import lax
from jax.experimental import pallas as pl
from jax.experimental.pallas import tpu as pltpu
from jax.sharding import PartitionSpec as P

HEADS = 4
MASKED_SCORE = -1e30
VARIANCE_EPS = 1e-05
F32 = jnp.float32
BF16 = jnp.bfloat16
MESH = pl.DeviceIdType.MESH
UNROLL = 16
BLOCK = 32
OUTER_FIRST = ()
LANES = 128
GROUP = 64
TILE = 8
CHUNK = 16

FEATURES, MIXED, SUMS, BACK_SUMS, BACK_ROWS = range(5)
EXCHANGES = 5
CORE, FIRST, SECOND, SECOND_BACK, FIRST_BACK, CORE_BACK = range(6)
STAGES = 6
ON_CORE_0 = ((1, 2), (1, 1))
BETWEEN = ((FIRST, 1, 2), (FIRST, 1, 0), (CORE, 0, 2))
AFTER = ((FIRST, 1, 1), (CORE, 0, 1))
TAILS = (
    (
        (SECOND, 1, 2),
        (SECOND, 1, 1),
        (SECOND_BACK, 1, 2),
        (SECOND_BACK, 1, 1),
        (FIRST_BACK, 1, 2),
        (FIRST_BACK, 1, 1),
        "part",
        "input",
        "end",
    ),
    (
        (CORE, 0, 0),
        (SECOND, 1, 0),
        (FIRST, 0, 2),
        "outer",
        (FIRST, 0, 1),
        (FIRST, 0, 0),
        (SECOND_BACK, 1, 0),
        (SECOND, 0, 2),
        (SECOND, 0, 1),
        "section",
        (SECOND, 0, 0),
        (FIRST_BACK, 1, 0),
        (SECOND_BACK, 0, 2),
        (SECOND_BACK, 0, 1),
        "back",
        (SECOND_BACK, 0, 0),
        (FIRST_BACK, 0, 2),
        (FIRST_BACK, 0, 1),
        (FIRST_BACK, 0, 0),
        "part",
        "input",
    ),
)


def halves(values):
    high = values.astype(BF16)
    return high, (values - high.astype(F32)).astype(BF16)


def mm(lhs, rhs):
    return jnp.dot(lhs, rhs, preferred_element_type=F32)


def mm_nt(lhs, rhs):
    return lax.dot_general(lhs, rhs, (((1,), (1,)), ((), ())), preferred_element_type=F32)


def mm3(lhs, rhs, product=mm):
    return product(lhs[0], rhs[0]) + product(lhs[1], rhs[0]) + product(lhs[0], rhs[1])


def iota(shape, dim):
    return lax.broadcasted_iota(jnp.int32, shape, dim)


def sigmoid(u):
    return 0.5 * jnp.tanh(0.5 * u) + 0.5


def as_ones(condition):
    return jnp.where(condition, 1.0, 0.0).astype(BF16)


def sizes_of(sections, partitions, rows, width, slots, listed):
    z = types.SimpleNamespace()
    z.sections, z.partitions, z.outer = sections, partitions, partitions // 2
    z.rows, z.width, z.slots, z.listed = rows, width, slots, listed
    z.send = listed // partitions
    z.halo = partitions * TILE
    z.halo_pad = -(-z.halo // LANES) * LANES
    z.table = rows + z.halo_pad
    z.picked = rows + z.halo
    return z


def shares_of(rows, first, second):
    share = rows // first
    piece = max(TILE, share // second)
    return share, piece, share // piece


def scratch_of(z):
    R, D, K, T = z.rows, z.width, z.slots, z.table
    S, O = z.sections, z.outer
    vmem = {
        "features_in": ((R, D), F32),
        "cotangent_in": ((R, D), F32),
        "mask_in": (None, jnp.int32),
        "degree_in": (None, jnp.int32),
        "slots_in": ((K, R), jnp.int32),
        "listed_in": (None, jnp.int32),
        "weights_in": ((3, 2, D, D), F32),
        "vector_in": ((2, D), F32),
        "gain_in": ((2, D), F32),
        "shift_in": ((2, D), F32),
        "weights_hi": ((2, 3, D, D), BF16),
        "weights_lo": ((2, 3, D, D), BF16),
        "prep": ((LANES, R), F32),
        "prep_t": ((R, LANES), F32),
        "listed_row": ((TILE, max(LANES, z.listed)), F32),
        "pick": ((K - 1, R, R + 2 * z.halo_pad), BF16),
        "pick_t": ((z.picked, (K - 1) * R), BF16),
        "list": ((z.halo, R), BF16),
        "list_t": ((R, z.halo_pad), BF16),
        "ones": ((2 * D, D), BF16),
        "h": ((T, D), F32),
        "h_hi": ((T, D), BF16),
        "h_lo": ((T, D), BF16),
        "ht_hi": ((2, D, T), BF16),
        "ht_lo": ((2, D, T), BF16),
        "table_hi": ((R, D), BF16),
        "table_lo": ((R, D), BF16),
        "halo_table": ((2 * z.halo_pad, D), BF16),
        "taken": ((2, K, R, D), F32),
        "act": ((2, K, R, D), F32),
        "rise": ((2, K, R, D), F32),
        "alpha": ((2, K, R, D), F32),
        "joined": ((2, R, D), F32),
        "right": ((2, R, D), F32),
        "skip": ((R, D), F32),
        "mixed": ((R, D), F32),
        "normed": ((2, R, D), F32),
        "slope": ((2, R, D), F32),
        "halo_normed": ((z.halo, D), F32),
        "halo_slope": ((z.halo, D), F32),
        "pair": ((K, R, 2 * D), BF16),
        "score": ((K, R, D), F32),
        "dpre": ((R, D), F32),
        "dmixed": ((R, D), F32),
        "dm_hi": ((R, D), BF16),
        "dm_lo": ((R, D), BF16),
        "dr_hi": ((R, D), BF16),
        "dr_lo": ((R, D), BF16),
        "dl_hi": ((T, D), BF16),
        "dl_lo": ((T, D), BF16),
        "dleft_self": ((R, D), F32),
        "dleft_hi": (((K - 1) * R, D), BF16),
        "dleft_lo": (((K - 1) * R, D), BF16),
        "dh": ((R, D), F32),
        "outgoing": ((EXCHANGES, z.halo, D), F32),
        "incoming": ((EXCHANGES, z.halo, D), F32),
        "small": ((4, TILE, D), F32),
        "small_core": ((2, TILE, D), F32),
        "small_outer": ((O, TILE, D), F32),
        "small_section": ((S, TILE, D), F32),
        "returning": ((z.halo, LANES), F32),
        "returned": ((z.halo, LANES), F32),
        "sums": ((2, 3, R, D), F32),
        "from_core": ((2, 3, R, D), F32),
    }
    for layer in range(2):
        for mat in range(3):
            first, second = (O, S) if (layer, mat) in OUTER_FIRST else (S, O)
            share, piece, _ = shares_of(R, first, second)
            vmem[f"first_{layer}{mat}"] = ((first - 1, share, D), F32)
            vmem[f"second_{layer}{mat}"] = ((second, piece, D), F32)
    return vmem


SEMAPHORES = {
    "load": (12,),
    "give": (EXCHANGES,),
    "take": (EXCHANGES,),
    "give_small": (4,),
    "take_small": (4,),
    "give_rows": (1,),
    "take_rows": (1,),
    "give_stage": (2, 3, STAGES),
    "take_stage": (2, 3, STAGES),
}


def kernel(z, names, *refs):
    features, cotangent, train_mask, degree, neighbours, send_rows = refs[:6]
    w_left, w_right, w_res, attn_vec, bn_gain, bn_shift = refs[6:12]
    out, grad_in, grads, g_vec, g_gain, g_shift = refs[12:18]
    v = types.SimpleNamespace(**dict(zip(names, refs[18:])))
    R, D, K, T = z.rows, z.width, z.slots, z.table
    S, N, O = z.sections, z.partitions, z.outer
    total_rows = R * N
    sec = lax.axis_index("section")
    me = lax.axis_index("nodes")
    core = lax.rem(me, 2)
    outer = lax.div(me, 2)
    mate = me + 1 - 2 * core
    side = 2 * lax.div(2 * me, N) - 1

    barrier = pltpu.get_barrier_semaphore()

    def greet(step, carry):
        pl.semaphore_signal(
            barrier, inc=1, device_id={"nodes": lax.rem(me + side * step + N, N)}, device_id_type=MESH
        )
        return carry

    lax.fori_loop(1, N, greet, 0)
    for step in range(1, S):
        pl.semaphore_signal(
            barrier, inc=1, device_id={"section": lax.rem(sec + step, S)}, device_id_type=MESH
        )

    loads = []
    for source, target in (
        (features.at[sec], v.features_in),
        (send_rows, v.listed_in),
        (w_left, v.weights_in.at[0]),
        (w_right, v.weights_in.at[1]),
        (w_res, v.weights_in.at[2]),
        (neighbours.at[sec], v.slots_in),
        (degree, v.degree_in),
        (train_mask, v.mask_in),
        (attn_vec, v.vector_in),
        (bn_gain, v.gain_in),
        (bn_shift, v.shift_in),
        (cotangent.at[sec], v.cotangent_in),
    ):
        copy = pltpu.make_async_copy(source, target, v.load.at[len(loads)])
        copy.start()
        loads.append(copy)

    def rows_loop(body, start):
        return lax.fori_loop(0, R // CHUNK, body, start, unroll=UNROLL)

    def chunk(i):
        return pl.ds(pl.multiple_of(i * CHUNK, CHUNK), CHUNK)

    def fold(values):
        return jnp.sum(values.reshape(values.shape[0] // TILE, TILE, values.shape[1]), axis=0)

    def add_rows(values):
        return jnp.sum(values, axis=0, keepdims=True)


    def start_exchange(which, one_tile=False):
        def send(step, carry):
            other = lax.rem(me + side * step + N, N)
            place = 0 if one_tile else pl.multiple_of(other * TILE, TILE)
            pltpu.make_async_remote_copy(
                src_ref=v.outgoing.at[which, pl.ds(place, TILE)],
                dst_ref=v.incoming.at[which, pl.ds(pl.multiple_of(me * TILE, TILE), TILE)],
                send_sem=v.give.at[which],
                recv_sem=v.take.at[which],
                device_id={"nodes": other},
                device_id_type=MESH,
            ).start()
            return carry

        lax.fori_loop(1, N, send, 0)
        own = pl.ds(pl.multiple_of(me * TILE, TILE), TILE)
        mine = pl.ds(0, TILE) if one_tile else own
        v.incoming[which, own, :] = v.outgoing[which, mine, :]

    def wait_bytes(ref, semaphore):
        pltpu.make_async_copy(ref, ref, semaphore).wait()

    def end_exchange(which):
        wait_exchange(which)

    def wait_exchange(which):
        wait_bytes(v.incoming.at[which, pl.ds(0, (N - 1) * TILE)], v.take.at[which])

    def row_in_tile(rows):
        return lax.rem(iota((rows, D), 0), TILE)

    def with_sums(values, first, second):
        row = row_in_tile(values.shape[0])
        return values + jnp.where(row == z.send, first, 0.0) + jnp.where(row == z.send + 1, second, 0.0)

    def arrived_sums(which):
        tile = jnp.sum(v.incoming[which].reshape(N, TILE, D), axis=0)
        return tile[z.send : z.send + 1, :], tile[z.send + 1 : z.send + 2, :]

    def arrived_rows(which):
        values = v.incoming[which]
        return jnp.where(row_in_tile(z.halo) < z.send, values, 0.0)

    def give_rows_back(which):
        high, low = halves(arrived_rows(which))
        listed = v.list_t[:, : z.halo]
        return mm(listed, high) + mm(listed, low)

    def owner(layer, mat):
        return 0 if (layer, mat) in ON_CORE_0 else 1

    sends_to_end = []

    def on(which, body):
        pl.when(core == which)(body)

    def stage_copy(layer, first, stage, source, target, device):
        pltpu.make_async_remote_copy(
            src_ref=source,
            dst_ref=target,
            send_sem=v.give_stage.at[layer, first, stage],
            recv_sem=v.take_stage.at[layer, first, stage],
            device_id=device,
            device_id_type=MESH,
        ).start()

    def stage_sent(layer, first, stage, ref, which):
        sends_to_end.append((ref, lambda: v.give_stage.at[layer, first, stage], which))

    def lane_of(layer, mat):
        lane = types.SimpleNamespace()
        over_section = (S, sec, lambda which: {"section": which})
        over_outer = (O, outer, lambda which: {"nodes": which * 2 + core})
        axes = (over_outer, over_section) if (layer, mat) in OUTER_FIRST else (over_section, over_outer)
        (lane.first, lane.first_me, lane.first_device), (lane.second, lane.second_me, lane.second_device) = axes
        lane.share, lane.piece, lane.owners = shares_of(R, lane.first, lane.second)
        lane.sums = v.sums.at[layer, mat]
        lane.result = grads.at[layer, mat]
        lane.from_first = getattr(v, f"first_{layer}{mat}")
        lane.from_second = getattr(v, f"second_{layer}{mat}")
        lane.share_rows = lambda which: pl.ds(pl.multiple_of(which * lane.share, TILE), lane.share)
        lane.piece_rows = lambda which: pl.ds(
            pl.multiple_of(lane.first_me * lane.share + which * lane.piece, TILE), lane.piece
        )
        return lane

    def start_core(layer, mat):
        on(
            1 - owner(layer, mat),
            lambda: stage_copy(
                layer, mat, CORE, v.sums.at[layer, mat], v.from_core.at[layer, mat], {"nodes": mate}
            ),
        )
        stage_sent(layer, mat, CORE, lambda: v.from_core.at[layer, mat], 1 - owner(layer, mat))

    def start_stage(stage, layer, mat):
        lane = lane_of(layer, mat)
        copy = functools.partial(stage_copy, layer, mat, stage)

        def sent(ref):
            stage_sent(layer, mat, stage, ref, owner(layer, mat))

        if stage == FIRST:
            for step in range(1, lane.first):
                other = lax.rem(lane.first_me + step, lane.first)
                copy(
                    lane.sums.at[lane.share_rows(other)],
                    lane.from_first.at[step - 1],
                    lane.first_device(other),
                )
            sent(lambda: lane_of(layer, mat).from_first)
        elif stage == SECOND:
            if lane.owners == lane.second:
                for step in range(1, lane.second):
                    other = lax.rem(lane.second_me + step, lane.second)
                    copy(
                        lane.sums.at[lane.piece_rows(other)],
                        lane.from_second.at[step],
                        lane.second_device(other),
                    )
                sent(lambda: lane_of(layer, mat).from_second.at[pl.ds(1, lane.second - 1)])
            else:
                for other in range(lane.owners):

                    @pl.when(lane.second_me != other)
                    def _():
                        copy(
                            lane.sums.at[lane.piece_rows(other)],
                            lane.from_second.at[
                                lax.rem(lane.second_me - other + lane.second, lane.second)
                            ],
                            lane.second_device(other),
                        )
                        wait_bytes(lane.from_second.at[0], v.give_stage.at[layer, mat, stage])

        elif stage == SECOND_BACK:

            def send_all():
                rows = lane.piece_rows(lane.second_me)
                for step in range(1, lane.second):
                    copy(
                        lane.result.at[rows],
                        lane.result.at[rows],
                        lane.second_device(lax.rem(lane.second_me + step, lane.second)),
                    )

            if lane.owners == lane.second:
                send_all()
                sent(lambda: lane_of(layer, mat).from_second.at[pl.ds(1, lane.second - 1)])
            else:

                @pl.when(lane.second_me < lane.owners)
                def _():
                    send_all()
                    wait_bytes(
                        lane.from_second.at[pl.ds(1, lane.second - 1)],
                        v.give_stage.at[layer, mat, stage],
                    )

        elif stage == FIRST_BACK:
            rows = lane.share_rows(lane.first_me)
            for step in range(1, lane.first):
                copy(
                    lane.result.at[rows],
                    lane.result.at[rows],
                    lane.first_device(lax.rem(lane.first_me + step, lane.first)),
                )
            sent(lambda: lane_of(layer, mat).from_first)
        elif stage == CORE_BACK:
            copy(lane.result, lane.result, {"nodes": mate})
            sent(lambda: grads.at[layer, mat])

    def end_stage(stage, layer, mat):
        lane = lane_of(layer, mat)
        taken = v.take_stage.at[layer, mat, stage]
        if stage == CORE:
            wait_bytes(v.from_core.at[layer, mat], taken)
            v.sums[layer, mat] = v.sums[layer, mat] + v.from_core[layer, mat]
        elif stage == FIRST:
            wait_bytes(lane.from_first, taken)
            rows = lane.share_rows(lane.first_me)
            value = v.sums[layer, mat, rows, :]
            for step in range(lane.first - 1):
                value = value + lane.from_first[step]
            v.sums[layer, mat, rows, :] = value
        elif stage == SECOND:

            def add():
                wait_bytes(lane.from_second.at[pl.ds(1, lane.second - 1)], taken)
                rows = lane.piece_rows(lane.second_me)
                value = v.sums[layer, mat, rows, :]
                for step in range(1, lane.second):
                    value = value + lane.from_second[step]
                grads[layer, mat, rows, :] = value

            if lane.owners == lane.second:
                add()
            else:
                pl.when(lane.second_me < lane.owners)(add)
        elif stage == SECOND_BACK:
            if lane.owners == lane.second:
                wait_bytes(lane.from_second.at[pl.ds(1, lane.second - 1)], taken)
            else:
                if lane.owners > 1:
                    wait_bytes(lane.from_second.at[pl.ds(1, lane.owners - 1)], taken)

                @pl.when(lane.second_me >= lane.owners)
                def _():
                    wait_bytes(lane.from_second.at[0], taken)

        elif stage == FIRST_BACK:
            wait_bytes(lane.from_first, taken)
        elif stage == CORE_BACK:
            wait_bytes(grads.at[layer, mat], taken)

    def advance(*moves):
        def run(which):
            for stage, layer, mat in moves:
                if owner(layer, mat) == which:
                    end_stage(stage, layer, mat)
                    start_stage(stage + 1, layer, mat)

        for which in range(2):
            if any(owner(layer, mat) == which for _, layer, mat in moves):
                on(which, functools.partial(run, which))


    loads[1].wait()
    v.listed_row[...] = jnp.zeros_like(v.listed_row)
    v.listed_row[0:1, : z.listed] = v.listed_in[pl.ds(sec, 1), :].astype(F32)
    spread_from = iota((v.listed_row.shape[1], z.halo_pad), 0)
    spread_to = iota((v.listed_row.shape[1], z.halo_pad), 1)
    spread = as_ones(
        (lax.div(spread_from, z.send) == lax.div(spread_to, TILE))
        & (lax.rem(spread_from, z.send) == lax.rem(spread_to, TILE))
        & (spread_from < z.listed)
    )
    listed = mm(v.listed_row[...].astype(BF16), spread)[0:1, :]
    place = iota((1, z.halo_pad), 1)
    real = (lax.rem(place, TILE) < z.send) & (place < z.halo)
    listed = jnp.where(real, listed, -1.0)
    list_t = jnp.where(iota((R, z.halo_pad), 0).astype(F32) == listed, 1.0, 0.0)
    v.list_t[...] = list_t.astype(BF16)
    v.list[...] = list_t.T[: z.halo, :].astype(BF16)

    loads[0].wait()
    own = v.features_in[...]
    v.h[pl.ds(0, R), :] = own
    high, low = halves(own)
    v.h_hi[pl.ds(0, R), :] = high
    v.h_lo[pl.ds(0, R), :] = low
    v.outgoing[FEATURES] = mm(v.list[...], high) + mm(v.list[...], low)
    pl.semaphore_wait(barrier, N - 1 + S - 1)
    start_exchange(FEATURES)

    for load in loads[2:5]:
        load.wait()
    for layer in range(2):
        for mat in range(3):
            high, low = halves(v.weights_in[mat, layer])
            v.weights_hi[layer, mat] = high
            v.weights_lo[layer, mat] = low

    def weight(layer, mat):
        return v.weights_hi[layer, mat], v.weights_lo[layer, mat]

    for load in loads[5:11]:
        load.wait()
    named = v.slots_in[...]
    offset = named - R
    remote = R + lax.div(offset, z.send) * TILE + lax.rem(offset, z.send)
    named = jnp.where(named < R, named, remote).astype(F32)
    v.prep[...] = jnp.zeros_like(v.prep)
    v.prep[pl.ds(0, K), :] = named
    v.prep[pl.ds(K, 1), :] = v.degree_in[pl.ds(sec, 1), :].astype(F32)
    v.prep[pl.ds(K + 1, 1), :] = v.mask_in[pl.ds(sec, 1), :].astype(F32)
    v.prep_t[...] = v.prep[...].T
    for slot in range(1, K):
        column = v.prep_t[:, slot : slot + 1]
        pick = as_ones(iota((R, T), 1).astype(F32) == column)
        v.pick[slot - 1, :, pl.ds(0, T)] = pick
        v.pick[slot - 1, :, pl.ds(T, z.halo_pad)] = pick[:, R:]
        row = v.prep[slot : slot + 1, :]
        v.pick_t[:, (slot - 1) * R : slot * R] = as_ones(iota((z.picked, R), 0).astype(F32) == row)
    block_row = lax.div(lax.rem(iota((2 * D, D), 0), D), GROUP)
    v.ones[...] = as_ones(block_row == lax.div(iota((2 * D, D), 1), GROUP))

    def project(layer):
        rows = pl.ds(0, R)
        own = (v.h_hi[rows, :], v.h_lo[rows, :])
        left = mm3(own, weight(layer, 0))
        v.taken[layer, 0] = left
        high, low = halves(left)
        v.table_hi[rows, :] = high
        v.table_lo[rows, :] = low
        v.right[layer] = mm3(own, weight(layer, 1))
        v.skip[...] = mm3(own, weight(layer, 2))

    def project_halo(layer):
        rows = pl.ds(R, z.halo_pad)
        left = mm3((v.h_hi[rows, :], v.h_lo[rows, :]), weight(layer, 0))
        high, low = halves(left)
        v.halo_table[pl.ds(0, z.halo_pad), :] = high
        v.halo_table[pl.ds(z.halo_pad, z.halo_pad), :] = low

    def store_halo(values):
        if z.halo < z.halo_pad:
            rest = pl.ds(R + z.halo, z.halo_pad - z.halo)
            v.h[rest, :] = jnp.zeros((z.halo_pad - z.halo, D), F32)
            v.h_hi[rest, :] = jnp.zeros((z.halo_pad - z.halo, D), BF16)
            v.h_lo[rest, :] = jnp.zeros((z.halo_pad - z.halo, D), BF16)
        rows = pl.ds(R, z.halo)
        v.h[rows, :] = values
        high, low = halves(values)
        v.h_hi[rows, :] = high
        v.h_lo[rows, :] = low

    def keep_transposed(layer):
        high, low = halves(v.h[...].T)
        v.ht_hi[layer] = high
        v.ht_lo[layer] = low

    def store_pair(slot, rows, values):
        high, low = halves(values)
        v.pair[slot, rows, pl.ds(0, D)] = high
        v.pair[slot, rows, pl.ds(D, D)] = low

    def gather_own(layer):
        def one(slot, carry):
            pick = v.pick[slot - 1, :, pl.ds(0, R)]
            v.taken[layer, slot] = mm(pick, v.table_hi[...]) + mm(pick, v.table_lo[...])
            return carry

        lax.fori_loop(1, K, one, 0, unroll=True)

    def head_sum(slot):
        v.score[slot] = mm(v.pair[slot], v.ones[...])

    def attend(layer):
        vector = v.vector_in[layer : layer + 1, :]

        def gather(slot):
            pick = v.pick[slot - 1, :, pl.ds(R, 2 * z.halo_pad)]
            value = mm(pick, v.halo_table[...])
            if layer == 0:
                value = v.taken[layer, slot] + value
            else:
                pick = v.pick[slot - 1, :, pl.ds(0, R)]
                value = mm(pick, v.table_hi[...]) + mm(pick, v.table_lo[...]) + value
            v.taken[layer, slot] = value

        def activate(slot):
            for place in range(0, R, BLOCK):
                rows = pl.ds(place, BLOCK)
                u = v.taken[layer, slot, rows, :] + v.right[layer, rows, :]
                store_pair(slot, rows, u * sigmoid(u) * vector)

        for slot in range(1, K + 3):
            if slot < K:
                gather(slot)
            if slot <= K:
                activate(slot - 1)
            if slot >= 3:
                head_sum(slot - 3)

        def mix(i, carry):
            rows = chunk(i)
            count = jnp.broadcast_to(v.prep_t[rows, K : K + 1], (CHUNK, D))
            scores = [
                jnp.where(count > slot, v.score[slot, rows, :], MASKED_SCORE) for slot in range(K)
            ]
            highest = functools.reduce(jnp.maximum, scores)
            powers = [jnp.exp(score - highest) for score in scores]
            scale = 1.0 / functools.reduce(jnp.add, powers)
            joined = jnp.zeros((CHUNK, D), F32)
            for slot in range(K):
                alpha = powers[slot] * scale
                v.alpha[layer, slot, rows, :] = alpha
                joined = joined + alpha * v.taken[layer, slot, rows, :]
            v.joined[layer, rows, :] = joined
            mixed = joined + v.skip[rows, :]
            v.mixed[rows, :] = mixed
            return carry[0] + fold(mixed), carry[1] + fold(mixed * mixed)

        nothing = jnp.zeros((TILE, D), F32)
        first, second = rows_loop(mix, (nothing, nothing))
        return add_rows(first), add_rows(second)

    def derive(layer):
        vector = v.vector_in[layer : layer + 1, :]

        def one(i, carry):
            rows = chunk(i)
            right = v.right[layer, rows, :]
            for slot in range(K):
                u = v.taken[layer, slot, rows, :] + right
                sig = sigmoid(u)
                act = u * sig
                v.act[layer, slot, rows, :] = act
                v.rise[layer, slot, rows, :] = vector * (sig + act * (1.0 - sig))
            return carry

        rows_loop(one, 0)

    def moments(which):
        first, second = arrived_sums(which)
        mean = first / total_rows
        return mean, lax.rsqrt(second / total_rows - mean * mean + VARIANCE_EPS)

    def activation(layer, mixed, mean, inverse):
        normed = (mixed - mean) * inverse
        pre = v.gain_in[layer : layer + 1, :] * normed + v.shift_in[layer : layer + 1, :]
        power = jnp.exp(jnp.minimum(pre, 0.0))
        return normed, jnp.where(pre > 0, 1.0, power), jnp.where(pre > 0, pre, power - 1.0)

    def sums_tile(which, first, second):
        v.outgoing[which, pl.ds(0, TILE), :] = with_sums(jnp.zeros((TILE, D), F32), first, second)

    def list_rows(values):
        high, low = halves(values)
        return mm(v.list[...], high) + mm(v.list[...], low)

    project(0)
    gather_own(0)
    end_exchange(FEATURES)
    store_halo(arrived_rows(FEATURES))
    project_halo(0)
    first, second = attend(0)
    v.outgoing[MIXED] = with_sums(list_rows(v.mixed[...]), first, second)
    start_exchange(MIXED)
    keep_transposed(0)
    derive(0)
    end_exchange(MIXED)
    mean0, inverse0 = moments(MIXED)

    def finish0(i, carry):
        rows = chunk(i)
        normed, slope, hidden = activation(0, v.mixed[rows, :], mean0, inverse0)
        v.normed[0, rows, :] = normed
        v.slope[0, rows, :] = slope
        v.h[rows, :] = hidden
        high, low = halves(hidden)
        v.h_hi[rows, :] = high
        v.h_lo[rows, :] = low
        return carry

    rows_loop(finish0, 0)
    normed, slope, hidden = activation(0, arrived_rows(MIXED), mean0, inverse0)
    v.halo_normed[...] = normed
    v.halo_slope[...] = slope
    store_halo(jnp.where(row_in_tile(z.halo) < z.send, hidden, 0.0))

    project(1)
    project_halo(1)
    first, second = attend(1)
    sums_tile(SUMS, first, second)
    start_exchange(SUMS, True)
    keep_transposed(1)
    derive(1)
    loads[11].wait()
    end_exchange(SUMS)
    mean1, inverse1 = moments(SUMS)

    def finish1(i, carry):
        rows = chunk(i)
        normed, slope, hidden = activation(1, v.mixed[rows, :], mean1, inverse1)
        v.normed[1, rows, :] = normed
        out[0, rows, :] = hidden
        dpre = v.cotangent_in[rows, :] * v.prep_t[rows, K + 1 : K + 2] * slope
        v.dpre[rows, :] = dpre
        return carry[0] + fold(dpre), carry[1] + fold(dpre * normed)

    nothing = jnp.zeros((TILE, D), F32)
    first, second = rows_loop(finish1, (nothing, nothing))
    shift1, gain1 = add_rows(first), add_rows(second)
    sums_tile(BACK_SUMS, shift1, gain1)
    start_exchange(BACK_SUMS, True)

    def normalization_back(layer, which, inverse):
        first, second = arrived_sums(which)
        first = first / total_rows
        second = second / total_rows
        scale = inverse * v.gain_in[layer : layer + 1, :]

        def one(i, carry):
            rows = chunk(i)
            dmixed = scale * (v.dpre[rows, :] - first - v.normed[layer, rows, :] * second)
            v.dmixed[rows, :] = dmixed
            high, low = halves(dmixed)
            v.dm_hi[rows, :] = high
            v.dm_lo[rows, :] = low
            return carry

        rows_loop(one, 0)

    def attend_back(layer, between=None):
        def differences(slot):
            for place in range(0, R, BLOCK):
                rows = pl.ds(place, BLOCK)
                value = (v.taken[layer, slot, rows, :] - v.joined[layer, rows, :]) * v.dmixed[rows, :]
                store_pair(slot, rows, value)

        weight_grad(layer, 2)
        for slot in range(K + 1):
            if slot < K:
                differences(slot)
            if slot >= 1:
                head_sum(slot - 1)
        start_core(layer, 2)

        def one(i, carry):
            rows = chunk(i)
            dmixed = v.dmixed[rows, :]
            dright = jnp.zeros((CHUNK, D), F32)
            for slot in range(K):
                alpha = v.alpha[layer, slot, rows, :]
                dscore = alpha * v.score[slot, rows, :]
                carry = carry + fold(dscore * v.act[layer, slot, rows, :])
                du = dscore * v.rise[layer, slot, rows, :]
                dright = dright + du
                dleft = du + alpha * dmixed
                if slot == 0:
                    v.dleft_self[rows, :] = dleft
                else:
                    high, low = halves(dleft)
                    place = pl.ds(pl.multiple_of((slot - 1) * R + i * CHUNK, CHUNK), CHUNK)
                    v.dleft_hi[place, :] = high
                    v.dleft_lo[place, :] = low
            high, low = halves(dright)
            v.dr_hi[rows, :] = high
            v.dr_lo[rows, :] = low
            return carry

        vector_sum = rows_loop(one, jnp.zeros((TILE, D), F32))
        if between is not None:
            between()

        def scattered(rows):
            pick = v.pick_t[rows, :]
            return mm(pick, v.dleft_hi[...]) + mm(pick, v.dleft_lo[...])

        rows = pl.ds(0, R)
        own = scattered(rows) + v.dleft_self[...]
        v.dleft_self[...] = own
        high, low = halves(own)
        v.dl_hi[rows, :] = high
        v.dl_lo[rows, :] = low
        rows = pl.ds(R, z.halo)
        halo = scattered(rows)
        if layer == 0:
            start_return(halo)
        high, low = halves(halo)
        v.dl_hi[rows, :] = high
        v.dl_lo[rows, :] = low
        return add_rows(vector_sum)

    def start_return(halo):
        v.returning[...] = halo[:, :LANES] + pltpu.roll(halo[:, LANES:], z.send, 0)
        own = pl.ds(pl.multiple_of(me * TILE, TILE), TILE)

        def send(step, carry):
            other = lax.rem(me + side * step + N, N)
            pltpu.make_async_remote_copy(
                src_ref=v.returning.at[pl.ds(pl.multiple_of(other * TILE, TILE), TILE)],
                dst_ref=v.returned.at[own],
                send_sem=v.give_rows.at[0],
                recv_sem=v.take_rows.at[0],
                device_id={"nodes": other},
                device_id_type=MESH,
            ).start()
            return carry

        lax.fori_loop(1, N, send, 0)
        v.returned[own, :] = v.returning[own, :]

    def dleft(rows):
        return v.dl_hi[rows, :], v.dl_lo[rows, :]

    def input_back(layer):
        own = pl.ds(0, R)
        v.dh[...] = (
            mm3(dleft(own), weight(layer, 0), mm_nt)
            + mm3((v.dr_hi[...], v.dr_lo[...]), weight(layer, 1), mm_nt)
            + mm3((v.dm_hi[...], v.dm_lo[...]), weight(layer, 2), mm_nt)
        )
        return mm3(dleft(pl.ds(R, z.halo)), weight(layer, 0), mm_nt)

    def weight_grad(layer, mat):
        if mat == 0:
            upstream = (v.dl_hi[...], v.dl_lo[...])
            inputs = (v.ht_hi[layer], v.ht_lo[layer])
        else:
            upstream = (v.dr_hi[...], v.dr_lo[...]) if mat == 1 else (v.dm_hi[...], v.dm_lo[...])
            inputs = (v.ht_hi[layer, :, pl.ds(0, R)], v.ht_lo[layer, :, pl.ds(0, R)])
        v.sums[layer, mat] = mm3(inputs, upstream)

    if z.halo < z.halo_pad:
        rest = pl.ds(R + z.halo, z.halo_pad - z.halo)
        v.dl_hi[rest, :] = jnp.zeros((z.halo_pad - z.halo, D), BF16)
        v.dl_lo[rest, :] = jnp.zeros((z.halo_pad - z.halo, D), BF16)

    end_exchange(BACK_SUMS)
    normalization_back(1, BACK_SUMS, inverse1)
    vector1 = attend_back(1)
    halo_back = input_back(1)
    dpre = v.dh[...] * v.slope[0]
    halo_dpre = halo_back * v.halo_slope[...]
    shift0 = add_rows(dpre) + add_rows(halo_dpre)
    gain0 = add_rows(dpre * v.normed[0]) + add_rows(halo_dpre * v.halo_normed[...])
    v.outgoing[BACK_ROWS] = with_sums(halo_back, shift0, gain0)
    start_exchange(BACK_ROWS)
    advance((CORE, 1, 2))
    weight_grad(1, 1)
    start_core(1, 1)
    weight_grad(1, 0)
    start_core(1, 0)
    advance((CORE, 1, 1), (CORE, 1, 0))
    end_exchange(BACK_ROWS)
    v.dpre[...] = (v.dh[...] + give_rows_back(BACK_ROWS)) * v.slope[0]

    normalization_back(0, BACK_ROWS, inverse0)

    def between():
        weight_grad(0, 1)
        start_core(0, 1)
        advance(*BETWEEN)

    vector0 = attend_back(0, between)
    weight_grad(0, 0)
    start_core(0, 0)

    row = iota((TILE, D), 0)
    tile = jnp.zeros((TILE, D), F32)
    for place, value in enumerate((vector0, vector1, gain0, gain1, shift0, shift1)):
        tile = jnp.where(row == place, value, tile)
    v.small[0] = tile

    def send_small(stage, source, target, device):
        pltpu.make_async_remote_copy(
            src_ref=source,
            dst_ref=target,
            send_sem=v.give_small.at[stage],
            recv_sem=v.take_small.at[stage],
            device_id=device,
            device_id_type=MESH,
        ).start()

    on(0, lambda: send_small(0, v.small.at[0], v.small_core.at[0], {"nodes": mate}))

    def small_outer():
        wait_bytes(v.small_core.at[0], v.take_small.at[0])
        value = v.small[0] + v.small_core[0]
        v.small[1] = value
        v.small_outer[outer] = value
        for step in range(1, O):
            send_small(
                1, v.small.at[1], v.small_outer.at[outer], {"nodes": lax.rem(outer + step, O) * 2 + core}
            )

    def small_section():
        wait_bytes(v.small_outer.at[pl.ds(1, O - 1)], v.take_small.at[1])
        value = jnp.sum(v.small_outer[...], axis=0)
        v.small[2] = value
        v.small_section[sec] = value
        for step in range(1, S):
            send_small(
                2, v.small.at[2], v.small_section.at[sec], {"section": lax.rem(sec + step, S)}
            )

    def put_small(value):
        g_vec[...] = value[0:2, :]
        g_gain[...] = value[2:4, :]
        g_shift[...] = value[4:6, :]

    def small_back():
        wait_bytes(v.small_section.at[pl.ds(1, S - 1)], v.take_small.at[2])
        value = jnp.sum(v.small_section[...], axis=0)
        v.small[3] = value
        send_small(3, v.small.at[3], v.small_core.at[1], {"nodes": mate})
        put_small(value)

    def small_end():
        wait_bytes(v.small_core.at[1], v.take_small.at[3])
        put_small(v.small_core[1])

    advance(*AFTER)
    def part_input():
        v.dh[...] = mm3((v.dr_hi[...], v.dr_lo[...]), weight(0, 1), mm_nt) + mm3(
            (v.dm_hi[...], v.dm_lo[...]), weight(0, 2), mm_nt
        )

    def store_input():
        wait_bytes(v.returned.at[pl.ds(0, (N - 1) * TILE)], v.take_rows.at[0])
        values = v.returned[...]
        values = jnp.concatenate([values, pltpu.roll(values, z.halo - z.send, 0)], axis=1)
        high, low = halves(jnp.where(row_in_tile(z.halo) < z.send, values, 0.0))
        listed = v.list_t[:, : z.halo]
        left = v.dleft_self[...] + (mm(listed, high) + mm(listed, low))
        grad_in[0] = v.dh[...] + mm3(halves(left), weight(0, 0), mm_nt)

    steps = {
        "outer": small_outer,
        "section": small_section,
        "back": small_back,
        "end": small_end,
        "part": part_input,
        "input": store_input,
    }

    def finish(which):
        for step in TAILS[which]:
            if isinstance(step, str):
                steps[step]()
            else:
                end_stage(*step)
                start_stage(step[0] + 1, *step[1:])

    on(0, lambda: finish(0))
    on(1, lambda: finish(1))

    def receive(which):
        for layer in (1, 0):
            for mat in (2, 1, 0):
                if owner(layer, mat) != which:
                    end_stage(CORE_BACK, layer, mat)

    for which in range(EXCHANGES):
        wait_bytes(v.outgoing.at[which, pl.ds(0, (N - 1) * TILE)], v.give.at[which])
    wait_bytes(v.returned.at[pl.ds(0, (N - 1) * TILE)], v.give_rows.at[0])

    def sent(which):
        for ref, semaphore, sender in sends_to_end:
            if sender == which:
                wait_bytes(ref(), semaphore())

    def sent_small(stage, count):
        wait_bytes(v.small_outer.at[pl.ds(0, count)], v.give_small.at[stage])

    def sent0():
        sent(0)
        sent_small(0, 1)
        receive(0)

    def sent1():
        sent(1)
        sent_small(1, O - 1)
        wait_bytes(v.small_section.at[pl.ds(1, S - 1)], v.give_small.at[2])
        sent_small(3, 1)
        receive(1)

    on(0, sent0)
    on(1, sent1)


def store_kernel(*refs):
    out, grad_in, grads, g_vec, g_gain, g_shift = refs[:6]
    pairs = [(out, refs[6]), (grad_in, refs[7])]
    for mat in range(3):
        pairs += [(grads.at[layer, mat], refs[8 + mat].at[layer]) for layer in range(2)]
    pairs += [(g_vec, refs[11]), (g_gain, refs[12]), (g_shift, refs[13])]
    copies = [pltpu.make_async_copy(*pair, refs[14].at[i]) for i, pair in enumerate(pairs)]
    for copy in copies:
        copy.start()
    for copy in copies:
        copy.wait()


def body(
    features,
    cotangent,
    train_mask,
    degree,
    neighbours,
    send_rows,
    w_left,
    w_right,
    w_res,
    attn_vec,
    bn_gain,
    bn_shift,
):
    batches, rows, width = features.shape
    sections = lax.axis_size("section")
    assert batches == sections and width == HEADS * GROUP
    z = sizes_of(
        sections, lax.axis_size("nodes"), rows, width, neighbours.shape[2], send_rows.shape[1]
    )
    shapes = scratch_of(z)
    shapes["mask_in"] = (train_mask.shape, jnp.int32)
    shapes["degree_in"] = (degree.shape, jnp.int32)
    shapes["listed_in"] = (send_rows.shape, jnp.int32)
    scratch = [pltpu.VMEM(shape, dtype) for shape, dtype in shapes.values()]
    scratch += [pltpu.SemaphoreType.DMA(shape) for shape in SEMAPHORES.values()]
    names = list(shapes) + list(SEMAPHORES)
    anywhere = pl.BlockSpec(memory_space=pl.ANY)
    square = jax.ShapeDtypeStruct((2, width, width), F32)
    columns = jax.ShapeDtypeStruct((2, width), F32)
    block = jax.ShapeDtypeStruct((1, rows, width), F32)
    results = (block, block, square, square, square, columns, columns, columns)
    in_vmem = pl.BlockSpec(memory_space=pltpu.VMEM)
    squares = jax.ShapeDtypeStruct((2, 3, width, width), F32)
    kept = (block, block, squares, columns, columns, columns)
    found = pl.pallas_call(
        functools.partial(kernel, z, names),
        out_shape=tuple(pltpu.VMEM(x.shape, x.dtype) for x in kept),
        in_specs=[pl.BlockSpec(memory_space=pltpu.HBM)] * 12,
        out_specs=(in_vmem,) * 6,
        scratch_shapes=scratch,
        compiler_params=pltpu.CompilerParams(
            collective_id=0, has_side_effects=True, vmem_limit_bytes=60 * 1024 * 1024
        ),
    )(
        features,
        cotangent,
        train_mask,
        degree,
        jnp.transpose(neighbours, (0, 2, 1)),
        send_rows,
        w_left,
        w_right,
        w_res,
        attn_vec,
        bn_gain,
        bn_shift,
    )
    return pl.pallas_call(
        store_kernel,
        out_shape=results,
        in_specs=[anywhere] * 6,
        out_specs=(anywhere,) * 8,
        scratch_shapes=[pltpu.SemaphoreType.DMA((11,))],
        compiler_params=pltpu.CompilerParams(vmem_limit_bytes=1024 * 1024),
    )(*found)


def solution(mesh):
    return jax.shard_map(
        body,
        mesh=mesh,
        in_specs=(
            P(None, "nodes", None),
            P(None, "nodes", None),
            P(None, "nodes"),
            P(None, "nodes"),
            P(None, "nodes", None),
            P(None, "nodes"),
            P(),
            P(),
            P(),
            P(),
            P(),
            P(),
        ),
        out_specs=(
            P("section", "nodes", None),
            P("section", "nodes", None),
            P(),
            P(),
            P(),
            P(),
            P(),
            P(),
        ),
        check_vma=False,
    )
```

```python
import functools
import types

import jax
import jax.numpy as jnp
from jax import lax
from jax.experimental import pallas as pl
from jax.experimental.pallas import tpu as pltpu
from jax.sharding import PartitionSpec as P

HEADS = 4
MASKED_SCORE = -1e30
VARIANCE_EPS = 1e-05
F32 = jnp.float32
BF16 = jnp.bfloat16
MESH = pl.DeviceIdType.MESH
UNROLL = 16
BLOCK = 32
OUTER_FIRST = ()
LANES = 128
GROUP = 64
TILE = 8
CHUNK = 16

FEATURES, MIXED, SUMS, BACK_SUMS, BACK_ROWS = range(5)
EXCHANGES = 5
CORE, FIRST, SECOND, SECOND_BACK, FIRST_BACK, CORE_BACK = range(6)
STAGES = 6
ON_CORE_0 = ((1, 2), (1, 1))
BETWEEN = ((FIRST, 1, 2), (FIRST, 1, 0), (CORE, 0, 2))
AFTER = ((FIRST, 1, 1), (CORE, 0, 1))
TAILS = (
    (
        (SECOND, 1, 2),
        (SECOND, 1, 1),
        (SECOND_BACK, 1, 2),
        (SECOND_BACK, 1, 1),
        (FIRST_BACK, 1, 2),
        (FIRST_BACK, 1, 1),
        "part",
        "input",
        "end",
    ),
    (
        (CORE, 0, 0),
        (SECOND, 1, 0),
        (FIRST, 0, 2),
        "outer",
        (FIRST, 0, 1),
        (FIRST, 0, 0),
        (SECOND_BACK, 1, 0),
        (SECOND, 0, 2),
        (SECOND, 0, 1),
        "section",
        (SECOND, 0, 0),
        (FIRST_BACK, 1, 0),
        (SECOND_BACK, 0, 2),
        (SECOND_BACK, 0, 1),
        "back",
        (SECOND_BACK, 0, 0),
        (FIRST_BACK, 0, 2),
        (FIRST_BACK, 0, 1),
        (FIRST_BACK, 0, 0),
        "part",
        "input",
    ),
)


def halves(values):
    high = values.astype(BF16)
    return high, (values - high.astype(F32)).astype(BF16)


def mm(lhs, rhs):
    return jnp.dot(lhs, rhs, preferred_element_type=F32)


def mm_nt(lhs, rhs):
    return lax.dot_general(lhs, rhs, (((1,), (1,)), ((), ())), preferred_element_type=F32)


def mm3(lhs, rhs, product=mm):
    return product(lhs[0], rhs[0]) + product(lhs[1], rhs[0]) + product(lhs[0], rhs[1])


def iota(shape, dim):
    return lax.broadcasted_iota(jnp.int32, shape, dim)


def sigmoid(u):
    return 0.5 * jnp.tanh(0.5 * u) + 0.5


def as_ones(condition):
    return jnp.where(condition, 1.0, 0.0).astype(BF16)


def sizes_of(sections, partitions, rows, width, slots, listed):
    z = types.SimpleNamespace()
    z.sections, z.partitions, z.outer = sections, partitions, partitions // 2
    z.rows, z.width, z.slots, z.listed = rows, width, slots, listed
    z.send = listed // partitions
    z.halo = partitions * TILE
    z.halo_pad = -(-z.halo // LANES) * LANES
    z.table = rows + z.halo_pad
    z.picked = rows + z.halo
    return z


def shares_of(rows, first, second):
    share = rows // first
    piece = max(TILE, share // second)
    return share, piece, share // piece


def scratch_of(z):
    R, D, K, T = z.rows, z.width, z.slots, z.table
    S, O = z.sections, z.outer
    vmem = {
        "features_in": ((R, D), F32),
        "cotangent_in": ((R, D), F32),
        "mask_in": (None, jnp.int32),
        "degree_in": (None, jnp.int32),
        "slots_in": ((K, R), jnp.int32),
        "listed_in": (None, jnp.int32),
        "weights_in": ((3, 2, D, D), F32),
        "vector_in": ((2, D), F32),
        "gain_in": ((2, D), F32),
        "shift_in": ((2, D), F32),
        "weights_hi": ((2, 3, D, D), BF16),
        "weights_lo": ((2, 3, D, D), BF16),
        "prep": ((LANES, R), F32),
        "prep_t": ((R, LANES), F32),
        "listed_row": ((TILE, max(LANES, z.listed)), F32),
        "pick": ((K - 1, R, R + 2 * z.halo_pad), BF16),
        "pick_t": ((z.picked, (K - 1) * R), BF16),
        "list": ((z.halo, R), BF16),
        "list_t": ((R, z.halo_pad), BF16),
        "ones": ((2 * D, D), BF16),
        "h": ((T, D), F32),
        "h_hi": ((T, D), BF16),
        "h_lo": ((T, D), BF16),
        "ht_hi": ((2, D, T), BF16),
        "ht_lo": ((2, D, T), BF16),
        "table_hi": ((R, D), BF16),
        "table_lo": ((R, D), BF16),
        "halo_table": ((2 * z.halo_pad, D), BF16),
        "taken": ((2, K, R, D), F32),
        "act": ((2, K, R, D), F32),
        "rise": ((2, K, R, D), F32),
        "alpha": ((2, K, R, D), F32),
        "joined": ((2, R, D), F32),
        "right": ((2, R, D), F32),
        "skip": ((R, D), F32),
        "mixed": ((R, D), F32),
        "normed": ((2, R, D), F32),
        "slope": ((2, R, D), F32),
        "halo_normed": ((z.halo, D), F32),
        "halo_slope": ((z.halo, D), F32),
        "pair": ((K, R, 2 * D), BF16),
        "score": ((K, R, D), F32),
        "dpre": ((R, D), F32),
        "dmixed": ((R, D), F32),
        "dm_hi": ((R, D), BF16),
        "dm_lo": ((R, D), BF16),
        "dr_hi": ((R, D), BF16),
        "dr_lo": ((R, D), BF16),
        "dl_hi": ((T, D), BF16),
        "dl_lo": ((T, D), BF16),
        "dleft_self": ((R, D), F32),
        "dleft_hi": (((K - 1) * R, D), BF16),
        "dleft_lo": (((K - 1) * R, D), BF16),
        "dh": ((R, D), F32),
        "outgoing": ((EXCHANGES, z.halo, D), F32),
        "incoming": ((EXCHANGES, z.halo, D), F32),
        "small": ((4, TILE, D), F32),
        "small_core": ((2, TILE, D), F32),
        "small_outer": ((O, TILE, D), F32),
        "small_section": ((S, TILE, D), F32),
        "returning": ((z.halo, LANES), F32),
        "returned": ((z.halo, LANES), F32),
        "sums": ((2, 3, R, D), F32),
        "from_core": ((2, 3, R, D), F32),
    }
    for layer in range(2):
        for mat in range(3):
            first, second = (O, S) if (layer, mat) in OUTER_FIRST else (S, O)
            share, piece, _ = shares_of(R, first, second)
            vmem[f"first_{layer}{mat}"] = ((first - 1, share, D), F32)
            vmem[f"second_{layer}{mat}"] = ((second, piece, D), F32)
    return vmem


SEMAPHORES = {
    "load": (12,),
    "give": (EXCHANGES,),
    "take": (EXCHANGES,),
    "give_small": (4,),
    "take_small": (4,),
    "give_rows": (1,),
    "take_rows": (1,),
    "give_stage": (2, 3, STAGES),
    "take_stage": (2, 3, STAGES),
}


def kernel(z, names, *refs):
    features, cotangent, train_mask, degree, neighbours, send_rows = refs[:6]
    w_left, w_right, w_res, attn_vec, bn_gain, bn_shift = refs[6:12]
    out, grad_in, grads, g_vec, g_gain, g_shift = refs[12:18]
    v = types.SimpleNamespace(**dict(zip(names, refs[18:])))
    R, D, K, T = z.rows, z.width, z.slots, z.table
    S, N, O = z.sections, z.partitions, z.outer
    total_rows = R * N
    sec = lax.axis_index("section")
    me = lax.axis_index("nodes")
    core = lax.rem(me, 2)
    outer = lax.div(me, 2)
    mate = me + 1 - 2 * core
    side = 2 * lax.div(2 * me, N) - 1

    barrier = pltpu.get_barrier_semaphore()

    def greet(step, carry):
        pl.semaphore_signal(
            barrier, inc=1, device_id={"nodes": lax.rem(me + side * step + N, N)}, device_id_type=MESH
        )
        return carry

    lax.fori_loop(1, N, greet, 0)
    for step in range(1, S):
        pl.semaphore_signal(
            barrier, inc=1, device_id={"section": lax.rem(sec + step, S)}, device_id_type=MESH
        )

    loads = []
    for source, target in (
        (features.at[sec], v.features_in),
        (send_rows, v.listed_in),
        (w_left, v.weights_in.at[0]),
        (w_right, v.weights_in.at[1]),
        (w_res, v.weights_in.at[2]),
        (neighbours.at[sec], v.slots_in),
        (degree, v.degree_in),
        (train_mask, v.mask_in),
        (attn_vec, v.vector_in),
        (bn_gain, v.gain_in),
        (bn_shift, v.shift_in),
        (cotangent.at[sec], v.cotangent_in),
    ):
        copy = pltpu.make_async_copy(source, target, v.load.at[len(loads)])
        copy.start()
        loads.append(copy)

    def rows_loop(body, start):
        return lax.fori_loop(0, R // CHUNK, body, start, unroll=UNROLL)

    def chunk(i):
        return pl.ds(pl.multiple_of(i * CHUNK, CHUNK), CHUNK)

    def fold(values):
        return jnp.sum(values.reshape(values.shape[0] // TILE, TILE, values.shape[1]), axis=0)

    def add_rows(values):
        return jnp.sum(values, axis=0, keepdims=True)


    def start_exchange(which, one_tile=False):
        def send(step, carry):
            other = lax.rem(me + side * step + N, N)
            place = 0 if one_tile else pl.multiple_of(other * TILE, TILE)
            pltpu.make_async_remote_copy(
                src_ref=v.outgoing.at[which, pl.ds(place, TILE)],
                dst_ref=v.incoming.at[which, pl.ds(pl.multiple_of(me * TILE, TILE), TILE)],
                send_sem=v.give.at[which],
                recv_sem=v.take.at[which],
                device_id={"nodes": other},
                device_id_type=MESH,
            ).start()
            return carry

        lax.fori_loop(1, N, send, 0)
        own = pl.ds(pl.multiple_of(me * TILE, TILE), TILE)
        mine = pl.ds(0, TILE) if one_tile else own
        v.incoming[which, own, :] = v.outgoing[which, mine, :]

    def wait_bytes(ref, semaphore):
        pltpu.make_async_copy(ref, ref, semaphore).wait()

    def end_exchange(which):
        wait_exchange(which)

    def wait_exchange(which):
        wait_bytes(v.incoming.at[which, pl.ds(0, (N - 1) * TILE)], v.take.at[which])

    def row_in_tile(rows):
        return lax.rem(iota((rows, D), 0), TILE)

    def with_sums(values, first, second):
        row = row_in_tile(values.shape[0])
        return values + jnp.where(row == z.send, first, 0.0) + jnp.where(row == z.send + 1, second, 0.0)

    def arrived_sums(which):
        tile = jnp.sum(v.incoming[which].reshape(N, TILE, D), axis=0)
        return tile[z.send : z.send + 1, :], tile[z.send + 1 : z.send + 2, :]

    def arrived_rows(which):
        values = v.incoming[which]
        return jnp.where(row_in_tile(z.halo) < z.send, values, 0.0)

    def give_rows_back(which):
        high, low = halves(arrived_rows(which))
        listed = v.list_t[:, : z.halo]
        return mm(listed, high) + mm(listed, low)

    def owner(layer, mat):
        return 0 if (layer, mat) in ON_CORE_0 else 1

    sends_to_end = []

    def on(which, body):
        pl.when(core == which)(body)

    def stage_copy(layer, first, stage, source, target, device):
        pltpu.make_async_remote_copy(
            src_ref=source,
            dst_ref=target,
            send_sem=v.give_stage.at[layer, first, stage],
            recv_sem=v.take_stage.at[layer, first, stage],
            device_id=device,
            device_id_type=MESH,
        ).start()

    def stage_sent(layer, first, stage, ref, which):
        sends_to_end.append((ref, lambda: v.give_stage.at[layer, first, stage], which))

    def lane_of(layer, mat):
        lane = types.SimpleNamespace()
        over_section = (S, sec, lambda which: {"section": which})
        over_outer = (O, outer, lambda which: {"nodes": which * 2 + core})
        axes = (over_outer, over_section) if (layer, mat) in OUTER_FIRST else (over_section, over_outer)
        (lane.first, lane.first_me, lane.first_device), (lane.second, lane.second_me, lane.second_device) = axes
        lane.share, lane.piece, lane.owners = shares_of(R, lane.first, lane.second)
        lane.sums = v.sums.at[layer, mat]
        lane.result = grads.at[layer, mat]
        lane.from_first = getattr(v, f"first_{layer}{mat}")
        lane.from_second = getattr(v, f"second_{layer}{mat}")
        lane.share_rows = lambda which: pl.ds(pl.multiple_of(which * lane.share, TILE), lane.share)
        lane.piece_rows = lambda which: pl.ds(
            pl.multiple_of(lane.first_me * lane.share + which * lane.piece, TILE), lane.piece
        )
        return lane

    def start_core(layer, mat):
        on(
            1 - owner(layer, mat),
            lambda: stage_copy(
                layer, mat, CORE, v.sums.at[layer, mat], v.from_core.at[layer, mat], {"nodes": mate}
            ),
        )
        stage_sent(layer, mat, CORE, lambda: v.from_core.at[layer, mat], 1 - owner(layer, mat))

    def start_stage(stage, layer, mat):
        lane = lane_of(layer, mat)
        copy = functools.partial(stage_copy, layer, mat, stage)

        def sent(ref):
            stage_sent(layer, mat, stage, ref, owner(layer, mat))

        if stage == FIRST:
            for step in range(1, lane.first):
                other = lax.rem(lane.first_me + step, lane.first)
                copy(
                    lane.sums.at[lane.share_rows(other)],
                    lane.from_first.at[step - 1],
                    lane.first_device(other),
                )
            sent(lambda: lane_of(layer, mat).from_first)
        elif stage == SECOND:
            if lane.owners == lane.second:
                for step in range(1, lane.second):
                    other = lax.rem(lane.second_me + step, lane.second)
                    copy(
                        lane.sums.at[lane.piece_rows(other)],
                        lane.from_second.at[step],
                        lane.second_device(other),
                    )
                sent(lambda: lane_of(layer, mat).from_second.at[pl.ds(1, lane.second - 1)])
            else:
                for other in range(lane.owners):

                    @pl.when(lane.second_me != other)
                    def _():
                        copy(
                            lane.sums.at[lane.piece_rows(other)],
                            lane.from_second.at[
                                lax.rem(lane.second_me - other + lane.second, lane.second)
                            ],
                            lane.second_device(other),
                        )
                        wait_bytes(lane.from_second.at[0], v.give_stage.at[layer, mat, stage])

        elif stage == SECOND_BACK:

            def send_all():
                rows = lane.piece_rows(lane.second_me)
                for step in range(1, lane.second):
                    copy(
                        lane.result.at[rows],
                        lane.result.at[rows],
                        lane.second_device(lax.rem(lane.second_me + step, lane.second)),
                    )

            if lane.owners == lane.second:
                send_all()
                sent(lambda: lane_of(layer, mat).from_second.at[pl.ds(1, lane.second - 1)])
            else:

                @pl.when(lane.second_me < lane.owners)
                def _():
                    send_all()
                    wait_bytes(
                        lane.from_second.at[pl.ds(1, lane.second - 1)],
                        v.give_stage.at[layer, mat, stage],
                    )

        elif stage == FIRST_BACK:
            rows = lane.share_rows(lane.first_me)
            for step in range(1, lane.first):
                copy(
                    lane.result.at[rows],
                    lane.result.at[rows],
                    lane.first_device(lax.rem(lane.first_me + step, lane.first)),
                )
            sent(lambda: lane_of(layer, mat).from_first)
        elif stage == CORE_BACK:
            copy(lane.result, lane.result, {"nodes": mate})
            sent(lambda: grads.at[layer, mat])

    def end_stage(stage, layer, mat):
        lane = lane_of(layer, mat)
        taken = v.take_stage.at[layer, mat, stage]
        if stage == CORE:
            wait_bytes(v.from_core.at[layer, mat], taken)
            v.sums[layer, mat] = v.sums[layer, mat] + v.from_core[layer, mat]
        elif stage == FIRST:
            wait_bytes(lane.from_first, taken)
            rows = lane.share_rows(lane.first_me)
            value = v.sums[layer, mat, rows, :]
            for step in range(lane.first - 1):
                value = value + lane.from_first[step]
            v.sums[layer, mat, rows, :] = value
        elif stage == SECOND:

            def add():
                wait_bytes(lane.from_second.at[pl.ds(1, lane.second - 1)], taken)
                rows = lane.piece_rows(lane.second_me)
                value = v.sums[layer, mat, rows, :]
                for step in range(1, lane.second):
                    value = value + lane.from_second[step]
                grads[layer, mat, rows, :] = value

            if lane.owners == lane.second:
                add()
            else:
                pl.when(lane.second_me < lane.owners)(add)
        elif stage == SECOND_BACK:
            if lane.owners == lane.second:
                wait_bytes(lane.from_second.at[pl.ds(1, lane.second - 1)], taken)
            else:
                if lane.owners > 1:
                    wait_bytes(lane.from_second.at[pl.ds(1, lane.owners - 1)], taken)

                @pl.when(lane.second_me >= lane.owners)
                def _():
                    wait_bytes(lane.from_second.at[0], taken)

        elif stage == FIRST_BACK:
            wait_bytes(lane.from_first, taken)
        elif stage == CORE_BACK:
            wait_bytes(grads.at[layer, mat], taken)

    def advance(*moves):
        def run(which):
            for stage, layer, mat in moves:
                if owner(layer, mat) == which:
                    end_stage(stage, layer, mat)
                    start_stage(stage + 1, layer, mat)

        for which in range(2):
            if any(owner(layer, mat) == which for _, layer, mat in moves):
                on(which, functools.partial(run, which))


    loads[1].wait()
    v.listed_row[...] = jnp.zeros_like(v.listed_row)
    v.listed_row[0:1, : z.listed] = v.listed_in[pl.ds(sec, 1), :].astype(F32)
    spread_from = iota((v.listed_row.shape[1], z.halo_pad), 0)
    spread_to = iota((v.listed_row.shape[1], z.halo_pad), 1)
    spread = as_ones(
        (lax.div(spread_from, z.send) == lax.div(spread_to, TILE))
        & (lax.rem(spread_from, z.send) == lax.rem(spread_to, TILE))
        & (spread_from < z.listed)
    )
    listed = mm(v.listed_row[...].astype(BF16), spread)[0:1, :]
    place = iota((1, z.halo_pad), 1)
    real = (lax.rem(place, TILE) < z.send) & (place < z.halo)
    listed = jnp.where(real, listed, -1.0)
    list_t = jnp.where(iota((R, z.halo_pad), 0).astype(F32) == listed, 1.0, 0.0)
    v.list_t[...] = list_t.astype(BF16)
    v.list[...] = list_t.T[: z.halo, :].astype(BF16)

    loads[0].wait()
    own = v.features_in[...]
    v.h[pl.ds(0, R), :] = own
    high, low = halves(own)
    v.h_hi[pl.ds(0, R), :] = high
    v.h_lo[pl.ds(0, R), :] = low
    v.outgoing[FEATURES] = mm(v.list[...], high) + mm(v.list[...], low)
    pl.semaphore_wait(barrier, N - 1 + S - 1)
    start_exchange(FEATURES)

    for load in loads[2:5]:
        load.wait()
    for layer in range(2):
        for mat in range(3):
            high, low = halves(v.weights_in[mat, layer])
            v.weights_hi[layer, mat] = high
            v.weights_lo[layer, mat] = low

    def weight(layer, mat):
        return v.weights_hi[layer, mat], v.weights_lo[layer, mat]

    for load in loads[5:11]:
        load.wait()
    named = v.slots_in[...]
    offset = named - R
    remote = R + lax.div(offset, z.send) * TILE + lax.rem(offset, z.send)
    named = jnp.where(named < R, named, remote).astype(F32)
    v.prep[...] = jnp.zeros_like(v.prep)
    v.prep[pl.ds(0, K), :] = named
    v.prep[pl.ds(K, 1), :] = v.degree_in[pl.ds(sec, 1), :].astype(F32)
    v.prep[pl.ds(K + 1, 1), :] = v.mask_in[pl.ds(sec, 1), :].astype(F32)
    v.prep_t[...] = v.prep[...].T
    for slot in range(1, K):
        column = v.prep_t[:, slot : slot + 1]
        pick = as_ones(iota((R, T), 1).astype(F32) == column)
        v.pick[slot - 1, :, pl.ds(0, T)] = pick
        v.pick[slot - 1, :, pl.ds(T, z.halo_pad)] = pick[:, R:]
        row = v.prep[slot : slot + 1, :]
        v.pick_t[:, (slot - 1) * R : slot * R] = as_ones(iota((z.picked, R), 0).astype(F32) == row)
    block_row = lax.div(lax.rem(iota((2 * D, D), 0), D), GROUP)
    v.ones[...] = as_ones(block_row == lax.div(iota((2 * D, D), 1), GROUP))

    def project(layer):
        rows = pl.ds(0, R)
        own = (v.h_hi[rows, :], v.h_lo[rows, :])
        left = mm3(own, weight(layer, 0))
        v.taken[layer, 0] = left
        high, low = halves(left)
        v.table_hi[rows, :] = high
        v.table_lo[rows, :] = low
        v.right[layer] = mm3(own, weight(layer, 1))
        v.skip[...] = mm3(own, weight(layer, 2))

    def project_halo(layer):
        rows = pl.ds(R, z.halo_pad)
        left = mm3((v.h_hi[rows, :], v.h_lo[rows, :]), weight(layer, 0))
        high, low = halves(left)
        v.halo_table[pl.ds(0, z.halo_pad), :] = high
        v.halo_table[pl.ds(z.halo_pad, z.halo_pad), :] = low

    def store_halo(values):
        if z.halo < z.halo_pad:
            rest = pl.ds(R + z.halo, z.halo_pad - z.halo)
            v.h[rest, :] = jnp.zeros((z.halo_pad - z.halo, D), F32)
            v.h_hi[rest, :] = jnp.zeros((z.halo_pad - z.halo, D), BF16)
            v.h_lo[rest, :] = jnp.zeros((z.halo_pad - z.halo, D), BF16)
        rows = pl.ds(R, z.halo)
        v.h[rows, :] = values
        high, low = halves(values)
        v.h_hi[rows, :] = high
        v.h_lo[rows, :] = low

    def keep_transposed(layer):
        high, low = halves(v.h[...].T)
        v.ht_hi[layer] = high
        v.ht_lo[layer] = low

    def store_pair(slot, rows, values):
        high, low = halves(values)
        v.pair[slot, rows, pl.ds(0, D)] = high
        v.pair[slot, rows, pl.ds(D, D)] = low

    def gather_own(layer):
        def one(slot, carry):
            pick = v.pick[slot - 1, :, pl.ds(0, R)]
            v.taken[layer, slot] = mm(pick, v.table_hi[...]) + mm(pick, v.table_lo[...])
            return carry

        lax.fori_loop(1, K, one, 0, unroll=True)

    def head_sum(slot):
        v.score[slot] = mm(v.pair[slot], v.ones[...])

    def attend(layer):
        vector = v.vector_in[layer : layer + 1, :]

        def gather(slot):
            pick = v.pick[slot - 1, :, pl.ds(R, 2 * z.halo_pad)]
            value = mm(pick, v.halo_table[...])
            if layer == 0:
                value = v.taken[layer, slot] + value
            else:
                pick = v.pick[slot - 1, :, pl.ds(0, R)]
                value = mm(pick, v.table_hi[...]) + mm(pick, v.table_lo[...]) + value
            v.taken[layer, slot] = value

        def activate(slot):
            for place in range(0, R, BLOCK):
                rows = pl.ds(place, BLOCK)
                half = 0.5 * (v.taken[layer, slot, rows, :] + v.right[layer, rows, :])
                store_pair(slot, rows, (half * jnp.tanh(half) + half) * vector)

        for slot in range(1, K + 3):
            if slot < K:
                gather(slot)
            if slot <= K:
                activate(slot - 1)
            if slot >= 3:
                head_sum(slot - 3)

        def mix(i, carry):
            rows = chunk(i)
            count = jnp.broadcast_to(v.prep_t[rows, K : K + 1], (CHUNK, D))
            scores = [v.score[0, rows, :], v.score[1, rows, :]]
            scores += [
                jnp.where(count > slot, v.score[slot, rows, :], MASKED_SCORE) for slot in range(2, K)
            ]
            highest = functools.reduce(jnp.maximum, scores)
            powers = [jnp.exp(score - highest) for score in scores]
            scale = 1.0 / functools.reduce(jnp.add, powers)
            joined = jnp.zeros((CHUNK, D), F32)
            for slot in range(K):
                alpha = powers[slot] * scale
                v.alpha[layer, slot, rows, :] = alpha
                joined = joined + alpha * v.taken[layer, slot, rows, :]
            v.joined[layer, rows, :] = joined
            mixed = joined + v.skip[rows, :]
            v.mixed[rows, :] = mixed
            return carry[0] + fold(mixed), carry[1] + fold(mixed * mixed)

        nothing = jnp.zeros((TILE, D), F32)
        first, second = rows_loop(mix, (nothing, nothing))
        return add_rows(first), add_rows(second)

    def derive(layer):
        vector = v.vector_in[layer : layer + 1, :]

        def one(i, carry):
            rows = chunk(i)
            right = v.right[layer, rows, :]
            for slot in range(K):
                u = v.taken[layer, slot, rows, :] + right
                sig = sigmoid(u)
                act = u * sig
                v.act[layer, slot, rows, :] = act
                v.rise[layer, slot, rows, :] = vector * (sig + act * (1.0 - sig))
            return carry

        rows_loop(one, 0)

    def moments(which):
        first, second = arrived_sums(which)
        mean = first / total_rows
        return mean, lax.rsqrt(second / total_rows - mean * mean + VARIANCE_EPS)

    def activation(layer, mixed, mean, inverse):
        normed = (mixed - mean) * inverse
        pre = v.gain_in[layer : layer + 1, :] * normed + v.shift_in[layer : layer + 1, :]
        power = jnp.exp(jnp.minimum(pre, 0.0))
        return normed, jnp.where(pre > 0, 1.0, power), jnp.where(pre > 0, pre, power - 1.0)

    def sums_tile(which, first, second):
        v.outgoing[which, pl.ds(0, TILE), :] = with_sums(jnp.zeros((TILE, D), F32), first, second)

    def list_rows(values):
        high, low = halves(values)
        return mm(v.list[...], high) + mm(v.list[...], low)

    project(0)
    gather_own(0)
    end_exchange(FEATURES)
    store_halo(arrived_rows(FEATURES))
    project_halo(0)
    first, second = attend(0)
    v.outgoing[MIXED] = with_sums(list_rows(v.mixed[...]), first, second)
    start_exchange(MIXED)
    keep_transposed(0)
    derive(0)
    end_exchange(MIXED)
    mean0, inverse0 = moments(MIXED)

    def finish0(i, carry):
        rows = chunk(i)
        normed, slope, hidden = activation(0, v.mixed[rows, :], mean0, inverse0)
        v.normed[0, rows, :] = normed
        v.slope[0, rows, :] = slope
        v.h[rows, :] = hidden
        high, low = halves(hidden)
        v.h_hi[rows, :] = high
        v.h_lo[rows, :] = low
        return carry

    rows_loop(finish0, 0)
    normed, slope, hidden = activation(0, arrived_rows(MIXED), mean0, inverse0)
    v.halo_normed[...] = normed
    v.halo_slope[...] = slope
    store_halo(jnp.where(row_in_tile(z.halo) < z.send, hidden, 0.0))

    project(1)
    project_halo(1)
    first, second = attend(1)
    sums_tile(SUMS, first, second)
    start_exchange(SUMS, True)
    keep_transposed(1)
    derive(1)
    loads[11].wait()
    end_exchange(SUMS)
    mean1, inverse1 = moments(SUMS)

    def finish1(i, carry):
        rows = chunk(i)
        normed, slope, hidden = activation(1, v.mixed[rows, :], mean1, inverse1)
        v.normed[1, rows, :] = normed
        out[0, rows, :] = hidden
        dpre = v.cotangent_in[rows, :] * v.prep_t[rows, K + 1 : K + 2] * slope
        v.dpre[rows, :] = dpre
        return carry[0] + fold(dpre), carry[1] + fold(dpre * normed)

    nothing = jnp.zeros((TILE, D), F32)
    first, second = rows_loop(finish1, (nothing, nothing))
    shift1, gain1 = add_rows(first), add_rows(second)
    sums_tile(BACK_SUMS, shift1, gain1)
    start_exchange(BACK_SUMS, True)

    def normalization_back(layer, which, inverse):
        first, second = arrived_sums(which)
        first = first / total_rows
        second = second / total_rows
        scale = inverse * v.gain_in[layer : layer + 1, :]

        def one(i, carry):
            rows = chunk(i)
            dmixed = scale * (v.dpre[rows, :] - first - v.normed[layer, rows, :] * second)
            v.dmixed[rows, :] = dmixed
            high, low = halves(dmixed)
            v.dm_hi[rows, :] = high
            v.dm_lo[rows, :] = low
            return carry

        rows_loop(one, 0)

    def attend_back(layer, between=None):
        def differences(slot):
            for place in range(0, R, BLOCK):
                rows = pl.ds(place, BLOCK)
                value = (v.taken[layer, slot, rows, :] - v.joined[layer, rows, :]) * v.dmixed[rows, :]
                store_pair(slot, rows, value)

        weight_grad(layer, 2)
        for slot in range(K + 1):
            if slot < K:
                differences(slot)
            if slot >= 1:
                head_sum(slot - 1)
        start_core(layer, 2)

        def one(i, carry):
            rows = chunk(i)
            dmixed = v.dmixed[rows, :]
            dright = jnp.zeros((CHUNK, D), F32)
            for slot in range(K):
                alpha = v.alpha[layer, slot, rows, :]
                dscore = alpha * v.score[slot, rows, :]
                carry = carry + fold(dscore * v.act[layer, slot, rows, :])
                du = dscore * v.rise[layer, slot, rows, :]
                dright = dright + du
                dleft = du + alpha * dmixed
                if slot == 0:
                    v.dleft_self[rows, :] = dleft
                else:
                    high, low = halves(dleft)
                    place = pl.ds(pl.multiple_of((slot - 1) * R + i * CHUNK, CHUNK), CHUNK)
                    v.dleft_hi[place, :] = high
                    v.dleft_lo[place, :] = low
            high, low = halves(dright)
            v.dr_hi[rows, :] = high
            v.dr_lo[rows, :] = low
            return carry

        vector_sum = rows_loop(one, jnp.zeros((TILE, D), F32))
        if between is not None:
            between()

        def scattered(rows):
            pick = v.pick_t[rows, :]
            return mm(pick, v.dleft_hi[...]) + mm(pick, v.dleft_lo[...])

        rows = pl.ds(0, R)
        own = scattered(rows) + v.dleft_self[...]
        v.dleft_self[...] = own
        high, low = halves(own)
        v.dl_hi[rows, :] = high
        v.dl_lo[rows, :] = low
        rows = pl.ds(R, z.halo)
        halo = scattered(rows)
        if layer == 0:
            start_return(halo)
        high, low = halves(halo)
        v.dl_hi[rows, :] = high
        v.dl_lo[rows, :] = low
        return add_rows(vector_sum)

    def start_return(halo):
        v.returning[...] = halo[:, :LANES] + pltpu.roll(halo[:, LANES:], z.send, 0)
        own = pl.ds(pl.multiple_of(me * TILE, TILE), TILE)

        def send(step, carry):
            other = lax.rem(me + side * step + N, N)
            pltpu.make_async_remote_copy(
                src_ref=v.returning.at[pl.ds(pl.multiple_of(other * TILE, TILE), TILE)],
                dst_ref=v.returned.at[own],
                send_sem=v.give_rows.at[0],
                recv_sem=v.take_rows.at[0],
                device_id={"nodes": other},
                device_id_type=MESH,
            ).start()
            return carry

        lax.fori_loop(1, N, send, 0)
        v.returned[own, :] = v.returning[own, :]

    def dleft(rows):
        return v.dl_hi[rows, :], v.dl_lo[rows, :]

    def input_back(layer):
        own = pl.ds(0, R)
        v.dh[...] = (
            mm3(dleft(own), weight(layer, 0), mm_nt)
            + mm3((v.dr_hi[...], v.dr_lo[...]), weight(layer, 1), mm_nt)
            + mm3((v.dm_hi[...], v.dm_lo[...]), weight(layer, 2), mm_nt)
        )
        return mm3(dleft(pl.ds(R, z.halo)), weight(layer, 0), mm_nt)

    def weight_grad(layer, mat):
        if mat == 0:
            upstream = (v.dl_hi[...], v.dl_lo[...])
            inputs = (v.ht_hi[layer], v.ht_lo[layer])
        else:
            upstream = (v.dr_hi[...], v.dr_lo[...]) if mat == 1 else (v.dm_hi[...], v.dm_lo[...])
            inputs = (v.ht_hi[layer, :, pl.ds(0, R)], v.ht_lo[layer, :, pl.ds(0, R)])
        v.sums[layer, mat] = mm3(inputs, upstream)

    if z.halo < z.halo_pad:
        rest = pl.ds(R + z.halo, z.halo_pad - z.halo)
        v.dl_hi[rest, :] = jnp.zeros((z.halo_pad - z.halo, D), BF16)
        v.dl_lo[rest, :] = jnp.zeros((z.halo_pad - z.halo, D), BF16)

    end_exchange(BACK_SUMS)
    normalization_back(1, BACK_SUMS, inverse1)
    vector1 = attend_back(1)
    halo_back = input_back(1)
    dpre = v.dh[...] * v.slope[0]
    halo_dpre = halo_back * v.halo_slope[...]
    shift0 = add_rows(dpre) + add_rows(halo_dpre)
    gain0 = add_rows(dpre * v.normed[0]) + add_rows(halo_dpre * v.halo_normed[...])
    v.outgoing[BACK_ROWS] = with_sums(halo_back, shift0, gain0)
    start_exchange(BACK_ROWS)
    advance((CORE, 1, 2))
    weight_grad(1, 1)
    start_core(1, 1)
    weight_grad(1, 0)
    start_core(1, 0)
    advance((CORE, 1, 1), (CORE, 1, 0))
    end_exchange(BACK_ROWS)
    v.dpre[...] = (v.dh[...] + give_rows_back(BACK_ROWS)) * v.slope[0]

    normalization_back(0, BACK_ROWS, inverse0)

    def between():
        weight_grad(0, 1)
        start_core(0, 1)
        advance(*BETWEEN)

    vector0 = attend_back(0, between)
    weight_grad(0, 0)
    start_core(0, 0)

    row = iota((TILE, D), 0)
    tile = jnp.zeros((TILE, D), F32)
    for place, value in enumerate((vector0, vector1, gain0, gain1, shift0, shift1)):
        tile = jnp.where(row == place, value, tile)
    v.small[0] = tile

    def send_small(stage, source, target, device):
        pltpu.make_async_remote_copy(
            src_ref=source,
            dst_ref=target,
            send_sem=v.give_small.at[stage],
            recv_sem=v.take_small.at[stage],
            device_id=device,
            device_id_type=MESH,
        ).start()

    on(0, lambda: send_small(0, v.small.at[0], v.small_core.at[0], {"nodes": mate}))

    def small_outer():
        wait_bytes(v.small_core.at[0], v.take_small.at[0])
        value = v.small[0] + v.small_core[0]
        v.small[1] = value
        v.small_outer[outer] = value
        for step in range(1, O):
            send_small(
                1, v.small.at[1], v.small_outer.at[outer], {"nodes": lax.rem(outer + step, O) * 2 + core}
            )

    def small_section():
        wait_bytes(v.small_outer.at[pl.ds(1, O - 1)], v.take_small.at[1])
        value = jnp.sum(v.small_outer[...], axis=0)
        v.small[2] = value
        v.small_section[sec] = value
        for step in range(1, S):
            send_small(
                2, v.small.at[2], v.small_section.at[sec], {"section": lax.rem(sec + step, S)}
            )

    def put_small(value):
        g_vec[...] = value[0:2, :]
        g_gain[...] = value[2:4, :]
        g_shift[...] = value[4:6, :]

    def small_back():
        wait_bytes(v.small_section.at[pl.ds(1, S - 1)], v.take_small.at[2])
        value = jnp.sum(v.small_section[...], axis=0)
        v.small[3] = value
        send_small(3, v.small.at[3], v.small_core.at[1], {"nodes": mate})
        put_small(value)

    def small_end():
        wait_bytes(v.small_core.at[1], v.take_small.at[3])
        put_small(v.small_core[1])

    advance(*AFTER)
    def part_input():
        v.dh[...] = mm3((v.dr_hi[...], v.dr_lo[...]), weight(0, 1), mm_nt) + mm3(
            (v.dm_hi[...], v.dm_lo[...]), weight(0, 2), mm_nt
        )

    def store_input():
        wait_bytes(v.returned.at[pl.ds(0, (N - 1) * TILE)], v.take_rows.at[0])
        values = v.returned[...]
        values = jnp.concatenate([values, pltpu.roll(values, z.halo - z.send, 0)], axis=1)
        high, low = halves(jnp.where(row_in_tile(z.halo) < z.send, values, 0.0))
        listed = v.list_t[:, : z.halo]
        left = v.dleft_self[...] + (mm(listed, high) + mm(listed, low))
        grad_in[0] = v.dh[...] + mm3(halves(left), weight(0, 0), mm_nt)

    steps = {
        "outer": small_outer,
        "section": small_section,
        "back": small_back,
        "end": small_end,
        "part": part_input,
        "input": store_input,
    }

    def finish(which):
        for step in TAILS[which]:
            if isinstance(step, str):
                steps[step]()
            else:
                end_stage(*step)
                start_stage(step[0] + 1, *step[1:])

    on(0, lambda: finish(0))
    on(1, lambda: finish(1))

    def receive(which):
        for layer in (1, 0):
            for mat in (2, 1, 0):
                if owner(layer, mat) != which:
                    end_stage(CORE_BACK, layer, mat)

    for which in range(EXCHANGES):
        wait_bytes(v.outgoing.at[which, pl.ds(0, (N - 1) * TILE)], v.give.at[which])
    wait_bytes(v.returned.at[pl.ds(0, (N - 1) * TILE)], v.give_rows.at[0])

    def sent(which):
        for ref, semaphore, sender in sends_to_end:
            if sender == which:
                wait_bytes(ref(), semaphore())

    def sent_small(stage, count):
        wait_bytes(v.small_outer.at[pl.ds(0, count)], v.give_small.at[stage])

    def sent0():
        sent(0)
        sent_small(0, 1)
        receive(0)

    def sent1():
        sent(1)
        sent_small(1, O - 1)
        wait_bytes(v.small_section.at[pl.ds(1, S - 1)], v.give_small.at[2])
        sent_small(3, 1)
        receive(1)

    on(0, sent0)
    on(1, sent1)


def store_kernel(*refs):
    out, grad_in, grads, g_vec, g_gain, g_shift = refs[:6]
    pairs = [(out, refs[6]), (grad_in, refs[7])]
    for mat in range(3):
        pairs += [(grads.at[layer, mat], refs[8 + mat].at[layer]) for layer in range(2)]
    pairs += [(g_vec, refs[11]), (g_gain, refs[12]), (g_shift, refs[13])]
    copies = [pltpu.make_async_copy(*pair, refs[14].at[i]) for i, pair in enumerate(pairs)]
    for copy in copies:
        copy.start()
    for copy in copies:
        copy.wait()


def body(
    features,
    cotangent,
    train_mask,
    degree,
    neighbours,
    send_rows,
    w_left,
    w_right,
    w_res,
    attn_vec,
    bn_gain,
    bn_shift,
):
    batches, rows, width = features.shape
    sections = lax.axis_size("section")
    assert batches == sections and width == HEADS * GROUP
    z = sizes_of(
        sections, lax.axis_size("nodes"), rows, width, neighbours.shape[2], send_rows.shape[1]
    )
    shapes = scratch_of(z)
    shapes["mask_in"] = (train_mask.shape, jnp.int32)
    shapes["degree_in"] = (degree.shape, jnp.int32)
    shapes["listed_in"] = (send_rows.shape, jnp.int32)
    scratch = [pltpu.VMEM(shape, dtype) for shape, dtype in shapes.values()]
    scratch += [pltpu.SemaphoreType.DMA(shape) for shape in SEMAPHORES.values()]
    names = list(shapes) + list(SEMAPHORES)
    anywhere = pl.BlockSpec(memory_space=pl.ANY)
    square = jax.ShapeDtypeStruct((2, width, width), F32)
    columns = jax.ShapeDtypeStruct((2, width), F32)
    block = jax.ShapeDtypeStruct((1, rows, width), F32)
    results = (block, block, square, square, square, columns, columns, columns)
    in_vmem = pl.BlockSpec(memory_space=pltpu.VMEM)
    squares = jax.ShapeDtypeStruct((2, 3, width, width), F32)
    kept = (block, block, squares, columns, columns, columns)
    found = pl.pallas_call(
        functools.partial(kernel, z, names),
        out_shape=tuple(pltpu.VMEM(x.shape, x.dtype) for x in kept),
        in_specs=[pl.BlockSpec(memory_space=pltpu.HBM)] * 12,
        out_specs=(in_vmem,) * 6,
        scratch_shapes=scratch,
        compiler_params=pltpu.CompilerParams(
            collective_id=0, has_side_effects=True, vmem_limit_bytes=60 * 1024 * 1024
        ),
    )(
        features,
        cotangent,
        train_mask,
        degree,
        jnp.transpose(neighbours, (0, 2, 1)),
        send_rows,
        w_left,
        w_right,
        w_res,
        attn_vec,
        bn_gain,
        bn_shift,
    )
    return pl.pallas_call(
        store_kernel,
        out_shape=results,
        in_specs=[anywhere] * 6,
        out_specs=(anywhere,) * 8,
        scratch_shapes=[pltpu.SemaphoreType.DMA((11,))],
        compiler_params=pltpu.CompilerParams(vmem_limit_bytes=1024 * 1024),
    )(*found)


def solution(mesh):
    return jax.shard_map(
        body,
        mesh=mesh,
        in_specs=(
            P(None, "nodes", None),
            P(None, "nodes", None),
            P(None, "nodes"),
            P(None, "nodes"),
            P(None, "nodes", None),
            P(None, "nodes"),
            P(),
            P(),
            P(),
            P(),
            P(),
            P(),
        ),
        out_specs=(
            P("section", "nodes", None),
            P("section", "nodes", None),
            P(),
            P(),
            P(),
            P(),
            P(),
            P(),
        ),
        check_vma=False,
    )
```
